32 devices in a mesh: ctx: 16 (over z, y, core), fsdp: 2 (over x).
Axes of the slice: x: 2, y: 2, z: 4, core: 2. Of those that a mesh axis runs over, the one named last changes fastest.
Arguments:
- tokens: bfloat16 [4096, 2560], P('ctx', 'fsdp'), may hold values from -6 to 6
- x_weight: bfloat16 [2560, 2560], P('fsdp'), may hold values from -0.125 to 0.125
- bc_weight: bfloat16 [2560, 256], P('fsdp'), may hold values from -0.125 to 0.125
- dt_weight: bfloat16 [2560, 40], P('fsdp'), may hold values from -0.125 to 0.125
- conv_inner: float32 [4, 2560], P(None, 'fsdp'), may hold values from -4 to 4
- conv_shared: float32 [4, 256], replicated, may hold values from -4 to 4
- dt_bias: float32 [40], P('fsdp'), may hold values from -3 to 3
- decay_rate: float32 [40], P('fsdp'), as said below
- norm_gain: float32 [2560], P('fsdp'), may hold values from 0.5 to 1.5
- doc_starts: int32 [4], replicated, may hold values from 0 to 3968, as said below
- grad_out: bfloat16 [4096, 2560], P('ctx', 'fsdp'), may hold values from -6 to 6
Outputs:
- mixed_out: bfloat16 [4096, 2560], P('ctx', 'fsdp')
- grad_tokens: bfloat16 [4096, 2560], P('ctx', 'fsdp')
The draws below stay inside these ranges and needn't reach their ends.
Inputs may be any that keep to these rules, and one draw needn't show every extreme that they name: `decay_rate`: positive rates, one a head. `doc_starts`: strictly increasing token offsets; the first is 0 and the last is 3968.
All inputs are finite; a program needn't handle non-finite values.
Results may differ from the reference program's by a relative error of at most 0.015.
Values may be sent and summed in bfloat16 or wider, within the bound.
No kernel may reach another device: no remote copies, remote signals or barrier semaphores. Data moves between devices by JAX's collectives and lax.ppermute only.
A program may use at most 128 MiB of HBM per device.

```python
import jax
import jax.numpy as jnp
from jax import lax

D = 2560
HEADS = 40
HEAD_DIM = 64
STATE = 128
TOK_DEV = 256
DOCS = 4
INNER = 2560
SEQ = 4096


def draw_decay_rate(key, part):
    fast_key, slow_key, pick_key = jax.random.split(key, 3)
    fast = jax.random.uniform(fast_key, (HEADS,), jnp.float32, 1.0 / 50.0, 1.0 / 25.0)
    slow = jax.random.uniform(slow_key, (HEADS,), jnp.float32, 0.2, 1.2) / SEQ
    share = 0.5
    pick = jax.random.uniform(pick_key, (HEADS,), jnp.float32) < share
    return jnp.where(pick, fast, slow).astype(jnp.float32)


def draw_doc_starts(key, part):
    last_start = SEQ - TOK_DEV // 2
    order = jax.random.permutation(key, last_start - 1)[:DOCS - 2] + 1
    picks = jnp.sort(order).astype(jnp.int32)
    return jnp.concatenate([jnp.zeros((1,), jnp.int32), picks, jnp.full((1,), last_start, jnp.int32)])


def block_levels(own_key, dims, cuts, smallest, largest):
    def one(axis_at, shards_of):
        heights = jax.random.uniform(jax.random.fold_in(jax.random.fold_in(own_key, 6), axis_at), (shards_of,), jnp.float32, smallest / len(cuts), largest / len(cuts))
        return jnp.repeat(jnp.exp(heights), dims[axis_at] // shards_of).reshape((-1,) + (1,) * (len(dims) - axis_at - 1))

    factor_of = one(*cuts[0])
    for cut in cuts[1:]:
        factor_of = factor_of * one(*cut)
    return factor_of


def normal_values(rng, extent, deviation, bound, pieces=(), kind=jnp.bfloat16):
    values = jax.random.normal(rng, extent, jnp.float32) * deviation
    if len(pieces) > 0:
        values = block_levels(rng, extent, pieces, -0.22, 0.18) * values
    return jnp.clip(values, min=-bound, max=bound).astype(kind)


def setup_inputs(seed: int = 0) -> dict:
    keys = jax.random.split(jax.random.key(seed), 12)
    tokens = normal_values(keys[0], (SEQ, D), 1.0, 6.0, ((0, 16), (1, 2)))
    x_weight = normal_values(keys[1], (D, INNER), D ** -0.5, 0.125, ((0, 2),))
    bc_weight = normal_values(keys[2], (D, 2 * STATE), D ** -0.5, 0.125, ((0, 2),))
    dt_weight = normal_values(keys[3], (D, HEADS), D ** -0.5, 0.125, ((0, 2),))
    conv_inner = normal_values(keys[4], (4, INNER), 2 ** -0.5, 4.0, ((1, 2),), jnp.float32)
    conv_shared = normal_values(keys[5], (4, 2 * STATE), 2 ** -0.5, 4.0, (), jnp.float32)
    dt_bias = normal_values(keys[6], (HEADS,), 0.7, 3.0, ((0, 2),), jnp.float32)
    decay_rate = draw_decay_rate(jax.random.fold_in(keys[11], 71), 0)
    norm_gain = jnp.clip(1.0 + 0.1 * jax.random.normal(keys[8], (INNER,), jnp.float32), 0.5, 1.5)
    doc_starts = draw_doc_starts(jax.random.fold_in(keys[11], 71), 0)
    grad_out = normal_values(keys[10], (SEQ, INNER), 1.0, 6.0, ((0, 16), (1, 2)))
    return dict(tokens=tokens, x_weight=x_weight, bc_weight=bc_weight, dt_weight=dt_weight, conv_inner=conv_inner, conv_shared=conv_shared, dt_bias=dt_bias, decay_rate=decay_rate, norm_gain=norm_gain, doc_starts=doc_starts, grad_out=grad_out)


exact = lax.Precision.HIGHEST
epsilon = 1e-05

def doc_index(positions, doc_starts):
    hits = (doc_starts[None, :] <= positions[:, None]).astype(jnp.int32)
    return lax.optimization_barrier(jnp.sum(hits, axis=1)).astype(jnp.int32) - 1

def causal_conv(padded, docs_ext, taps):
    count = padded.shape[0] - 3
    docs_now = docs_ext[3:]
    total = jnp.zeros((count, padded.shape[1]), jnp.float32)
    for offset in range(4):
        rows = padded[3 - offset:3 - offset + count]
        same = (docs_ext[3 - offset:3 - offset + count] == docs_now).astype(jnp.float32)
        total = total + taps[offset][None, :] * rows * same[:, None]
    return total

def block_out(x_act, b_act, c_act, delta, docs, doc_before, state_in, decay_rate):
    count = delta.shape[0]
    places = jnp.arange(count, dtype=jnp.int32)
    lower = places[:, None] >= places[None, :]
    ramp = -jnp.dot(lower.astype(jnp.float32), delta, precision=exact) * decay_rate[None, :]
    same = jnp.logical_and(docs[:, None] == docs[None, :], lower)
    gap = ramp[:, None, :] - ramp[None, :, :]
    decay = jnp.exp(jnp.where(same[:, :, None], gap, 0.0)) * same.astype(jnp.float32)[:, :, None]
    scores = jnp.dot(c_act, b_act.T, precision=exact)
    mixing = decay * scores[:, :, None] * delta[None, :, :]
    inner = jnp.einsum('tsh,shp->thp', mixing, x_act, precision=exact)
    carried = (docs == doc_before).astype(jnp.float32)
    enter = jnp.exp(ramp) * carried[:, None]
    from_state = jnp.einsum('tn,hpn->thp', c_act, state_in, precision=exact) * enter[:, :, None]
    last_doc = docs[count - 1]
    tail = jnp.exp(ramp[count - 1][None, :] - ramp) * (docs == last_doc).astype(jnp.float32)[:, None] * delta
    weighted = tail[:, :, None] * x_act
    state_loc = jnp.einsum('shp,sn->hpn', weighted, b_act, precision=exact)
    keep = jnp.exp(ramp[count - 1]) * (last_doc == doc_before).astype(jnp.float32)
    return (inner + from_state, state_loc, keep)

def head_norm(values, norm_gain):
    scale = lax.rsqrt(lax.optimization_barrier(jnp.mean(values * values, axis=-1, keepdims=True)) + epsilon)
    normed = values * scale
    return normed.reshape(values.shape[0], values.shape[1] * values.shape[2]) * norm_gain[None, :]

def core(x_proj, bc_proj, dt_raw, conv_inner, conv_shared, dt_bias, decay_rate, norm_gain, doc_starts):
    total = x_proj.shape[0]
    positions = jnp.arange(total + 3, dtype=jnp.int32) - 3
    docs_ext = doc_index(positions, doc_starts)
    x_pad = jnp.concatenate([jnp.zeros((3, x_proj.shape[1]), jnp.float32), x_proj], axis=0)
    bc_pad = jnp.concatenate([jnp.zeros((3, bc_proj.shape[1]), jnp.float32), bc_proj], axis=0)
    x_act = jax.nn.silu(causal_conv(x_pad, docs_ext, conv_inner))
    bc_act = jax.nn.silu(causal_conv(bc_pad, docs_ext, conv_shared))
    delta = jax.nn.softplus(dt_raw + dt_bias[None, :])
    blocks = total // TOK_DEV
    items = (x_act.reshape(blocks, TOK_DEV, HEADS, HEAD_DIM), bc_act[:, :STATE].reshape(blocks, TOK_DEV, STATE), bc_act[:, STATE:].reshape(blocks, TOK_DEV, STATE), delta.reshape(blocks, TOK_DEV, HEADS), docs_ext[3:].reshape(blocks, TOK_DEV), docs_ext[2:2 + total:TOK_DEV])

    def advance(state, item):
        x_blk, b_blk, c_blk, d_blk, doc_blk, before = item
        values, state_loc, keep = block_out(x_blk, b_blk, c_blk, d_blk, doc_blk, before, state, decay_rate)
        return (keep[:, None, None] * state + state_loc, values)
    start = jnp.zeros((HEADS, HEAD_DIM, STATE), jnp.float32)
    _, values = lax.scan(jax.checkpoint(advance), start, items)
    return head_norm(values.reshape(total, HEADS, HEAD_DIM), norm_gain)

def reference(tokens, x_weight, bc_weight, dt_weight, conv_inner, conv_shared, dt_bias, decay_rate, norm_gain, doc_starts, grad_out):
    x_proj = jnp.dot(tokens, x_weight, preferred_element_type=jnp.float32).astype(jnp.bfloat16)
    bc_proj = jnp.dot(tokens, bc_weight, preferred_element_type=jnp.float32)
    dt_raw = jnp.dot(tokens, dt_weight, preferred_element_type=jnp.float32)

    def layer(x_in, bc_in, dt_in):
        return core(x_in, bc_in, dt_in, conv_inner, conv_shared, dt_bias, decay_rate, norm_gain, doc_starts)
    x_wide = lax.optimization_barrier(x_proj).astype(jnp.float32)
    normed, pull = jax.vjp(layer, x_wide, bc_proj, dt_raw)
    grad_x, grad_bc, grad_dt = pull(grad_out.astype(jnp.float32))
    grad_xb = grad_x.astype(jnp.bfloat16)
    grad_in = jnp.dot(grad_xb, x_weight.T, preferred_element_type=jnp.float32)
    grad_in = grad_in + jnp.dot(grad_bc, bc_weight.T.astype(jnp.float32), precision=exact)
    grad_in = grad_in + jnp.dot(grad_dt, dt_weight.T.astype(jnp.float32), precision=exact)
    return (normed.astype(jnp.bfloat16), grad_in.astype(jnp.bfloat16))
```

```python
import functools

import jax
import jax.numpy as jnp
from jax import lax
from jax.experimental import pallas as pl
from jax.experimental.pallas import tpu as pltpu
from jax.sharding import PartitionSpec as P

HEAD_DIM = 64
STATE = 128


exact = lax.Precision.HIGHEST
epsilon = 1e-05


def from_behind(value, axis, steps):
    count = lax.axis_size(axis)
    leading, last = (max(0, -steps), min(count, count - steps))
    return lax.ppermute(value, axis, [(source, source + steps) for source in range(leading, last)])


def prefix(part, axis, combine, identity, reverse):
    count = lax.axis_size(axis)
    place = lax.axis_index(axis)
    ahead = count - 1 - place if reverse else place
    gathered = jax.tree.map(lambda a: lax.all_gather(a, axis), part)
    state = jax.tree.map(lambda a, e: jnp.zeros_like(a) + jnp.asarray(e, a.dtype), part, identity)

    def one(step, state):
        source = count - 1 - step if reverse else step
        return combine(
            state, jax.tree.map(lambda a: lax.dynamic_index_in_dim(a, source, 0, False), gathered)
        )

    return lax.fori_loop(0, ahead, one, state)


def doc_index(positions, doc_starts):
    hits = (doc_starts[None, :] <= positions[:, None]).astype(jnp.int32)
    return jnp.sum(hits, axis=1) - 1


def causal_conv(padded, docs_ext, taps):
    count = padded.shape[0] - 3
    docs_now = docs_ext[3:]
    total = jnp.zeros((count, padded.shape[1]), jnp.float32)
    for offset in range(4):
        rows = padded[3 - offset : 3 - offset + count]
        same = (docs_ext[3 - offset : 3 - offset + count] == docs_now).astype(jnp.float32)
        total = total + taps[offset][None, :] * rows * same[:, None]
    return total


def block_out(x_act, b_act, c_act, delta, docs, doc_before, state_in, decay_rate):
    count = delta.shape[0]
    places = jnp.arange(count, dtype=jnp.int32)
    lower = places[:, None] >= places[None, :]
    ramp = -jnp.dot(lower.astype(jnp.float32), delta, precision=exact) * decay_rate[None, :]
    same = jnp.logical_and(docs[:, None] == docs[None, :], lower)
    gap = ramp[:, None, :] - ramp[None, :, :]
    decay = jnp.exp(jnp.where(same[:, :, None], gap, 0.0)) * same.astype(jnp.float32)[:, :, None]
    scores = jnp.dot(c_act, b_act.T, precision=exact)
    mixing = decay * scores[:, :, None] * delta[None, :, :]
    inner = jnp.einsum("tsh,shp->thp", mixing, x_act, precision=exact)
    carried = (docs == doc_before).astype(jnp.float32)
    enter = jnp.exp(ramp) * carried[:, None]
    from_state = jnp.einsum("tn,hpn->thp", c_act, state_in, precision=exact) * enter[:, :, None]
    last_doc = docs[count - 1]
    tail = (
        jnp.exp(ramp[count - 1][None, :] - ramp)
        * (docs == last_doc).astype(jnp.float32)[:, None]
        * delta
    )
    weighted = tail[:, :, None] * x_act
    state_loc = jnp.einsum("shp,sn->hpn", weighted, b_act, precision=exact)
    keep = jnp.exp(ramp[count - 1]) * (last_doc == doc_before).astype(jnp.float32)
    return (inner + from_state, state_loc, keep)


def head_norm(values, norm_gain):
    scale = lax.rsqrt(jnp.mean(values * values, axis=-1, keepdims=True) + epsilon)
    normed = values * scale
    return normed.reshape(values.shape[0], values.shape[1] * values.shape[2]) * norm_gain[None, :]


def link(earlier, later):
    return (earlier[0] * later[0], later[0][:, None, None] * earlier[1] + later[1])


def on_device(
    tokens,
    x_weight,
    bc_weight,
    dt_weight,
    conv_inner,
    conv_shared,
    dt_bias,
    decay_rate,
    norm_gain,
    doc_starts,
    grad_out,
):
    count = tokens.shape[0]
    heads_here = decay_rate.shape[0]
    features = lax.all_gather(tokens, "fsdp", axis=1, tiled=True)
    x_cols, dt_cols = (
        lax.all_to_all(x_weight, "fsdp", split_axis=1, concat_axis=0, tiled=True),
        lax.all_to_all(dt_weight, "fsdp", split_axis=1, concat_axis=0, tiled=True),
    )
    bc_all = lax.all_gather(bc_weight, "fsdp", axis=0, tiled=True)
    x_proj = jnp.dot(features, x_cols, preferred_element_type=jnp.float32).astype(jnp.bfloat16)
    bc_proj = jnp.dot(features, bc_all, preferred_element_type=jnp.float32)
    dt_raw = jnp.dot(features, dt_cols, preferred_element_type=jnp.float32)
    x_wide = lax.optimization_barrier(x_proj).astype(jnp.float32)
    rim_x, rim_bc = from_behind((x_wide[count - 3 :], bc_proj[count - 3 :]), "ctx", 1)
    x_ext = jnp.concatenate([rim_x, x_wide], axis=0)
    bc_ext = jnp.concatenate([rim_bc, bc_proj], axis=0)
    first = lax.axis_index("ctx") * count
    positions = first - 3 + jnp.arange(count + 3, dtype=jnp.int32)
    docs_ext = doc_index(positions, doc_starts)
    docs = docs_ext[3:]
    doc_before = docs_ext[2]

    def layer(x_in, bc_in, dt_in, state_in):
        x_act = jax.nn.silu(causal_conv(x_in, docs_ext, conv_inner))
        bc_act = jax.nn.silu(causal_conv(bc_in, docs_ext, conv_shared))
        delta = jax.nn.softplus(dt_in + dt_bias[None, :])
        values, state_loc, keep = block_out(
            x_act.reshape(count, heads_here, HEAD_DIM),
            bc_act[:, :STATE],
            bc_act[:, STATE:],
            delta,
            docs,
            doc_before,
            state_in,
            decay_rate,
        )
        return (head_norm(values, norm_gain), state_loc, keep)

    blank = jnp.zeros((heads_here, HEAD_DIM, STATE), jnp.float32)
    unit = jnp.ones((heads_here,), jnp.float32)
    _, state_loc, keep = layer(x_ext, bc_ext, dt_raw, blank)
    state_in = prefix((keep, state_loc), "ctx", link, (unit, blank), False)[1]
    outputs, pull = jax.vjp(layer, x_ext, bc_ext, dt_raw, state_in)
    normed = outputs[0]
    grads_out = pull((grad_out.astype(jnp.float32), jnp.zeros_like(blank), jnp.zeros_like(unit)))
    adjoint = prefix((keep, grads_out[3]), "ctx", link, (unit, blank), True)[1]
    keep_grad = jnp.sum(adjoint * state_in, axis=(1, 2))
    grads_state = pull((jnp.zeros_like(normed), adjoint, keep_grad))
    grad_xe = grads_out[0] + grads_state[0]
    grad_bce = grads_out[1] + grads_state[1]
    grad_dt = grads_out[2] + grads_state[2]
    back_x, back_bc = from_behind((grad_xe[:3], grad_bce[:3]), "ctx", -1)
    grad_x = grad_xe[3:].at[count - 3 :].add(back_x)
    grad_bc = grad_bce[3:].at[count - 3 :].add(back_bc)
    grad_xb = grad_x.astype(jnp.bfloat16)
    grad_rows = lax.all_gather(grad_xb, "fsdp", axis=1, tiled=True)
    column = lax.axis_index("fsdp") * heads_here
    dt_wide = lax.dynamic_update_slice(
        jnp.zeros((count, dt_weight.shape[1]), jnp.float32), grad_dt, (jnp.int32(0), column)
    )
    bc_total, dt_total = lax.psum((grad_bc, dt_wide), "fsdp")
    grad_local = jnp.dot(grad_rows, x_weight.T, preferred_element_type=jnp.float32)
    grad_local = grad_local + jnp.dot(bc_total, bc_weight.T.astype(jnp.float32), precision=exact)
    grad_local = grad_local + jnp.dot(dt_total, dt_weight.T.astype(jnp.float32), precision=exact)
    grad_tokens = grad_local.astype(jnp.bfloat16)
    return (normed.astype(jnp.bfloat16), grad_tokens)


BF = jnp.bfloat16
F32 = jnp.float32
LOG2E = 1.4426950408889634
LANES = 128
NEG = -1e30


def params(mb=60, **kw):
    return pltpu.CompilerParams(vmem_limit_bytes=mb * 1024 * 1024, **kw)


def cost(flops, nbytes):
    return pl.CostEstimate(flops=int(flops), bytes_accessed=int(nbytes), transcendentals=0)


def mm(a, b):
    return jnp.dot(a, b, preferred_element_type=F32)


def mm_nt(a, b):
    return lax.dot_general(a, b, (((1,), (1,)), ((), ())), preferred_element_type=F32)


def mm_tn(a, b):
    return lax.dot_general(a, b, (((0,), (0,)), ((), ())), preferred_element_type=F32)


def split2(v):
    hi = v.astype(BF)
    return hi, (v - hi.astype(F32)).astype(BF)


def iota(shape, dim):
    return lax.broadcasted_iota(jnp.int32, shape, dim)


def doc_start_of(pos, docs_ref, count):
    start = jnp.zeros_like(pos)
    for i in range(count):
        start = jnp.where(docs_ref[i] <= pos, docs_ref[i], start)
    return start


def spread(heads, width):
    shape = (LANES, width)
    row, col = iota(shape, 0), iota(shape, 1)
    head = jnp.right_shift(col, 6)
    return jnp.where((row == head) | (row == head + 16), 1.0, 0.0).astype(BF)


def gather_heads(width):
    shape = (width, LANES)
    return jnp.where(jnp.right_shift(iota(shape, 0), 6) == iota(shape, 1), 1.0, 0.0).astype(BF)


def packed(v):
    hi = v.astype(BF).astype(F32)
    lo = v - hi
    lane = iota(v.shape, 1)
    return jnp.where(lane < 16, hi, pltpu.roll(lo, 16, 1)).astype(BF)


def over_heads(v, gather):
    hi, lo = split2(v)
    return mm(hi, gather) + mm(lo, gather)


def silu_parts(v):
    sig = 1.0 / (1.0 + jnp.exp(-v))
    return v * sig, sig * (1.0 + v * (1.0 - sig))


def small_proj_kernel(tok_ref, bcw_ref, dtw_ref, out_ref, low_ref):
    states = bcw_ref.shape[1]
    heads = dtw_ref.shape[1]
    tok = tok_ref[...]
    out_ref[:, :states], low_ref[...] = split2(mm(tok, bcw_ref[...]))
    hi, lo = split2(mm(tok, dtw_ref[...]))
    shape = (heads, LANES)
    row, col = iota(shape, 0), iota(shape, 1)
    first = jnp.where(row == col, 1.0, 0.0).astype(BF)
    second = jnp.where(row + heads == col, 1.0, 0.0).astype(BF)
    out_ref[:, states:] = (mm(hi, first) + mm(lo, second)).astype(BF)


def small_proj(tokens, bc_weight, dt_weight):
    rows = tokens.shape[0]
    return pl.pallas_call(
        small_proj_kernel,
        out_shape=[
            jax.ShapeDtypeStruct((rows, bc_weight.shape[1] + LANES), BF),
            jax.ShapeDtypeStruct((rows, bc_weight.shape[1]), BF),
        ],
        compiler_params=params(),
        cost_estimate=cost(3e8, 2e6),
        name="small_proj",
    )(tokens, bc_weight, dt_weight)


def piece_kernel(meta_ref, tok_ref, w_ref, out_ref):
    out_ref[...] = mm(tok_ref[...], w_ref[...]).astype(BF)


def proj_piece(tokens, x_weight, block, width):
    rows, depth = tokens.shape
    tiles = width // LANES
    return pl.pallas_call(
        piece_kernel,
        grid_spec=pltpu.PrefetchScalarGridSpec(
            num_scalar_prefetch=1,
            grid=(tiles,),
            in_specs=[
                pl.BlockSpec((rows, depth), lambda i, m: (0, 0)),
                pl.BlockSpec((depth, LANES), lambda i, m: (0, m[0] * tiles + i)),
            ],
            out_specs=pl.BlockSpec((rows, LANES), lambda i, m: (0, i)),
        ),
        out_shape=jax.ShapeDtypeStruct((rows, width), BF),
        compiler_params=params(),
        cost_estimate=cost(2 * rows * depth * width, 2 * depth * width),
        name="proj_piece",
    )(block, tokens, x_weight)


def rim_kernel(meta_ref, ra_ref, rb_ref, own_w_ref, peer_w_ref, bcw_ref, own_ref, send_ref):
    width = own_w_ref.shape[1]
    rows = ra_ref[...] + rb_ref[...]
    shared = mm(rows, bcw_ref[...]).astype(BF)
    own_ref[:, :width] = mm(rows, own_w_ref[...]).astype(BF)
    own_ref[:, width:] = shared
    send_ref[:, :width] = mm(rows, peer_w_ref[...]).astype(BF)
    send_ref[:, width:] = shared


def rim_proj(ra, rb, x_weight, bc_weight, blocks, width):
    rows, depth = ra.shape
    states = bc_weight.shape[1]
    out = jax.ShapeDtypeStruct((rows, width + states), BF)
    full = lambda shape: pl.BlockSpec(shape, lambda i, m: (0, 0))
    return pl.pallas_call(
        rim_kernel,
        grid_spec=pltpu.PrefetchScalarGridSpec(
            num_scalar_prefetch=1,
            grid=(1,),
            in_specs=[
                full((rows, depth)),
                full((rows, depth)),
                pl.BlockSpec((depth, width), lambda i, m: (0, m[0])),
                pl.BlockSpec((depth, width), lambda i, m: (0, m[1])),
                full((depth, states)),
            ],
            out_specs=[full((rows, width + states)), full((rows, width + states))],
        ),
        out_shape=[out, out],
        compiler_params=params(),
        cost_estimate=cost(4 * rows * depth * width, 4 * depth * width),
        name="rim_proj",
    )(blocks, ra, rb, x_weight, x_weight, bc_weight)


def conv_masks(docs_ref, count, base, rows, lanes):
    pos = base + iota((rows, lanes), 0)
    start = doc_start_of(pos, docs_ref, count)
    return [jnp.where(pos - k >= start, 1.0, 0.0) for k in range(1, 4)]


def shared_kernel(
    docs, heads, all_heads, meta_ref, docs_ref, own_ref, xr_ref, cr_ref, dr_ref, rim_own_ref,
    rim_recv_ref, taps_ref, prm_ref, bact_ref, bpre_ref, delta_ref, ramp_ref, sig_ref, rampt_ref,
    dpk_ref, wpk_ref, epk_ref, keep_ref, ext_ref,
):
    k, x, chip = meta_ref[0], meta_ref[1], meta_ref[2]
    rows = own_ref.shape[0]
    total = 2 * rows
    states2 = bact_ref.shape[1]
    base = chip * total
    mine = pl.multiple_of(8 + k * rows, 8)
    other = pl.multiple_of(8 + (1 - k) * rows, 8)
    width = rim_own_ref.shape[1] - states2
    rim = rim_own_ref[:, width:].astype(F32) + rim_recv_ref[:, width:].astype(F32)
    ext_ref[0:8, :] = rim[8:16, :]
    ext_ref[pl.ds(mine, rows), :] = own_ref[:, :states2].astype(F32) + xr_ref[:, :states2].astype(F32)
    ext_ref[pl.ds(other, rows), :] = cr_ref[:, :states2].astype(F32) + dr_ref[:, :states2].astype(F32)

    tile = 64

    def conv(step, _):
        at = pl.multiple_of(step * tile, tile)
        masks = conv_masks(docs_ref, docs, base + at, tile, LANES)
        for lane in range(0, states2, LANES):
            sl = slice(lane, lane + LANES)
            window = ext_ref[pl.ds(at, tile + 8), sl]
            value = window[8:] * taps_ref[0:1, sl]
            for j in range(1, 4):
                value = value + window[8 - j : 8 - j + tile] * taps_ref[j : j + 1, sl] * masks[j - 1]
            bpre_ref[pl.ds(at, tile), sl] = value
            bact_ref[pl.ds(at, tile), sl] = (value / (1.0 + jnp.exp(-value))).astype(BF)
        return 0

    lax.fori_loop(0, total // tile, conv, 0)

    shape = (LANES, LANES)
    row, col = iota(shape, 0), iota(shape, 1)
    first = x * (all_heads // 2) + k * heads
    wanted = (col < heads) & ((row == first + col) | (row == all_heads + first + col))
    select = jnp.where(wanted, 1.0, 0.0).astype(BF)
    square = (rows, rows)
    lower = jnp.where(iota(square, 0) >= iota(square, 1), 1.0, 0.0).astype(BF)
    bias, rate = prm_ref[0:1, :], prm_ref[1:2, :]

    def steps(part, ref_a, ref_b):
        at = pl.multiple_of(part * rows, rows)
        raw = mm(ref_a[:, states2:], select) + mm(ref_b[:, states2:], select) + bias
        delta = jnp.maximum(raw, 0.0) + jnp.log1p(jnp.exp(-jnp.abs(raw)))
        delta_ref[pl.ds(at, rows), :] = delta
        sig_ref[pl.ds(at, rows), :] = 1.0 / (1.0 + jnp.exp(-raw))
        dpk_ref[pl.ds(at, rows), :] = packed(delta)
        hi, rest = split2(delta)
        mid = rest
        low = (delta - hi.astype(F32) - mid.astype(F32)).astype(BF)
        ramp = -(mm(lower, hi) + mm(lower, mid) + mm(lower, low)) * (rate * LOG2E)
        ramp_ref[pl.ds(at, rows), :] = ramp
        rampt_ref[part] = jnp.transpose(ramp)[:16, :]
        begin = base + at
        end = begin + rows - 1
        pos = begin + iota((rows, LANES), 0)
        start = doc_start_of(pos, docs_ref, docs)
        last = doc_start_of(jnp.zeros((1, LANES), jnp.int32) + end, docs_ref, docs)
        final = ramp[rows - 1 : rows, :]
        epk_ref[pl.ds(at, rows), :] = packed(jnp.where(start < begin, jnp.exp2(ramp), 0.0))
        wpk_ref[pl.ds(at, rows), :] = packed(jnp.where(pos >= last, jnp.exp2(final - ramp), 0.0))
        keep_ref[part] = jnp.zeros((8, LANES), F32) + jnp.where(last < begin, jnp.exp2(final), 0.0)

    steps(k, own_ref, xr_ref)
    steps(1 - k, cr_ref, dr_ref)


def shared_maps(meta, doc_starts, own, xr, cr, dr, rim_own, rim_recv, taps, prm, heads, all_heads):
    rows = own.shape[0]
    total, states2 = 2 * rows, own.shape[1] - LANES
    compact = jax.ShapeDtypeStruct((total, LANES), F32)
    compact_b = jax.ShapeDtypeStruct((total, LANES), BF)
    vm = pl.BlockSpec(memory_space=pltpu.VMEM)
    return pl.pallas_call(
        functools.partial(shared_kernel, doc_starts.shape[0], heads, all_heads),
        grid_spec=pltpu.PrefetchScalarGridSpec(
            num_scalar_prefetch=2,
            grid=(),
            in_specs=[vm] * 8,
            out_specs=[vm] * 10,
            scratch_shapes=[pltpu.VMEM((total + 8, states2), F32)],
        ),
        out_shape=[
            jax.ShapeDtypeStruct((total, states2), BF),
            jax.ShapeDtypeStruct((total, states2), F32),
            compact,
            compact,
            compact,
            jax.ShapeDtypeStruct((2, 16, rows), F32),
            compact_b,
            compact_b,
            compact_b,
            jax.ShapeDtypeStruct((2, 8, LANES), F32),
        ],
        compiler_params=params(),
        cost_estimate=cost(4e9, 4e6),
        name="shared_maps",
    )(meta, doc_starts, own, xr, cr, dr, rim_own, rim_recv, taps, prm)


def keep_row(keep, heads, width):
    hi, rest = split2(keep)
    low = (keep - hi.astype(F32) - rest.astype(F32)).astype(BF)
    wide = spread(heads, width)
    lane = iota(keep.shape, 1)
    clean = lambda v: jnp.where(lane < 16, v.astype(F32), 0.0).astype(BF)
    return mm(clean(hi), wide) + mm(clean(rest), wide) + mm(clean(low), wide)


def inner_kernel(
    docs, heads, meta_ref, docs_ref, own_ref, xr_ref, cr_ref, dr_ref, rim_own_ref, rim_recv_ref,
    taps_ref, bact_ref, dpk_ref, wpk_ref, keep_ref, pre_ref, xd_ref, loc_ref, send_ref, ext_ref,
    wx_ref,
):
    k, chip = meta_ref[0], meta_ref[2]
    rows, width = own_ref.shape
    total = 2 * rows
    states = bact_ref.shape[1] // 2
    base = chip * total
    mine = pl.multiple_of(8 + k * rows, 8)
    other = pl.multiple_of(8 + (1 - k) * rows, 8)
    rim = (rim_own_ref[:, :width].astype(F32) + rim_recv_ref[:, :width].astype(F32))
    ext_ref[0:8, :] = rim.astype(BF).astype(F32)[8:16, :]

    def total_of(a, b):
        return (a[...].astype(F32) + b[...].astype(F32)).astype(BF).astype(F32)

    ext_ref[pl.ds(mine, rows), :] = total_of(own_ref, xr_ref)
    ext_ref[pl.ds(other, rows), :] = total_of(cr_ref, dr_ref)
    wide = spread(heads, width)
    tile = 64

    def conv(step, _):
        at = pl.multiple_of(step * tile, tile)
        masks = conv_masks(docs_ref, docs, base + at, tile, LANES)
        dpk = dpk_ref[pl.ds(at, tile), :]
        wpk = wpk_ref[pl.ds(at, tile), :]
        for lane in range(0, width, LANES):
            sl = slice(lane, lane + LANES)
            window = ext_ref[pl.ds(at, tile + 8), sl]
            value = window[8:] * taps_ref[0:1, sl]
            for j in range(1, 4):
                value = value + window[8 - j : 8 - j + tile] * taps_ref[j : j + 1, sl] * masks[j - 1]
            pre_ref[pl.ds(at, tile), sl] = value
            act = value / (1.0 + jnp.exp(-value))
            xd = act * mm(dpk, wide[:, sl])
            xd_ref[pl.ds(at, tile), sl] = xd.astype(BF)
            wx_ref[pl.ds(at, tile), sl] = (xd * mm(wpk, wide[:, sl])).astype(BF)
        return 0

    lax.fori_loop(0, total // tile, conv, 0)
    locs = []
    for part in range(2):
        sl = slice(part * rows, (part + 1) * rows)
        loc = mm_tn(bact_ref[sl, :states], wx_ref[sl, :])
        loc_ref[part] = loc
        locs.append(loc)
    second = keep_row(keep_ref[1], heads, width)[0:1, :]
    state = locs[0] * second + locs[1]
    chips, piece = send_ref.shape[0], send_ref.shape[1]
    for i in range(chips):
        send_ref[i, :, :width] = state[i * piece : (i + 1) * piece, :].astype(BF)
    keep = jnp.where(iota((8, LANES), 1) < 16, keep_ref[0] * keep_ref[1], 0.0)
    hi, mid = split2(keep)
    low = (keep - hi.astype(F32) - mid.astype(F32)).astype(BF)
    row = iota((8, LANES), 0)
    stack = jnp.where(row == 0, hi.astype(F32), jnp.where(row == 1, mid.astype(F32), low.astype(F32)))
    stack = jnp.concatenate([stack, jnp.zeros((piece - 8, LANES), F32)], axis=0).astype(BF)
    for i in range(chips):
        send_ref[i, :, width:] = stack


def inner_maps(
    meta, doc_starts, own, xr, cr, dr, rim_own, rim_recv, taps, bact, dpk, wpk, keep, heads, chips
):
    rows, width = own.shape
    total, states = 2 * rows, bact.shape[1] // 2
    vm = pl.BlockSpec(memory_space=pltpu.VMEM)
    whole = lambda shape: pl.BlockSpec(shape, lambda i, m, d: (0,) * len(shape))
    half = pl.BlockSpec((taps.shape[0], width), lambda i, m, d: (0, m[0]))
    outs = [
        jax.ShapeDtypeStruct((total, width), F32),
        jax.ShapeDtypeStruct((total, width), BF),
        jax.ShapeDtypeStruct((2, states, width), F32),
        jax.ShapeDtypeStruct((chips, states // chips, width + LANES), BF),
    ]
    return pl.pallas_call(
        functools.partial(inner_kernel, doc_starts.shape[0], heads),
        grid_spec=pltpu.PrefetchScalarGridSpec(
            num_scalar_prefetch=2,
            grid=(1,),
            in_specs=[
                whole(own.shape), whole(xr.shape), whole(cr.shape), whole(dr.shape),
                whole(rim_own.shape), whole(rim_recv.shape), half, whole(bact.shape),
                whole(dpk.shape), whole(wpk.shape), whole(keep.shape),
            ],
            out_specs=[whole(o.shape) for o in outs],
            scratch_shapes=[pltpu.VMEM((total + 8, width), F32), pltpu.VMEM((total, width), BF)],
        ),
        out_shape=outs,
        compiler_params=params(),
        cost_estimate=cost(4e9, 4e6),
        name="inner_maps",
    )(meta, doc_starts, own, xr, cr, dr, rim_own, rim_recv, taps, bact, dpk, wpk, keep)


def within_kernel(
    docs, heads, meta_ref, docs_ref, xd_ref, ramp_ref, rampt_ref, own_ref, xr_ref, cr_ref, dr_ref,
    own_low_ref, xr_low_ref, cr_low_ref, dr_low_ref, rim_own_ref, rim_recv_ref, taps_ref, y_ref,
    cbt_ref, cb_ref, gate_ref, ext_ref, high_ref, low_ref,
):
    k, chip = meta_ref[0], meta_ref[2]
    total, width = xd_ref.shape
    rows = total // 2
    states2 = own_low_ref.shape[1]
    states = states2 // 2
    mine = pl.multiple_of(8 + k * rows, 8)
    other = pl.multiple_of(8 + (1 - k) * rows, 8)
    rim = rim_own_ref[:, width:].astype(F32) + rim_recv_ref[:, width:].astype(F32)
    ext_ref[0:8, :] = rim[8:16, :]

    def exact_sum(a, a_low, b, b_low):
        high = a[:, :states2].astype(F32) + b[:, :states2].astype(F32)
        return high + (a_low[...].astype(F32) + b_low[...].astype(F32))

    ext_ref[pl.ds(mine, rows), :] = exact_sum(own_ref, own_low_ref, xr_ref, xr_low_ref)
    ext_ref[pl.ds(other, rows), :] = exact_sum(cr_ref, cr_low_ref, dr_ref, dr_low_ref)
    tile = 64

    def conv(step, _):
        at = pl.multiple_of(step * tile, tile)
        masks = conv_masks(docs_ref, docs, chip * total + at, tile, LANES)
        for lane in range(0, states2, LANES):
            sl = slice(lane, lane + LANES)
            window = ext_ref[pl.ds(at, tile + 8), sl]
            value = window[8:] * taps_ref[0:1, sl]
            for j in range(1, 4):
                value = value + window[8 - j : 8 - j + tile] * taps_ref[j : j + 1, sl] * masks[j - 1]
            high, low = split2(value / (1.0 + jnp.exp(-value)))
            high_ref[pl.ds(at, tile), sl] = high
            low_ref[pl.ds(at, tile), sl] = low
        return 0

    lax.fori_loop(0, total // tile, conv, 0)
    square = (rows, rows)
    lane = iota((rows, LANES), 1)
    for part in range(2):
        sl = slice(part * rows, (part + 1) * rows)
        begin = chip * total + part * rows
        b, c = high_ref[sl, :states], high_ref[sl, states:]
        b_low, c_low = low_ref[sl, :states], low_ref[sl, states:]
        cb_ref[...] = mm_nt(c, b) + (mm_nt(c, b_low) + mm_nt(c_low, b))
        cbt_ref[part] = jnp.transpose(cb_ref[...])
        pos, src = begin + iota(square, 0), begin + iota(square, 1)
        start = doc_start_of(pos, docs_ref, docs)
        gate_ref[...] = jnp.where((src <= pos) & (src >= start), 0.0, NEG)
        for pair in range(heads // 2):
            cols = slice(pair * LANES, (pair + 1) * LANES)
            xd = xd_ref[sl, cols]
            found = []
            for head in (2 * pair, 2 * pair + 1):
                gap = ramp_ref[sl, head : head + 1] - rampt_ref[part, head : head + 1, :]
                high, low = split2(jnp.exp2(gap + gate_ref[...]) * cb_ref[...])
                found.append(mm(high, xd) + mm(low, xd))
            y_ref[sl, cols] = jnp.where(lane < HEAD_DIM, found[0], found[1])


def within(meta, doc_starts, xd, ramp, rampt, smalls, lows, rim_own, rim_recv, taps, heads):
    total, width = xd.shape
    rows, states2 = total // 2, lows[0].shape[1]
    vm = pl.BlockSpec(memory_space=pltpu.VMEM)
    return pl.pallas_call(
        functools.partial(within_kernel, doc_starts.shape[0], heads),
        grid_spec=pltpu.PrefetchScalarGridSpec(
            num_scalar_prefetch=2,
            grid=(),
            in_specs=[vm] * 14,
            out_specs=[vm] * 2,
            scratch_shapes=[
                pltpu.VMEM((rows, rows), F32),
                pltpu.VMEM((rows, rows), F32),
                pltpu.VMEM((total + 8, states2), F32),
                pltpu.VMEM((total, states2), BF),
                pltpu.VMEM((total, states2), BF),
            ],
        ),
        out_shape=[
            jax.ShapeDtypeStruct((total, width), F32),
            jax.ShapeDtypeStruct((2, rows, rows), F32),
        ],
        compiler_params=params(),
        cost_estimate=cost(6e9, 4e6),
        name="within",
    )(meta, doc_starts, xd, ramp, rampt, *smalls, *lows, rim_own, rim_recv, taps)


def chain_kernel(heads, reverse, recv_ref, keep_ref, out_ref):
    chips = recv_ref.shape[0]
    width = out_ref.shape[2]
    state = jnp.zeros(out_ref.shape[1:], F32)
    wide = spread(heads, width)
    for step in range(chips):
        i = chips - 1 - step if reverse else step
        out_ref[i] = state.astype(BF)
        if step < chips - 1:
            factor = mm(keep_ref[i, :, width:], wide)
            factor = factor[0:1] + factor[1:2] + factor[2:3]
            state = state * factor + recv_ref[i, :, :width].astype(F32)


def chain(recv, keeps, heads, width, reverse):
    chips, piece = recv.shape[0], recv.shape[1]
    return pl.pallas_call(
        functools.partial(chain_kernel, heads, reverse),
        out_shape=jax.ShapeDtypeStruct((chips, piece, width), BF),
        compiler_params=params(),
        cost_estimate=cost(1e8, 1e6),
        name="chain",
    )(recv, keeps)


def out_kernel(
    heads, meta_ref, y_ref, state_ref, loc_ref, bact_ref, epk_ref, keep_ref, go_ref, go_recv_ref,
    gain_ref, mix_own_ref, mix_send_ref, dy_ref, edy_ref, dot_ref, both_ref, late_ref, send_ref,
    go_all_ref, mix_ref,
):
    k = meta_ref[0]
    total, width = y_ref.shape
    rows = total // 2
    states = bact_ref.shape[1] // 2
    mine = pl.multiple_of(k * rows, rows)
    other = pl.multiple_of((1 - k) * rows, rows)
    go_all_ref[pl.ds(mine, rows), :] = go_ref[...]
    go_all_ref[pl.ds(other, rows), :] = go_recv_ref[...]
    state = state_ref[...]
    keep0 = keep_row(keep_ref[0], heads, width)[0:1, :]
    both_ref[0] = state
    both_ref[1] = (state.astype(F32) * keep0 + loc_ref[0]).astype(BF)
    wide = spread(heads, width)
    gather = gather_heads(width)
    tile = 128
    per = rows // tile

    def one(step, _):
        at = pl.multiple_of(step * tile, tile)
        sl = pl.ds(at, tile)
        enter = mm(epk_ref[sl, :], wide)
        carried = mm(bact_ref[sl, states:], both_ref[step // per])
        y = y_ref[sl, :] + carried * enter
        u = go_all_ref[sl, :].astype(F32) * gain_ref[...]
        mean = over_heads(y * y, gather) * (1.0 / HEAD_DIM)
        along = over_heads(u * y, gather)
        scale = lax.rsqrt(mean + epsilon)
        cube = scale * scale * scale
        wide_scale = mm(packed(scale), wide)
        wide_back = mm(packed(cube * along * (1.0 / HEAD_DIM)), wide)
        mix_ref[sl, :] = (y * wide_scale * gain_ref[...]).astype(BF)
        dy = u * wide_scale - y * wide_back
        hi, lo = split2(dy)
        for pair in range(width // LANES):
            cols = slice(pair * LANES, (pair + 1) * LANES)
            dy_ref[sl, 2 * pair * LANES : (2 * pair + 1) * LANES] = hi[:, cols]
            dy_ref[sl, (2 * pair + 1) * LANES : (2 * pair + 2) * LANES] = lo[:, cols]
        edy_ref[sl, :] = (dy * enter).astype(BF)
        dot_ref[sl, :] = epsilon * cube * along
        return 0

    lax.fori_loop(0, total // tile, one, 0)
    mix_own_ref[...] = mix_ref[pl.ds(mine, rows), :]
    mix_send_ref[...] = mix_ref[pl.ds(other, rows), :]
    late = mm_tn(bact_ref[rows:, states:], edy_ref[rows:, :])
    late_ref[...] = late
    back = late * keep0 + mm_tn(bact_ref[:rows, states:], edy_ref[:rows, :])
    chips, piece = send_ref.shape[0], send_ref.shape[1]
    for i in range(chips):
        send_ref[i] = back[i * piece : (i + 1) * piece, :].astype(BF)


def outputs_of(meta, y, state, loc, bact, epk, keep, grad_out, go_recv, gain, heads, chips):
    total, width = y.shape
    rows, states = total // 2, bact.shape[1] // 2
    whole = lambda shape: pl.BlockSpec(shape, lambda i, m: (0,) * len(shape))
    half = lambda count: pl.BlockSpec((count, width), lambda i, m: (0, m[0]))
    outs = [
        jax.ShapeDtypeStruct((rows, width), BF),
        jax.ShapeDtypeStruct((rows, width), BF),
        jax.ShapeDtypeStruct((total, 2 * width), BF),
        jax.ShapeDtypeStruct((total, width), BF),
        jax.ShapeDtypeStruct((total, LANES), F32),
        jax.ShapeDtypeStruct((2, states, width), BF),
        jax.ShapeDtypeStruct((states, width), F32),
        jax.ShapeDtypeStruct((chips, states // chips, width), BF),
    ]
    return pl.pallas_call(
        functools.partial(out_kernel, heads),
        grid_spec=pltpu.PrefetchScalarGridSpec(
            num_scalar_prefetch=1,
            grid=(1,),
            in_specs=[
                whole(y.shape), whole(state.shape), whole(loc.shape), whole(bact.shape),
                whole(epk.shape), whole(keep.shape), half(rows), whole(go_recv.shape), half(1),
            ],
            out_specs=[whole(o.shape) for o in outs],
            scratch_shapes=[pltpu.VMEM((total, width), BF), pltpu.VMEM((total, width), BF)],
        ),
        out_shape=outs,
        compiler_params=params(),
        cost_estimate=cost(4e9, 4e6),
        name="outputs_of",
    )(meta, y, state, loc, bact, epk, keep, grad_out, go_recv, gain)


def within_back_kernel(
    docs, heads, meta_ref, docs_ref, dy_ref, edy_ref, both_ref, xd_ref, bact_ref, ramp_ref,
    rampt_ref, cbt_ref, dxd_ref, dbc_ref, gate_ref, sum_ref,
):
    chip = meta_ref[2]
    total, width = xd_ref.shape
    rows = total // 2
    states = bact_ref.shape[1] // 2
    square = (rows, rows)
    lane = iota((rows, LANES), 1)
    for part in range(2):
        sl = slice(part * rows, (part + 1) * rows)
        begin = chip * total + part * rows
        b, c = bact_ref[sl, :states], bact_ref[sl, states:]
        src, pos = begin + iota(square, 0), begin + iota(square, 1)
        start = doc_start_of(pos, docs_ref, docs)
        gate_ref[...] = jnp.where((src <= pos) & (src >= start), 0.0, NEG)
        sum_ref[...] = jnp.zeros(square, F32)
        for pair in range(heads // 2):
            cols = slice(pair * LANES, (pair + 1) * LANES)
            xd = xd_ref[sl, cols]
            dy_both = dy_ref[sl, 2 * pair * LANES : (2 * pair + 2) * LANES]
            dy = dy_both[:, :LANES]
            found = []
            for side, head in enumerate((2 * pair, 2 * pair + 1)):
                keep_side = (lane < HEAD_DIM) if side == 0 else (lane >= HEAD_DIM)
                only = jnp.where(keep_side, xd.astype(F32), 0.0).astype(BF)
                only = jnp.concatenate([only, only], axis=1)
                gap = rampt_ref[part, head : head + 1, :] - ramp_ref[sl, head : head + 1]
                decay = jnp.exp2(gap + gate_ref[...])
                found.append(mm((decay * cbt_ref[part]).astype(BF), dy))
                sum_ref[...] += mm_nt(only, dy_both) * decay
            dxd_ref[sl, cols] = jnp.where(lane < HEAD_DIM, found[0], found[1])
        grad, low = split2(sum_ref[...])
        dbc_ref[sl, :states] = mm(grad, c) + mm(low, c)
        dbc_ref[sl, states:] = mm_tn(grad, b) + mm_tn(low, b) + mm_nt(edy_ref[sl, :], both_ref[part])


def within_back(meta, doc_starts, dy, edy, both, xd, bact, ramp, rampt, cbt, heads):
    total, width = xd.shape
    rows = total // 2
    vm = pl.BlockSpec(memory_space=pltpu.VMEM)
    return pl.pallas_call(
        functools.partial(within_back_kernel, doc_starts.shape[0], heads),
        grid_spec=pltpu.PrefetchScalarGridSpec(
            num_scalar_prefetch=2,
            grid=(),
            in_specs=[vm] * 8,
            out_specs=[vm] * 2,
            scratch_shapes=[pltpu.VMEM((rows, rows), F32)] * 2,
        ),
        out_shape=[
            jax.ShapeDtypeStruct((total, width), F32),
            jax.ShapeDtypeStruct((total, bact.shape[1]), F32),
        ],
        compiler_params=params(),
        cost_estimate=cost(1e10, 6e6),
        name="within_back",
    )(meta, doc_starts, dy, edy, both, xd, bact, ramp, rampt, cbt)


def grads_kernel(
    docs, heads, meta_ref, docs_ref, adj_ref, late_ref, loc_ref, both_ref, dxd_ref, dbc_ref,
    pre_ref, bpre_ref, xd_ref, bact_ref, delta_ref, sig_ref, dpk_ref, wpk_ref, keep_ref, dot_ref,
    prm_ref, taps_ref, taps_bc_ref, own_ref, other_ref, bc_own_ref, bc_other_ref, rim_ref,
    adj2_ref, gx_ref, gb_ref, q_ref, wx_ref, all_ref, bc_all_ref,
):
    k, chip = meta_ref[0], meta_ref[2]
    total, width = dxd_ref.shape
    rows = total // 2
    states2 = bact_ref.shape[1]
    states = states2 // 2
    base = chip * total
    mine = pl.multiple_of(k * rows, rows)
    other = pl.multiple_of((1 - k) * rows, rows)
    keep1 = keep_row(keep_ref[1], heads, width)[0:1, :]
    adj = adj_ref[...].astype(F32)
    early = adj * keep1 + late_ref[...]
    adj2_ref[0] = early.astype(BF)
    adj2_ref[1] = adj_ref[...]
    middle = both_ref[1].astype(F32)
    final = middle * keep1 + loc_ref[1]
    gather = gather_heads(width)
    ends = [
        over_heads(jnp.sum(a * s, axis=0, keepdims=True) + jnp.zeros((8, width), F32), gather)
        for a, s in ((early, middle), (adj, final))
    ]
    wide = spread(heads, width)
    tile = 64
    per = rows // tile
    gx_ref[0:8, :] = jnp.zeros((8, width), F32)
    gx_ref[total + 8 :, :] = jnp.zeros((8, width), F32)
    gb_ref[0:8, :] = jnp.zeros((8, states2), F32)
    gb_ref[total + 8 :, :] = jnp.zeros((8, states2), F32)

    def one(step, _):
        at = pl.multiple_of(step * tile, tile)
        sl = pl.ds(at, tile)
        part = step // per
        b = bact_ref[sl, :states]
        q = jnp.zeros((tile, LANES), F32)
        for lane in range(0, width, LANES):
            ls = slice(lane, lane + LANES)
            far = mm(b, adj2_ref[part, :, ls])
            w = mm(wpk_ref[sl, :], wide[:, ls])
            dxd = dxd_ref[sl, ls] + far * w
            act, slope = silu_parts(pre_ref[sl, ls])
            q = q + over_heads(act * dxd, gather[ls, :])
            gx_ref[pl.ds(pl.multiple_of(at + 8, 8), tile), ls] = dxd * mm(dpk_ref[sl, :], wide[:, ls]) * slope
            wx_ref[sl, ls] = (xd_ref[sl, ls].astype(F32) * w).astype(BF)
        q_ref[sl, :] = q
        return 0

    lax.fori_loop(0, total // tile, one, 0)
    square = (rows, rows)
    upper = jnp.where(iota(square, 0) <= iota(square, 1), 1.0, 0.0).astype(BF)
    rate = prm_ref[1:2, :]
    row = iota((rows, LANES), 0)
    for part in range(2):
        sl = slice(part * rows, (part + 1) * rows)
        q = q_ref[sl, :]
        ramp_grad = dot_ref[sl, :] - delta_ref[sl, :] * q
        ramp_grad = ramp_grad + jnp.where(row == rows - 1, ends[part][0:1, :], 0.0)
        hi, mid = split2(ramp_grad)
        low = (ramp_grad - hi.astype(F32) - mid.astype(F32)).astype(BF)
        later = mm(upper, hi) + mm(upper, mid) + mm(upper, low)
        bc_all_ref[sl, states2:] = ((q - rate * later) * sig_ref[sl, :])
        back = mm_nt(wx_ref[sl, :], adj2_ref[part])
        for lane, grad in ((0, dbc_ref[sl, :states] + back), (states, dbc_ref[sl, states:])):
            ls = slice(lane, lane + states)
            _, slope = silu_parts(bpre_ref[sl, ls])
            gb_ref[8 + part * rows : 8 + (part + 1) * rows, ls] = grad * slope

    def spill(src_ref, taps, at, count, ls):
        window = src_ref[pl.ds(at, count + 8), ls]
        value = window[:count] * taps[0:1, ls]
        pos = base + at - 8 + iota((count, LANES), 0)
        for j in range(1, 4):
            start = doc_start_of(pos + j, docs_ref, docs)
            mask = jnp.where(pos >= start, 1.0, 0.0)
            value = value + window[j : j + count] * taps[j : j + 1, ls] * mask
        return value

    def back(step, _):
        at = pl.multiple_of(step * tile, tile)
        sl = pl.ds(at, tile)
        for lane in range(0, width, LANES):
            ls = slice(lane, lane + LANES)
            all_ref[sl, ls] = spill(gx_ref, taps_ref, pl.multiple_of(at + 8, 8), tile, ls).astype(BF)
        for lane in range(0, states2, LANES):
            ls = slice(lane, lane + LANES)
            bc_all_ref[sl, ls] = spill(gb_ref, taps_bc_ref, pl.multiple_of(at + 8, 8), tile, ls)
        return 0

    lax.fori_loop(0, total // tile, back, 0)
    rim_ref[...] = jnp.zeros(rim_ref.shape, BF)
    pad = jnp.zeros((8, LANES), F32)
    for lane in range(0, width, LANES):
        ls = slice(lane, lane + LANES)
        value = jnp.concatenate([pad, spill(gx_ref, taps_ref, 0, 8, ls)], axis=0)
        rim_ref[:, ls] = value.astype(BF)
    for lane in range(0, states2, LANES):
        ls = slice(lane, lane + LANES)
        value = jnp.concatenate([pad, spill(gb_ref, taps_bc_ref, 0, 8, ls)], axis=0)
        rim_ref[:, width + lane : width + lane + LANES] = value.astype(BF)
    own_ref[...] = all_ref[pl.ds(mine, rows), :]
    other_ref[...] = all_ref[pl.ds(other, rows), :]
    bc_own_ref[...] = bc_all_ref[pl.ds(mine, rows), :]
    bc_other_ref[...] = bc_all_ref[pl.ds(other, rows), :]


def grads_of(
    meta, doc_starts, adj, late, loc, both, dxd, dbc, pre, bpre, xd, bact, delta, sig, dpk, wpk,
    keep, dots, prm, taps, taps_bc, heads,
):
    total, width = dxd.shape
    rows, states2 = total // 2, bact.shape[1]
    states = states2 // 2
    whole = lambda shape: pl.BlockSpec(shape, lambda i, m, d: (0,) * len(shape))
    half = pl.BlockSpec((taps.shape[0], width), lambda i, m, d: (0, m[0]))
    outs = [
        jax.ShapeDtypeStruct((rows, width), BF),
        jax.ShapeDtypeStruct((rows, width), BF),
        jax.ShapeDtypeStruct((rows, states2 + LANES), F32),
        jax.ShapeDtypeStruct((rows, states2 + LANES), F32),
        jax.ShapeDtypeStruct((16, width + states2), BF),
    ]
    ins = [adj, late, loc, both, dxd, dbc, pre, bpre, xd, bact, delta, sig, dpk, wpk, keep, dots, prm]
    return pl.pallas_call(
        functools.partial(grads_kernel, doc_starts.shape[0], heads),
        grid_spec=pltpu.PrefetchScalarGridSpec(
            num_scalar_prefetch=2,
            grid=(1,),
            in_specs=[whole(a.shape) for a in ins] + [half, whole(taps_bc.shape)],
            out_specs=[whole(o.shape) for o in outs],
            scratch_shapes=[
                pltpu.VMEM((2, states, width), BF),
                pltpu.VMEM((total + 16, width), F32),
                pltpu.VMEM((total + 16, states2), F32),
                pltpu.VMEM((total, LANES), F32),
                pltpu.VMEM((total, width), BF),
                pltpu.VMEM((total, width), BF),
                pltpu.VMEM((total, states2 + LANES), F32),
            ],
        ),
        out_shape=outs,
        compiler_params=params(),
        cost_estimate=cost(4e9, 8e6),
        name="grads_of",
    )(meta, doc_starts, *ins, taps, taps_bc)


def join_kernel(heads, meta_ref, own_ref, recv_ref, out_ref, send_ref):
    k = meta_ref[0]
    states2 = own_ref.shape[1] - LANES
    total = own_ref[:, :states2] + recv_ref[:, :states2]
    out_ref[:, :states2] = total
    send_ref[:, :states2] = total.astype(BF)
    shape = (LANES, LANES)
    row, col = iota(shape, 0), iota(shape, 1)
    mine = jnp.where((row < heads) & (col == row + k * heads), 1.0, 0.0).astype(BF)
    other = jnp.where((row < heads) & (col == row + (1 - k) * heads), 1.0, 0.0).astype(BF)
    steps = mm(own_ref[:, states2:].astype(BF), mine) + mm(recv_ref[:, states2:].astype(BF), other)
    out_ref[:, states2:] = steps
    send_ref[:, states2:] = steps.astype(BF)


def join(meta, own, recv, heads):
    vm = pl.BlockSpec(memory_space=pltpu.VMEM)
    return pl.pallas_call(
        functools.partial(join_kernel, heads),
        grid_spec=pltpu.PrefetchScalarGridSpec(
            num_scalar_prefetch=1, grid=(), in_specs=[vm] * 2, out_specs=[vm] * 2
        ),
        out_shape=[jax.ShapeDtypeStruct(own.shape, F32), jax.ShapeDtypeStruct(own.shape, BF)],
        compiler_params=params(),
        cost_estimate=cost(1e8, 1e6),
        name="join",
    )(meta, own, recv)


def first_kernel(meta_ref, mine_ref, other_ref, rim_ref, w_mine_ref, w_other_ref, out_ref):
    rows, width = mine_ref.shape

    def whole(ref, rim):
        tail = ref[rows - 16 :, :].astype(F32) + rim.astype(F32)
        return jnp.concatenate([ref[: rows - 16, :], tail.astype(BF)], axis=0)

    mine = whole(mine_ref, rim_ref[:16, :width])
    other = whole(other_ref, rim_ref[16:, :width])
    out_ref[...] = mm_nt(mine, w_mine_ref[...]) + mm_nt(other, w_other_ref[...])


def first_half(blocks, mine, other, rim, x_weight, tile):
    rows, width = mine.shape
    depth = x_weight.shape[0]
    whole = lambda shape: pl.BlockSpec(shape, lambda i, m: (0, 0))
    return pl.pallas_call(
        first_kernel,
        grid_spec=pltpu.PrefetchScalarGridSpec(
            num_scalar_prefetch=1,
            grid=(depth // tile,),
            in_specs=[
                whole(mine.shape), whole(other.shape), whole(rim.shape),
                pl.BlockSpec((tile, width), lambda i, m: (i, m[0])),
                pl.BlockSpec((tile, width), lambda i, m: (i, m[1])),
            ],
            out_specs=pl.BlockSpec((rows, tile), lambda i, m: (0, i)),
        ),
        out_shape=jax.ShapeDtypeStruct((rows, depth), F32),
        compiler_params=params(),
        cost_estimate=cost(2e9, 4e6),
        name="first_half",
    )(blocks, mine, other, rim, x_weight, x_weight)


def last_kernel(
    heads, side_ref, part_ref, mine_ref, other_ref, rim_ref, rim0_ref, bc_own_ref, bc_recv_ref,
    w_mine_ref, w_other_ref, bcw_ref, dtw_ref, out_ref, bc_ref, dt_ref, left_ref, right_ref,
):
    rows, width = mine_ref.shape
    states2 = bcw_ref.shape[1]
    all_heads = dtw_ref.shape[1]

    @pl.when(pl.program_id(0) == 0)
    def _():
        for ref, rim, to_ref in (
            (mine_ref, rim_ref[:16, :width], left_ref),
            (other_ref, rim_ref[16:, :width], right_ref),
        ):
            to_ref[: rows - 16, :] = ref[: rows - 16, :]
            to_ref[rows - 16 :, :] = (ref[rows - 16 :, :].astype(F32) + rim.astype(F32)).astype(BF)
        bc = bc_own_ref[:, :states2] + bc_recv_ref[:, :states2].astype(F32)
        rim = rim_ref[...].astype(F32) + rim0_ref[...].astype(F32)
        extra = rim[:16, width:] + rim[16:, width:]
        for at, value in ((0, bc[: rows - 16, :]), (rows - 16, bc[rows - 16 :, :] + extra)):
            high, low = split2(value)
            bc_ref[at : at + value.shape[0], :states2] = high
            bc_ref[at : at + value.shape[0], states2:] = low
        shape = (LANES, all_heads)
        row, col = iota(shape, 0), iota(shape, 1)
        x = side_ref[2]
        here = jnp.where((row < heads) & (col == row + x * heads), 1.0, 0.0).astype(BF)
        there = jnp.where((row < heads) & (col == row + (1 - x) * heads), 1.0, 0.0).astype(BF)
        dt_ref[...] = (mm(bc_own_ref[:, states2:].astype(BF), here) + mm(bc_recv_ref[:, states2:], there)).astype(BF)

    total = part_ref[...] + mm_nt(left_ref[...], w_mine_ref[...])
    total = total + mm_nt(right_ref[...], w_other_ref[...])
    bcw = bcw_ref[...]
    total = total + mm_nt(bc_ref[...], jnp.concatenate([bcw, bcw], axis=1)) + mm_nt(dt_ref[...], dtw_ref[...])
    out_ref[...] = total.astype(BF)


def last_half(blocks, part, mine, other, rim, rim0, bc_own, bc_recv, x_weight, bc_weight, dt_weight, tile):
    rows, width = mine.shape
    depth = x_weight.shape[0]
    states2, all_heads = bc_weight.shape[1], dt_weight.shape[1]
    whole = lambda a: pl.BlockSpec(a.shape, lambda i, m: (0, 0))
    return pl.pallas_call(
        functools.partial(last_kernel, all_heads // 2),
        grid_spec=pltpu.PrefetchScalarGridSpec(
            num_scalar_prefetch=1,
            grid=(depth // tile,),
            in_specs=[
                pl.BlockSpec((rows, tile), lambda i, m: (0, i)),
                whole(mine), whole(other), whole(rim), whole(rim0), whole(bc_own), whole(bc_recv),
                pl.BlockSpec((tile, width), lambda i, m: (i, m[0])),
                pl.BlockSpec((tile, width), lambda i, m: (i, m[1])),
                pl.BlockSpec((tile, states2), lambda i, m: (i, 0)),
                pl.BlockSpec((tile, all_heads), lambda i, m: (i, 0)),
            ],
            out_specs=pl.BlockSpec((rows, tile), lambda i, m: (0, i)),
            scratch_shapes=[
                pltpu.VMEM((rows, 2 * states2), BF),
                pltpu.VMEM((rows, all_heads), BF),
                pltpu.VMEM((rows, width), BF),
                pltpu.VMEM((rows, width), BF),
            ],
        ),
        out_shape=jax.ShapeDtypeStruct((rows, depth), BF),
        compiler_params=params(),
        cost_estimate=cost(2e9, 4e6),
        name="last_half",
    )(blocks, part, mine, other, rim, rim0, bc_own, bc_recv, x_weight, x_weight, bc_weight, dt_weight)


def by_chips(
    tokens, x_weight, bc_weight, dt_weight, conv_inner, conv_shared, dt_bias, decay_rate, norm_gain,
    doc_starts, grad_out,
):
    blocks = lax.axis_size("ctx")
    chips = blocks // 2
    rows = tokens.shape[0]
    all_heads = dt_weight.shape[1]
    heads = decay_rate.shape[0] // 2
    width = heads * HEAD_DIM
    place = lax.axis_index("ctx").astype(jnp.int32)
    x = lax.axis_index("fsdp").astype(jnp.int32)
    k = place % 2
    meta = jnp.stack([k, x, place // 2])

    core = [(i, i ^ 1) for i in range(blocks)]
    pair = [(0, 1), (1, 0)]
    cross = [(2 * i + j, 2 * (i ^ 1) + (1 - j)) for i in range(blocks) for j in range(2)]
    by_core = lambda a: lax.ppermute(a, "ctx", core)
    by_x = lambda a: lax.ppermute(a, "fsdp", pair)
    by_both = lambda a: lax.ppermute(a, ("ctx", "fsdp"), cross)
    groups = [[2 * i for i in range(chips)], [2 * i + 1 for i in range(chips)]]
    exchange = lambda a: lax.all_to_all(a, "ctx", 0, 0, axis_index_groups=groups)

    def column_block(side, half):
        return (side * 2 + half)[None]

    tail = tokens[rows - 16 :]
    ra = lax.ppermute(tail, "ctx", [(2 * i - 1, 2 * i) for i in range(1, chips)])
    rb = lax.ppermute(tail, "ctx", [(2 * i - 1, 2 * i + 1) for i in range(1, chips)])

    small, low = small_proj(tokens, bc_weight, dt_weight)
    small_x = by_x(small)
    to_cross = proj_piece(tokens, x_weight, column_block(1 - x, 1 - k), width)
    from_cross = by_both(to_cross)
    to_x = proj_piece(tokens, x_weight, column_block(1 - x, k), width)
    from_x = by_x(to_x)
    to_core = proj_piece(tokens, x_weight, column_block(x, 1 - k), width)
    from_core = by_core(to_core)
    mine = proj_piece(tokens, x_weight, column_block(x, k), width)
    rim_own, rim_send = rim_proj(
        ra, rb, x_weight, bc_weight, jnp.stack([x * 2 + k, (1 - x) * 2 + k]), width
    )
    rim_recv = by_x(rim_send)
    small_core = by_core(small)
    small_cross = by_core(small_x)
    low_x = by_x(low)
    lows = (low, low_x, by_core(low), by_core(low_x))
    go_recv = by_core(lax.dynamic_slice(grad_out, (jnp.int32(0), (1 - k) * width), (rows, width)))

    prm = jnp.stack([lax.dynamic_slice(v, (k * heads,), (heads,)) for v in (dt_bias, decay_rate)])
    prm = jnp.pad(prm, ((0, 6), (0, LANES - heads)))
    bact, bpre, delta, ramp, sig, rampt, dpk, wpk, epk, keep = shared_maps(
        meta, doc_starts, small, small_x, small_core, small_cross, rim_own, rim_recv, conv_shared,
        prm, heads, all_heads,
    )
    pre, xd, loc, send = inner_maps(
        meta, doc_starts, mine, from_x, from_core, from_cross, rim_own, rim_recv, conv_inner, bact,
        dpk, wpk, keep, heads, chips,
    )
    keeps = exchange(send)
    y, cbt = within(
        meta, doc_starts, xd, ramp, rampt, (small, small_x, small_core, small_cross), lows, rim_own, rim_recv,
        conv_shared, heads,
    )
    states = exchange(chain(keeps, keeps, heads, width, False))
    state = states.reshape(STATE, width)
    mix_own, mix_send, dy, edy, dots, both, late, back = outputs_of(
        meta, y, state, loc, bact, epk, keep, grad_out, go_recv, norm_gain[None, :], heads, chips
    )
    backs = exchange(back)
    dxd, dbc = within_back(meta, doc_starts, dy, edy, both, xd, bact, ramp, rampt, cbt, heads)
    mix_recv = by_core(mix_send)
    mixed = jnp.where(
        k == 0,
        jnp.concatenate([mix_own, mix_recv], axis=1),
        jnp.concatenate([mix_recv, mix_own], axis=1),
    )
    adj = exchange(chain(backs, keeps, heads, width, True)).reshape(STATE, width)
    g_mine, g_other, bc_mine, bc_other, rim = grads_of(
        meta, doc_starts, adj, late, loc, both, dxd, dbc, pre, bpre, xd, bact, delta, sig, dpk, wpk,
        keep, dots, prm, conv_inner, conv_shared, heads,
    )
    g_x = by_x(g_mine)
    g_cross = by_both(g_other)
    g_core = by_core(g_other)
    rims = jnp.concatenate([rim, by_core(rim)], axis=0)
    back_perm = [(2 * i + 1, 2 * i - 1) for i in range(1, chips)]
    rim0 = lax.ppermute(rims, "ctx", back_perm)
    rim1 = lax.ppermute(
        rims, ("ctx", "fsdp"), [(2 * a + j, 2 * b + (1 - j)) for a, b in back_perm for j in range(2)]
    )
    bc_chip, bc_send = join(meta, bc_mine, by_core(bc_other), heads)
    bc_recv = by_x(bc_send)
    part = first_half(
        jnp.stack([x * 2 + k, x * 2 + 1 - k]), g_mine, g_core, rim0, x_weight, 256
    )
    grad_tokens = last_half(
        jnp.stack([(1 - x) * 2 + k, (1 - x) * 2 + 1 - k, x]), part, g_x, g_cross, rim1, rim0, bc_chip,
        bc_recv, x_weight, bc_weight, dt_weight, 256,
    )
    return (mixed, grad_tokens)


def splits_by_chip(mesh):
    return mesh.shape["fsdp"] == 2 and mesh.shape["ctx"] == 16


def solution(mesh):
    in_specs = (
        P("ctx", "fsdp"),
        P("fsdp", None),
        P("fsdp", None),
        P("fsdp", None),
        P(None, "fsdp"),
        P(),
        P("fsdp"),
        P("fsdp"),
        P("fsdp"),
        P(),
        P("ctx", "fsdp"),
    )
    body = by_chips if splits_by_chip(mesh) else on_device
    out_specs = (P("ctx", "fsdp"), P("ctx", "fsdp"))
    return jax.shard_map(
        body, mesh=mesh, in_specs=in_specs, out_specs=out_specs, check_vma=False
    )
```

```python
import functools

import jax
import jax.numpy as jnp
from jax import lax
from jax.experimental import pallas as pl
from jax.experimental.pallas import tpu as pltpu
from jax.sharding import PartitionSpec as P

HEAD_DIM = 64
STATE = 128


exact = lax.Precision.HIGHEST
epsilon = 1e-05


def from_behind(value, axis, steps):
    count = lax.axis_size(axis)
    leading, last = (max(0, -steps), min(count, count - steps))
    return lax.ppermute(value, axis, [(source, source + steps) for source in range(leading, last)])


def prefix(part, axis, combine, identity, reverse):
    count = lax.axis_size(axis)
    place = lax.axis_index(axis)
    ahead = count - 1 - place if reverse else place
    gathered = jax.tree.map(lambda a: lax.all_gather(a, axis), part)
    state = jax.tree.map(lambda a, e: jnp.zeros_like(a) + jnp.asarray(e, a.dtype), part, identity)

    def one(step, state):
        source = count - 1 - step if reverse else step
        return combine(
            state, jax.tree.map(lambda a: lax.dynamic_index_in_dim(a, source, 0, False), gathered)
        )

    return lax.fori_loop(0, ahead, one, state)


def doc_index(positions, doc_starts):
    hits = (doc_starts[None, :] <= positions[:, None]).astype(jnp.int32)
    return jnp.sum(hits, axis=1) - 1


def causal_conv(padded, docs_ext, taps):
    count = padded.shape[0] - 3
    docs_now = docs_ext[3:]
    total = jnp.zeros((count, padded.shape[1]), jnp.float32)
    for offset in range(4):
        rows = padded[3 - offset : 3 - offset + count]
        same = (docs_ext[3 - offset : 3 - offset + count] == docs_now).astype(jnp.float32)
        total = total + taps[offset][None, :] * rows * same[:, None]
    return total


def block_out(x_act, b_act, c_act, delta, docs, doc_before, state_in, decay_rate):
    count = delta.shape[0]
    places = jnp.arange(count, dtype=jnp.int32)
    lower = places[:, None] >= places[None, :]
    ramp = -jnp.dot(lower.astype(jnp.float32), delta, precision=exact) * decay_rate[None, :]
    same = jnp.logical_and(docs[:, None] == docs[None, :], lower)
    gap = ramp[:, None, :] - ramp[None, :, :]
    decay = jnp.exp(jnp.where(same[:, :, None], gap, 0.0)) * same.astype(jnp.float32)[:, :, None]
    scores = jnp.dot(c_act, b_act.T, precision=exact)
    mixing = decay * scores[:, :, None] * delta[None, :, :]
    inner = jnp.einsum("tsh,shp->thp", mixing, x_act, precision=exact)
    carried = (docs == doc_before).astype(jnp.float32)
    enter = jnp.exp(ramp) * carried[:, None]
    from_state = jnp.einsum("tn,hpn->thp", c_act, state_in, precision=exact) * enter[:, :, None]
    last_doc = docs[count - 1]
    tail = (
        jnp.exp(ramp[count - 1][None, :] - ramp)
        * (docs == last_doc).astype(jnp.float32)[:, None]
        * delta
    )
    weighted = tail[:, :, None] * x_act
    state_loc = jnp.einsum("shp,sn->hpn", weighted, b_act, precision=exact)
    keep = jnp.exp(ramp[count - 1]) * (last_doc == doc_before).astype(jnp.float32)
    return (inner + from_state, state_loc, keep)


def head_norm(values, norm_gain):
    scale = lax.rsqrt(jnp.mean(values * values, axis=-1, keepdims=True) + epsilon)
    normed = values * scale
    return normed.reshape(values.shape[0], values.shape[1] * values.shape[2]) * norm_gain[None, :]


def link(earlier, later):
    return (earlier[0] * later[0], later[0][:, None, None] * earlier[1] + later[1])


def on_device(
    tokens,
    x_weight,
    bc_weight,
    dt_weight,
    conv_inner,
    conv_shared,
    dt_bias,
    decay_rate,
    norm_gain,
    doc_starts,
    grad_out,
):
    count = tokens.shape[0]
    heads_here = decay_rate.shape[0]
    features = lax.all_gather(tokens, "fsdp", axis=1, tiled=True)
    x_cols, dt_cols = (
        lax.all_to_all(x_weight, "fsdp", split_axis=1, concat_axis=0, tiled=True),
        lax.all_to_all(dt_weight, "fsdp", split_axis=1, concat_axis=0, tiled=True),
    )
    bc_all = lax.all_gather(bc_weight, "fsdp", axis=0, tiled=True)
    x_proj = jnp.dot(features, x_cols, preferred_element_type=jnp.float32).astype(jnp.bfloat16)
    bc_proj = jnp.dot(features, bc_all, preferred_element_type=jnp.float32)
    dt_raw = jnp.dot(features, dt_cols, preferred_element_type=jnp.float32)
    x_wide = lax.optimization_barrier(x_proj).astype(jnp.float32)
    rim_x, rim_bc = from_behind((x_wide[count - 3 :], bc_proj[count - 3 :]), "ctx", 1)
    x_ext = jnp.concatenate([rim_x, x_wide], axis=0)
    bc_ext = jnp.concatenate([rim_bc, bc_proj], axis=0)
    first = lax.axis_index("ctx") * count
    positions = first - 3 + jnp.arange(count + 3, dtype=jnp.int32)
    docs_ext = doc_index(positions, doc_starts)
    docs = docs_ext[3:]
    doc_before = docs_ext[2]

    def layer(x_in, bc_in, dt_in, state_in):
        x_act = jax.nn.silu(causal_conv(x_in, docs_ext, conv_inner))
        bc_act = jax.nn.silu(causal_conv(bc_in, docs_ext, conv_shared))
        delta = jax.nn.softplus(dt_in + dt_bias[None, :])
        values, state_loc, keep = block_out(
            x_act.reshape(count, heads_here, HEAD_DIM),
            bc_act[:, :STATE],
            bc_act[:, STATE:],
            delta,
            docs,
            doc_before,
            state_in,
            decay_rate,
        )
        return (head_norm(values, norm_gain), state_loc, keep)

    blank = jnp.zeros((heads_here, HEAD_DIM, STATE), jnp.float32)
    unit = jnp.ones((heads_here,), jnp.float32)
    _, state_loc, keep = layer(x_ext, bc_ext, dt_raw, blank)
    state_in = prefix((keep, state_loc), "ctx", link, (unit, blank), False)[1]
    outputs, pull = jax.vjp(layer, x_ext, bc_ext, dt_raw, state_in)
    normed = outputs[0]
    grads_out = pull((grad_out.astype(jnp.float32), jnp.zeros_like(blank), jnp.zeros_like(unit)))
    adjoint = prefix((keep, grads_out[3]), "ctx", link, (unit, blank), True)[1]
    keep_grad = jnp.sum(adjoint * state_in, axis=(1, 2))
    grads_state = pull((jnp.zeros_like(normed), adjoint, keep_grad))
    grad_xe = grads_out[0] + grads_state[0]
    grad_bce = grads_out[1] + grads_state[1]
    grad_dt = grads_out[2] + grads_state[2]
    back_x, back_bc = from_behind((grad_xe[:3], grad_bce[:3]), "ctx", -1)
    grad_x = grad_xe[3:].at[count - 3 :].add(back_x)
    grad_bc = grad_bce[3:].at[count - 3 :].add(back_bc)
    grad_xb = grad_x.astype(jnp.bfloat16)
    grad_rows = lax.all_gather(grad_xb, "fsdp", axis=1, tiled=True)
    column = lax.axis_index("fsdp") * heads_here
    dt_wide = lax.dynamic_update_slice(
        jnp.zeros((count, dt_weight.shape[1]), jnp.float32), grad_dt, (jnp.int32(0), column)
    )
    bc_total, dt_total = lax.psum((grad_bc, dt_wide), "fsdp")
    grad_local = jnp.dot(grad_rows, x_weight.T, preferred_element_type=jnp.float32)
    grad_local = grad_local + jnp.dot(bc_total, bc_weight.T.astype(jnp.float32), precision=exact)
    grad_local = grad_local + jnp.dot(dt_total, dt_weight.T.astype(jnp.float32), precision=exact)
    grad_tokens = grad_local.astype(jnp.bfloat16)
    return (normed.astype(jnp.bfloat16), grad_tokens)


BF = jnp.bfloat16
F32 = jnp.float32
LOG2E = 1.4426950408889634
LANES = 128
NEG = -1e30


def params(mb=60, **kw):
    return pltpu.CompilerParams(vmem_limit_bytes=mb * 1024 * 1024, **kw)


def cost(flops, nbytes):
    return pl.CostEstimate(flops=int(flops), bytes_accessed=int(nbytes), transcendentals=0)


def mm(a, b):
    return jnp.dot(a, b, preferred_element_type=F32)


def mm_nt(a, b):
    return lax.dot_general(a, b, (((1,), (1,)), ((), ())), preferred_element_type=F32)


def mm_tn(a, b):
    return lax.dot_general(a, b, (((0,), (0,)), ((), ())), preferred_element_type=F32)


def split2(v):
    hi = v.astype(BF)
    return hi, (v - hi.astype(F32)).astype(BF)


def iota(shape, dim):
    return lax.broadcasted_iota(jnp.int32, shape, dim)


def doc_start_of(pos, docs_ref, count):
    start = jnp.zeros_like(pos)
    for i in range(count):
        start = jnp.where(docs_ref[i] <= pos, docs_ref[i], start)
    return start


def spread(heads, width):
    shape = (LANES, width)
    row, col = iota(shape, 0), iota(shape, 1)
    head = jnp.right_shift(col, 6)
    return jnp.where((row == head) | (row == head + 16), 1.0, 0.0).astype(BF)


def gather_heads(width):
    shape = (width, LANES)
    return jnp.where(jnp.right_shift(iota(shape, 0), 6) == iota(shape, 1), 1.0, 0.0).astype(BF)


def packed(v):
    hi = v.astype(BF).astype(F32)
    lo = v - hi
    lane = iota(v.shape, 1)
    return jnp.where(lane < 16, hi, pltpu.roll(lo, 16, 1)).astype(BF)


def over_heads(v, gather):
    hi, lo = split2(v)
    return mm(hi, gather) + mm(lo, gather)


def silu_parts(v):
    sig = 1.0 / (1.0 + jnp.exp(-v))
    return v * sig, sig * (1.0 + v * (1.0 - sig))


def fetch(src, dst, sem):
    copy = pltpu.make_async_copy(src, dst, sem)
    copy.start()
    return copy


def columns(w_ref, block, width):
    return w_ref.at[:, pl.ds(pl.multiple_of(block * width, LANES), width)]


def lead_kernel(
    meta_ref, tok_hbm, w_hbm, bcw_hbm, dtw_hbm, piece_ref, out_ref, low_ref, tok_ref, w_ref, bcw_ref,
    dtw_ref, sems,
):
    width = w_ref.shape[1]
    get_tok = fetch(tok_hbm, tok_ref, sems.at[0])
    get_w = fetch(columns(w_hbm, meta_ref[0], width), w_ref, sems.at[1])
    get_bcw = fetch(bcw_hbm, bcw_ref, sems.at[2])
    get_dtw = fetch(dtw_hbm, dtw_ref, sems.at[3])
    get_tok.wait()
    get_w.wait()
    piece_ref[...] = mm(tok_ref[...], w_ref[...]).astype(BF)
    get_bcw.wait()
    get_dtw.wait()
    states = bcw_ref.shape[1]
    heads = dtw_ref.shape[0]
    out_ref[:, :states], low_ref[...] = split2(mm(tok_ref[...], bcw_ref[...]))
    hi, lo = split2(mm_nt(tok_ref[...], dtw_ref[...]))
    shape = (heads, LANES)
    row, col = iota(shape, 0), iota(shape, 1)
    first = jnp.where(row == col, 1.0, 0.0).astype(BF)
    second = jnp.where(row + heads == col, 1.0, 0.0).astype(BF)
    out_ref[:, states:] = (mm(hi, first) + mm(lo, second)).astype(BF)


def lead_proj(block, tokens, x_weight, bc_weight, dt_rows, width):
    rows, depth = tokens.shape
    states = bc_weight.shape[1]
    hbm = pl.BlockSpec(memory_space=pl.ANY)
    vm = pl.BlockSpec(memory_space=pltpu.VMEM)
    return pl.pallas_call(
        lead_kernel,
        grid_spec=pltpu.PrefetchScalarGridSpec(
            num_scalar_prefetch=1,
            grid=(),
            in_specs=[hbm] * 4,
            out_specs=[vm] * 3,
            scratch_shapes=[
                pltpu.VMEM((rows, depth), BF),
                pltpu.VMEM((depth, width), BF),
                pltpu.VMEM((depth, states), BF),
                pltpu.VMEM(dt_rows.shape, BF),
                pltpu.SemaphoreType.DMA((4,)),
            ],
        ),
        out_shape=[
            jax.ShapeDtypeStruct((rows, width), BF),
            jax.ShapeDtypeStruct((rows, states + LANES), BF),
            jax.ShapeDtypeStruct((rows, states), BF),
        ],
        compiler_params=params(),
        cost_estimate=cost(2 * rows * depth * width, 3e6),
        name="lead_proj",
    )(block, tokens, x_weight, bc_weight, dt_rows)


def rest_kernel(
    meta_ref, tok_hbm, w_hbm, bcw_hbm, ra_hbm, rb_hbm, peer_ref, core_ref, mine_ref, own_ref, send_ref,
    tok_ref, w_ref, bcw_ref, ra_ref, rb_ref, sems,
):
    width = w_ref.shape[2]
    get_tok = fetch(tok_hbm, tok_ref, sems.at[0])
    get_w = [fetch(columns(w_hbm, meta_ref[i], width), w_ref.at[i], sems.at[1 + i]) for i in range(3)]
    get_bcw = fetch(bcw_hbm, bcw_ref, sems.at[4])
    get_ra = fetch(ra_hbm, ra_ref, sems.at[5])
    get_rb = fetch(rb_hbm, rb_ref, sems.at[6])
    get_tok.wait()
    for i, ref in enumerate((peer_ref, core_ref, mine_ref)):
        get_w[i].wait()
        ref[...] = mm(tok_ref[...], w_ref[i]).astype(BF)
    get_bcw.wait()
    get_ra.wait()
    get_rb.wait()
    rim = ra_ref[...] + rb_ref[...]
    shared = mm(rim, bcw_ref[...]).astype(BF)
    own_ref[:, :width] = mm(rim, w_ref[2]).astype(BF)
    own_ref[:, width:] = shared
    send_ref[:, :width] = mm(rim, w_ref[0]).astype(BF)
    send_ref[:, width:] = shared


def rest_proj(blocks, tokens, x_weight, bc_weight, ra, rb, width):
    rows, depth = tokens.shape
    states = bc_weight.shape[1]
    hbm = pl.BlockSpec(memory_space=pl.ANY)
    vm = pl.BlockSpec(memory_space=pltpu.VMEM)
    piece = jax.ShapeDtypeStruct((rows, width), BF)
    rim = jax.ShapeDtypeStruct((ra.shape[0], width + states), BF)
    return pl.pallas_call(
        rest_kernel,
        grid_spec=pltpu.PrefetchScalarGridSpec(
            num_scalar_prefetch=1,
            grid=(),
            in_specs=[hbm] * 5,
            out_specs=[vm] * 5,
            scratch_shapes=[
                pltpu.VMEM((rows, depth), BF),
                pltpu.VMEM((3, depth, width), BF),
                pltpu.VMEM((depth, states), BF),
                pltpu.VMEM(ra.shape, BF),
                pltpu.VMEM(rb.shape, BF),
                pltpu.SemaphoreType.DMA((7,)),
            ],
        ),
        out_shape=[piece, piece, piece, rim, rim],
        compiler_params=params(),
        cost_estimate=cost(6 * rows * depth * width, 6e6),
        name="rest_proj",
    )(blocks, tokens, x_weight, bc_weight, ra, rb)


def conv_masks(docs_ref, count, base, rows, lanes):
    pos = base + iota((rows, lanes), 0)
    start = doc_start_of(pos, docs_ref, count)
    return [jnp.where(pos - k >= start, 1.0, 0.0) for k in range(1, 4)]


def shared_kernel(
    docs, heads, all_heads, meta_ref, docs_ref, own_ref, xr_ref, cr_ref, dr_ref, rim_own_ref,
    rim_recv_ref, taps_ref, prm_ref, bact_ref, bpre_ref, delta_ref, ramp_ref, sig_ref, rampt_ref,
    dpk_ref, wpk_ref, epk_ref, keep_ref, ext_ref,
):
    k, x, chip = meta_ref[0], meta_ref[1], meta_ref[2]
    rows = own_ref.shape[0]
    total = 2 * rows
    states2 = bact_ref.shape[1]
    base = chip * total
    mine = pl.multiple_of(8 + k * rows, 8)
    other = pl.multiple_of(8 + (1 - k) * rows, 8)
    width = rim_own_ref.shape[1] - states2
    rim = rim_own_ref[:, width:].astype(F32) + rim_recv_ref[:, width:].astype(F32)
    ext_ref[0:8, :] = rim[8:16, :]
    ext_ref[pl.ds(mine, rows), :] = own_ref[:, :states2].astype(F32) + xr_ref[:, :states2].astype(F32)
    ext_ref[pl.ds(other, rows), :] = cr_ref[:, :states2].astype(F32) + dr_ref[:, :states2].astype(F32)

    tile = 64

    def conv(step, _):
        at = pl.multiple_of(step * tile, tile)
        masks = conv_masks(docs_ref, docs, base + at, tile, LANES)
        for lane in range(0, states2, LANES):
            sl = slice(lane, lane + LANES)
            window = ext_ref[pl.ds(at, tile + 8), sl]
            value = window[8:] * taps_ref[0:1, sl]
            for j in range(1, 4):
                value = value + window[8 - j : 8 - j + tile] * taps_ref[j : j + 1, sl] * masks[j - 1]
            bpre_ref[pl.ds(at, tile), sl] = value
            bact_ref[pl.ds(at, tile), sl] = (value / (1.0 + jnp.exp(-value))).astype(BF)
        return 0

    lax.fori_loop(0, total // tile, conv, 0)

    shape = (LANES, LANES)
    row, col = iota(shape, 0), iota(shape, 1)
    first = x * (all_heads // 2) + k * heads
    wanted = (col < heads) & ((row == first + col) | (row == all_heads + first + col))
    select = jnp.where(wanted, 1.0, 0.0).astype(BF)
    square = (rows, rows)
    lower = jnp.where(iota(square, 0) >= iota(square, 1), 1.0, 0.0).astype(BF)
    bias, rate = prm_ref[0:1, :], prm_ref[1:2, :]

    def steps(part, ref_a, ref_b):
        at = pl.multiple_of(part * rows, rows)
        raw = mm(ref_a[:, states2:], select) + mm(ref_b[:, states2:], select) + bias
        delta = jnp.maximum(raw, 0.0) + jnp.log1p(jnp.exp(-jnp.abs(raw)))
        delta_ref[pl.ds(at, rows), :] = delta
        sig_ref[pl.ds(at, rows), :] = 1.0 / (1.0 + jnp.exp(-raw))
        dpk_ref[pl.ds(at, rows), :] = packed(delta)
        hi, rest = split2(delta)
        mid = rest
        low = (delta - hi.astype(F32) - mid.astype(F32)).astype(BF)
        ramp = -(mm(lower, hi) + mm(lower, mid) + mm(lower, low)) * (rate * LOG2E)
        ramp_ref[pl.ds(at, rows), :] = ramp
        rampt_ref[part] = jnp.transpose(ramp)[:16, :]
        begin = base + at
        end = begin + rows - 1
        pos = begin + iota((rows, LANES), 0)
        start = doc_start_of(pos, docs_ref, docs)
        last = doc_start_of(jnp.zeros((1, LANES), jnp.int32) + end, docs_ref, docs)
        final = ramp[rows - 1 : rows, :]
        epk_ref[pl.ds(at, rows), :] = packed(jnp.where(start < begin, jnp.exp2(ramp), 0.0))
        wpk_ref[pl.ds(at, rows), :] = packed(jnp.where(pos >= last, jnp.exp2(final - ramp), 0.0))
        keep_ref[part] = jnp.zeros((8, LANES), F32) + jnp.where(last < begin, jnp.exp2(final), 0.0)

    steps(k, own_ref, xr_ref)
    steps(1 - k, cr_ref, dr_ref)


def shared_maps(meta, doc_starts, own, xr, cr, dr, rim_own, rim_recv, taps, prm, heads, all_heads):
    rows = own.shape[0]
    total, states2 = 2 * rows, own.shape[1] - LANES
    compact = jax.ShapeDtypeStruct((total, LANES), F32)
    compact_b = jax.ShapeDtypeStruct((total, LANES), BF)
    vm = pl.BlockSpec(memory_space=pltpu.VMEM)
    return pl.pallas_call(
        functools.partial(shared_kernel, doc_starts.shape[0], heads, all_heads),
        grid_spec=pltpu.PrefetchScalarGridSpec(
            num_scalar_prefetch=2,
            grid=(),
            in_specs=[vm] * 8,
            out_specs=[vm] * 10,
            scratch_shapes=[pltpu.VMEM((total + 8, states2), F32)],
        ),
        out_shape=[
            jax.ShapeDtypeStruct((total, states2), BF),
            jax.ShapeDtypeStruct((total, states2), F32),
            compact,
            compact,
            compact,
            jax.ShapeDtypeStruct((2, 16, rows), F32),
            compact_b,
            compact_b,
            compact_b,
            jax.ShapeDtypeStruct((2, 8, LANES), F32),
        ],
        compiler_params=params(),
        cost_estimate=cost(4e9, 4e6),
        name="shared_maps",
    )(meta, doc_starts, own, xr, cr, dr, rim_own, rim_recv, taps, prm)


def keep_row(keep, heads, width):
    hi, rest = split2(keep)
    low = (keep - hi.astype(F32) - rest.astype(F32)).astype(BF)
    wide = spread(heads, width)
    lane = iota(keep.shape, 1)
    clean = lambda v: jnp.where(lane < 16, v.astype(F32), 0.0).astype(BF)
    return mm(clean(hi), wide) + mm(clean(rest), wide) + mm(clean(low), wide)


def inner_kernel(
    docs, heads, meta_ref, docs_ref, own_ref, xr_ref, cr_ref, dr_ref, rim_own_ref, rim_recv_ref,
    taps_ref, bact_ref, dpk_ref, wpk_ref, keep_ref, pre_ref, xd_ref, loc_ref, send_ref, ext_ref,
    wx_ref,
):
    k, chip = meta_ref[0], meta_ref[2]
    rows, width = own_ref.shape
    total = 2 * rows
    states = bact_ref.shape[1] // 2
    base = chip * total
    mine = pl.multiple_of(8 + k * rows, 8)
    other = pl.multiple_of(8 + (1 - k) * rows, 8)
    rim = (rim_own_ref[:, :width].astype(F32) + rim_recv_ref[:, :width].astype(F32))
    ext_ref[0:8, :] = rim.astype(BF).astype(F32)[8:16, :]

    def total_of(a, b):
        return (a[...].astype(F32) + b[...].astype(F32)).astype(BF).astype(F32)

    ext_ref[pl.ds(mine, rows), :] = total_of(own_ref, xr_ref)
    ext_ref[pl.ds(other, rows), :] = total_of(cr_ref, dr_ref)
    wide = spread(heads, width)
    tile = 64

    def conv(step, _):
        at = pl.multiple_of(step * tile, tile)
        masks = conv_masks(docs_ref, docs, base + at, tile, LANES)
        dpk = dpk_ref[pl.ds(at, tile), :]
        wpk = wpk_ref[pl.ds(at, tile), :]
        for lane in range(0, width, LANES):
            sl = slice(lane, lane + LANES)
            window = ext_ref[pl.ds(at, tile + 8), sl]
            value = window[8:] * taps_ref[0:1, sl]
            for j in range(1, 4):
                value = value + window[8 - j : 8 - j + tile] * taps_ref[j : j + 1, sl] * masks[j - 1]
            pre_ref[pl.ds(at, tile), sl] = value
            act = value / (1.0 + jnp.exp(-value))
            xd = act * mm(dpk, wide[:, sl])
            xd_ref[pl.ds(at, tile), sl] = xd.astype(BF)
            wx_ref[pl.ds(at, tile), sl] = (xd * mm(wpk, wide[:, sl])).astype(BF)
        return 0

    lax.fori_loop(0, total // tile, conv, 0)
    locs = []
    for part in range(2):
        sl = slice(part * rows, (part + 1) * rows)
        loc = mm_tn(bact_ref[sl, :states], wx_ref[sl, :])
        loc_ref[part] = loc
        locs.append(loc)
    second = keep_row(keep_ref[1], heads, width)[0:1, :]
    state = locs[0] * second + locs[1]
    chips, piece = send_ref.shape[0], send_ref.shape[1]
    for i in range(chips):
        send_ref[i, :, :width] = state[i * piece : (i + 1) * piece, :].astype(BF)
    keep = jnp.where(iota((8, LANES), 1) < 16, keep_ref[0] * keep_ref[1], 0.0)
    hi, mid = split2(keep)
    low = (keep - hi.astype(F32) - mid.astype(F32)).astype(BF)
    row = iota((8, LANES), 0)
    stack = jnp.where(row == 0, hi.astype(F32), jnp.where(row == 1, mid.astype(F32), low.astype(F32)))
    stack = jnp.concatenate([stack, jnp.zeros((piece - 8, LANES), F32)], axis=0).astype(BF)
    for i in range(chips):
        send_ref[i, :, width:] = stack


def inner_maps(
    meta, doc_starts, own, xr, cr, dr, rim_own, rim_recv, taps, bact, dpk, wpk, keep, heads, chips
):
    rows, width = own.shape
    total, states = 2 * rows, bact.shape[1] // 2
    vm = pl.BlockSpec(memory_space=pltpu.VMEM)
    whole = lambda shape: pl.BlockSpec(shape, lambda i, m, d: (0,) * len(shape))
    half = pl.BlockSpec((taps.shape[0], width), lambda i, m, d: (0, m[0]))
    outs = [
        jax.ShapeDtypeStruct((total, width), F32),
        jax.ShapeDtypeStruct((total, width), BF),
        jax.ShapeDtypeStruct((2, states, width), F32),
        jax.ShapeDtypeStruct((chips, states // chips, width + LANES), BF),
    ]
    return pl.pallas_call(
        functools.partial(inner_kernel, doc_starts.shape[0], heads),
        grid_spec=pltpu.PrefetchScalarGridSpec(
            num_scalar_prefetch=2,
            grid=(1,),
            in_specs=[
                whole(own.shape), whole(xr.shape), whole(cr.shape), whole(dr.shape),
                whole(rim_own.shape), whole(rim_recv.shape), half, whole(bact.shape),
                whole(dpk.shape), whole(wpk.shape), whole(keep.shape),
            ],
            out_specs=[whole(o.shape) for o in outs],
            scratch_shapes=[pltpu.VMEM((total + 8, width), F32), pltpu.VMEM((total, width), BF)],
        ),
        out_shape=outs,
        compiler_params=params(),
        cost_estimate=cost(4e9, 4e6),
        name="inner_maps",
    )(meta, doc_starts, own, xr, cr, dr, rim_own, rim_recv, taps, bact, dpk, wpk, keep)


def within_kernel(
    docs, heads, meta_ref, docs_ref, xd_ref, ramp_ref, rampt_ref, own_ref, xr_ref, cr_ref, dr_ref,
    own_low_ref, xr_low_ref, cr_low_ref, dr_low_ref, rim_own_ref, rim_recv_ref, taps_ref, y_ref,
    cbt_ref, cb_ref, gate_ref, ext_ref, high_ref, low_ref,
):
    k, chip = meta_ref[0], meta_ref[2]
    total, width = xd_ref.shape
    rows = total // 2
    states2 = own_low_ref.shape[1]
    states = states2 // 2
    mine = pl.multiple_of(8 + k * rows, 8)
    other = pl.multiple_of(8 + (1 - k) * rows, 8)
    rim = rim_own_ref[:, width:].astype(F32) + rim_recv_ref[:, width:].astype(F32)
    ext_ref[0:8, :] = rim[8:16, :]

    def exact_sum(a, a_low, b, b_low):
        high = a[:, :states2].astype(F32) + b[:, :states2].astype(F32)
        return high + (a_low[...].astype(F32) + b_low[...].astype(F32))

    ext_ref[pl.ds(mine, rows), :] = exact_sum(own_ref, own_low_ref, xr_ref, xr_low_ref)
    ext_ref[pl.ds(other, rows), :] = exact_sum(cr_ref, cr_low_ref, dr_ref, dr_low_ref)
    tile = 64

    def conv(step, _):
        at = pl.multiple_of(step * tile, tile)
        masks = conv_masks(docs_ref, docs, chip * total + at, tile, LANES)
        for lane in range(0, states2, LANES):
            sl = slice(lane, lane + LANES)
            window = ext_ref[pl.ds(at, tile + 8), sl]
            value = window[8:] * taps_ref[0:1, sl]
            for j in range(1, 4):
                value = value + window[8 - j : 8 - j + tile] * taps_ref[j : j + 1, sl] * masks[j - 1]
            high, low = split2(value / (1.0 + jnp.exp(-value)))
            high_ref[pl.ds(at, tile), sl] = high
            low_ref[pl.ds(at, tile), sl] = low
        return 0

    lax.fori_loop(0, total // tile, conv, 0)
    square = (rows, rows)
    lane = iota((rows, LANES), 1)
    for part in range(2):
        sl = slice(part * rows, (part + 1) * rows)
        begin = chip * total + part * rows
        b, c = high_ref[sl, :states], high_ref[sl, states:]
        b_low, c_low = low_ref[sl, :states], low_ref[sl, states:]
        cb_ref[...] = mm_nt(c, b) + (mm_nt(c, b_low) + mm_nt(c_low, b))
        cbt_ref[part] = jnp.transpose(cb_ref[...])
        pos, src = begin + iota(square, 0), begin + iota(square, 1)
        start = doc_start_of(pos, docs_ref, docs)
        gate_ref[...] = jnp.where((src <= pos) & (src >= start), 0.0, NEG)
        for pair in range(heads // 2):
            cols = slice(pair * LANES, (pair + 1) * LANES)
            xd = xd_ref[sl, cols]
            found = []
            for head in (2 * pair, 2 * pair + 1):
                gap = ramp_ref[sl, head : head + 1] - rampt_ref[part, head : head + 1, :]
                high, low = split2(jnp.exp2(gap + gate_ref[...]) * cb_ref[...])
                found.append(mm(high, xd) + mm(low, xd))
            y_ref[sl, cols] = jnp.where(lane < HEAD_DIM, found[0], found[1])


def within(meta, doc_starts, xd, ramp, rampt, smalls, lows, rim_own, rim_recv, taps, heads):
    total, width = xd.shape
    rows, states2 = total // 2, lows[0].shape[1]
    vm = pl.BlockSpec(memory_space=pltpu.VMEM)
    return pl.pallas_call(
        functools.partial(within_kernel, doc_starts.shape[0], heads),
        grid_spec=pltpu.PrefetchScalarGridSpec(
            num_scalar_prefetch=2,
            grid=(),
            in_specs=[vm] * 14,
            out_specs=[vm] * 2,
            scratch_shapes=[
                pltpu.VMEM((rows, rows), F32),
                pltpu.VMEM((rows, rows), F32),
                pltpu.VMEM((total + 8, states2), F32),
                pltpu.VMEM((total, states2), BF),
                pltpu.VMEM((total, states2), BF),
            ],
        ),
        out_shape=[
            jax.ShapeDtypeStruct((total, width), F32),
            jax.ShapeDtypeStruct((2, rows, rows), F32),
        ],
        compiler_params=params(),
        cost_estimate=cost(6e9, 4e6),
        name="within",
    )(meta, doc_starts, xd, ramp, rampt, *smalls, *lows, rim_own, rim_recv, taps)


def chain_kernel(heads, reverse, recv_ref, keep_ref, out_ref):
    chips = recv_ref.shape[0]
    width = out_ref.shape[2]
    state = jnp.zeros(out_ref.shape[1:], F32)
    wide = spread(heads, width)
    for step in range(chips):
        i = chips - 1 - step if reverse else step
        out_ref[i] = state.astype(BF)
        if step < chips - 1:
            factor = mm(keep_ref[i, :, width:], wide)
            factor = factor[0:1] + factor[1:2] + factor[2:3]
            state = state * factor + recv_ref[i, :, :width].astype(F32)


def chain(recv, keeps, heads, width, reverse):
    chips, piece = recv.shape[0], recv.shape[1]
    return pl.pallas_call(
        functools.partial(chain_kernel, heads, reverse),
        out_shape=jax.ShapeDtypeStruct((chips, piece, width), BF),
        compiler_params=params(16),
        cost_estimate=cost(1e8, 1e6),
        name="chain",
    )(recv, keeps)


def out_kernel(
    heads, meta_ref, y_ref, state_ref, loc_ref, bact_ref, epk_ref, keep_ref, go_ref, go_recv_ref,
    gain_ref, mix_own_ref, mix_send_ref, dy_ref, edy_ref, dot_ref, both_ref, late_ref, send_ref,
    go_all_ref, mix_ref,
):
    k = meta_ref[0]
    total, width = y_ref.shape
    rows = total // 2
    states = bact_ref.shape[1] // 2
    mine = pl.multiple_of(k * rows, rows)
    other = pl.multiple_of((1 - k) * rows, rows)
    go_all_ref[pl.ds(mine, rows), :] = go_ref[...]
    go_all_ref[pl.ds(other, rows), :] = go_recv_ref[...]
    state = state_ref[...]
    keep0 = keep_row(keep_ref[0], heads, width)[0:1, :]
    both_ref[0] = state
    middle = state.astype(F32) * keep0 + loc_ref[0]
    both_ref[1] = middle.astype(BF)
    both_ref[2] = (middle * keep_row(keep_ref[1], heads, width)[0:1, :] + loc_ref[1]).astype(BF)
    wide = spread(heads, width)
    gather = gather_heads(width)
    tile = 256
    per = rows // tile

    def one(step, _):
        at = pl.multiple_of(step * tile, tile)
        sl = pl.ds(at, tile)
        enter = mm(epk_ref[sl, :], wide)
        carried = mm(bact_ref[sl, states:], both_ref[step // per])
        y = y_ref[sl, :] + carried * enter
        u = go_all_ref[sl, :].astype(F32) * gain_ref[...]
        mean = over_heads(y * y, gather) * (1.0 / HEAD_DIM)
        along = over_heads(u * y, gather)
        scale = lax.rsqrt(mean + epsilon)
        cube = scale * scale * scale
        wide_scale = mm(packed(scale), wide)
        wide_back = mm(packed(cube * along * (1.0 / HEAD_DIM)), wide)
        mix_ref[sl, :] = (y * wide_scale * gain_ref[...]).astype(BF)
        dy = u * wide_scale - y * wide_back
        hi, lo = split2(dy)
        for pair in range(width // LANES):
            cols = slice(pair * LANES, (pair + 1) * LANES)
            dy_ref[sl, 2 * pair * LANES : (2 * pair + 1) * LANES] = hi[:, cols]
            dy_ref[sl, (2 * pair + 1) * LANES : (2 * pair + 2) * LANES] = lo[:, cols]
        edy_ref[sl, :] = (dy * enter).astype(BF)
        dot_ref[sl, :] = epsilon * cube * along
        return 0

    lax.fori_loop(0, total // tile, one, 0)
    mix_own_ref[...] = mix_ref[pl.ds(mine, rows), :]
    mix_send_ref[...] = mix_ref[pl.ds(other, rows), :]
    late = mm_tn(bact_ref[rows:, states:], edy_ref[rows:, :])
    late_ref[...] = late
    back = late * keep0 + mm_tn(bact_ref[:rows, states:], edy_ref[:rows, :])
    chips, piece = send_ref.shape[0], send_ref.shape[1]
    for i in range(chips):
        send_ref[i] = back[i * piece : (i + 1) * piece, :].astype(BF)


def outputs_of(meta, y, state, loc, bact, epk, keep, grad_out, go_recv, gain, heads, chips):
    total, width = y.shape
    rows, states = total // 2, bact.shape[1] // 2
    whole = lambda shape: pl.BlockSpec(shape, lambda i, m: (0,) * len(shape))
    half = lambda count: pl.BlockSpec((count, width), lambda i, m: (0, m[0]))
    outs = [
        jax.ShapeDtypeStruct((rows, width), BF),
        jax.ShapeDtypeStruct((rows, width), BF),
        jax.ShapeDtypeStruct((total, 2 * width), BF),
        jax.ShapeDtypeStruct((total, width), BF),
        jax.ShapeDtypeStruct((total, LANES), F32),
        jax.ShapeDtypeStruct((3, states, width), BF),
        jax.ShapeDtypeStruct((states, width), F32),
        jax.ShapeDtypeStruct((chips, states // chips, width), BF),
    ]
    return pl.pallas_call(
        functools.partial(out_kernel, heads),
        grid_spec=pltpu.PrefetchScalarGridSpec(
            num_scalar_prefetch=1,
            grid=(1,),
            in_specs=[
                whole(y.shape), whole(state.shape), whole(loc.shape), whole(bact.shape),
                whole(epk.shape), whole(keep.shape), half(rows), whole(go_recv.shape), half(1),
            ],
            out_specs=[whole(o.shape) for o in outs],
            scratch_shapes=[pltpu.VMEM((total, width), BF), pltpu.VMEM((total, width), BF)],
        ),
        out_shape=outs,
        compiler_params=params(),
        cost_estimate=cost(4e9, 4e6),
        name="outputs_of",
    )(meta, y, state, loc, bact, epk, keep, grad_out, go_recv, gain)


def within_back_kernel(
    docs, heads, meta_ref, docs_ref, dy_ref, edy_ref, both_ref, xd_ref, bact_ref, ramp_ref,
    rampt_ref, cbt_ref, act_ref, slope_ref, near_ref, q_ref, dbc_ref, gate_ref, sum_ref,
):
    gather = gather_heads(xd_ref.shape[1])
    chip = meta_ref[2]
    total, width = xd_ref.shape
    rows = total // 2
    states = bact_ref.shape[1] // 2
    square = (rows, rows)
    lane = iota((rows, LANES), 1)
    for part in range(2):
        sl = slice(part * rows, (part + 1) * rows)
        begin = chip * total + part * rows
        b, c = bact_ref[sl, :states], bact_ref[sl, states:]
        src, pos = begin + iota(square, 0), begin + iota(square, 1)
        start = doc_start_of(pos, docs_ref, docs)
        gate_ref[...] = jnp.where((src <= pos) & (src >= start), 0.0, NEG)
        sum_ref[...] = jnp.zeros(square, F32)
        q = jnp.zeros((rows, LANES), F32)
        for pair in range(heads // 2):
            cols = slice(pair * LANES, (pair + 1) * LANES)
            xd = xd_ref[sl, cols]
            dy_both = dy_ref[sl, 2 * pair * LANES : (2 * pair + 2) * LANES]
            dy = dy_both[:, :LANES]
            found = []
            for side, head in enumerate((2 * pair, 2 * pair + 1)):
                keep_side = (lane < HEAD_DIM) if side == 0 else (lane >= HEAD_DIM)
                only = jnp.where(keep_side, xd.astype(F32), 0.0).astype(BF)
                only = jnp.concatenate([only, only], axis=1)
                gap = rampt_ref[part, head : head + 1, :] - ramp_ref[sl, head : head + 1]
                decay = jnp.exp2(gap + gate_ref[...])
                found.append(mm((decay * cbt_ref[part]).astype(BF), dy))
                sum_ref[...] += mm_nt(only, dy_both) * decay
            dxd = jnp.where(lane < HEAD_DIM, found[0], found[1])
            near_ref[sl, cols] = (dxd * slope_ref[sl, cols].astype(F32)).astype(BF)
            q = q + mm((dxd * act_ref[sl, cols].astype(F32)).astype(BF), gather[cols, :])
        q_ref[sl, :] = q
        grad, low = split2(sum_ref[...])
        dbc_ref[sl, :states] = mm(grad, c) + mm(low, c)
        dbc_ref[sl, states:] = mm_tn(grad, b) + mm_tn(low, b) + mm_nt(edy_ref[sl, :], both_ref[part])


def within_back(meta, doc_starts, dy, edy, both, xd, bact, ramp, rampt, cbt, act, slope, heads):
    total, width = xd.shape
    rows = total // 2
    vm = pl.BlockSpec(memory_space=pltpu.VMEM)
    return pl.pallas_call(
        functools.partial(within_back_kernel, doc_starts.shape[0], heads),
        grid_spec=pltpu.PrefetchScalarGridSpec(
            num_scalar_prefetch=2,
            grid=(),
            in_specs=[vm] * 10,
            out_specs=[vm] * 3,
            scratch_shapes=[pltpu.VMEM((rows, rows), F32)] * 2,
        ),
        out_shape=[
            jax.ShapeDtypeStruct((total, width), BF),
            jax.ShapeDtypeStruct((total, LANES), F32),
            jax.ShapeDtypeStruct((total, bact.shape[1]), F32),
        ],
        compiler_params=params(),
        cost_estimate=cost(1e10, 6e6),
        name="within_back",
    )(meta, doc_starts, dy, edy, both, xd, bact, ramp, rampt, cbt, act, slope)


def slopes_kernel(pre_ref, dpk_ref, wpk_ref, act_ref, far_ref, wx_ref, slope_ref, reach_ref):
    total, width = pre_ref.shape
    wide = spread(width // HEAD_DIM, width)
    tile = total // 2
    for at in range(0, total, tile):
        sl = slice(at, at + tile)
        for lane in range(0, width, LANES):
            ls = slice(lane, lane + LANES)
            w = mm(wpk_ref[sl, :], wide[:, ls])
            step = mm(dpk_ref[sl, :], wide[:, ls])
            act, slope = silu_parts(pre_ref[sl, ls])
            slope = slope * step
            act_ref[sl, ls] = act.astype(BF)
            far_ref[sl, ls] = (act * w).astype(BF)
            wx_ref[sl, ls] = (act * step * w).astype(BF)
            slope_ref[sl, ls] = slope.astype(BF)
            reach_ref[sl, ls] = (slope * w).astype(BF)


def slopes_of(pre, dpk, wpk):
    return pl.pallas_call(
        slopes_kernel,
        out_shape=[jax.ShapeDtypeStruct(pre.shape, BF)] * 5,
        compiler_params=params(),
        cost_estimate=cost(2e9, 4e6),
        name="slopes_of",
    )(pre, dpk, wpk)


def back_masks(docs_ref, docs, pos):
    return [jnp.where(pos >= doc_start_of(pos + j, docs_ref, docs), 1.0, 0.0) for j in range(1, 4)]


def conv_back(src_ref, taps, at, count, ls, masks):
    window = src_ref[pl.ds(at, count + 8), ls]
    value = window[:count] * taps[0:1, ls]
    for j in range(1, 4):
        value = value + window[j : j + count] * taps[j : j + 1, ls] * masks[j - 1]
    return value


def grads_kernel(
    docs, heads, meta_ref, docs_ref, adj_ref, late_ref, keep_ref, both_ref, b_ref, near_ref, far_ref,
    wx_ref, reach_ref, q_ref, dbc_ref, bpre_ref, delta_ref, sig_ref, dot_ref, prm_ref, taps_bc_ref,
    taps_ref, own_ref, other_ref, bc_own_ref, bc_other_ref, rim_ref, adj2_ref, gx_ref, gb_ref, all_ref,
    bc_all_ref,
):
    k, chip = meta_ref[0], meta_ref[2]
    total, width = near_ref.shape
    rows = total // 2
    states = b_ref.shape[1]
    states2 = 2 * states
    base = chip * total
    adj = adj_ref[...].astype(F32)
    early = adj * keep_row(keep_ref[1], heads, width)[0:1, :] + late_ref[...]
    adj2_ref[0] = early.astype(BF)
    adj2_ref[1] = adj_ref[...]
    gather = gather_heads(width)
    ends = [
        over_heads(
            jnp.sum(a * both_ref[i].astype(F32), axis=0, keepdims=True) + jnp.zeros((8, width), F32),
            gather,
        )
        for i, a in ((1, early), (2, adj))
    ]
    for ref, lanes in ((gx_ref, width), (gb_ref, states2)):
        ref[0:8, :] = jnp.zeros((8, lanes), F32)
        ref[total + 8 :, :] = jnp.zeros((8, lanes), F32)
    square = (rows, rows)
    upper = jnp.where(iota(square, 0) <= iota(square, 1), 1.0, 0.0).astype(BF)
    rate = prm_ref[1:2, :]
    row = iota((rows, LANES), 0)
    for part in range(2):
        sl = slice(part * rows, (part + 1) * rows)
        inside = slice(8 + part * rows, 8 + (part + 1) * rows)
        q = q_ref[sl, :]
        for lane in range(0, width, LANES):
            ls = slice(lane, lane + LANES)
            back = mm(b_ref[sl, :], adj2_ref[part, :, ls])
            gx_ref[inside, ls] = near_ref[sl, ls].astype(F32) + back * reach_ref[sl, ls].astype(F32)
            q = q + mm((back * far_ref[sl, ls].astype(F32)).astype(BF), gather[ls, :])
        ramp_grad = dot_ref[sl, :] - delta_ref[sl, :] * q
        ramp_grad = ramp_grad + jnp.where(row == rows - 1, ends[part][0:1, :], 0.0)
        hi, lo = split2(ramp_grad)
        later = mm(upper, hi) + mm(upper, lo)
        bc_all_ref[sl, states2:] = (q - rate * later) * sig_ref[sl, :]
        back = mm_nt(wx_ref[sl, :], adj2_ref[part])
        for lane, grad in ((0, dbc_ref[sl, :states] + back), (states, dbc_ref[sl, states:])):
            ls = slice(lane, lane + states)
            _, slope = silu_parts(bpre_ref[sl, ls])
            gb_ref[inside, ls] = grad * slope
    tile = 64

    def back(step, _):
        at = pl.multiple_of(step * tile, tile)
        begin = pl.multiple_of(at + 8, 8)
        masks = back_masks(docs_ref, docs, base + at + iota((tile, LANES), 0))
        for lane in range(0, width, LANES):
            ls = slice(lane, lane + LANES)
            all_ref[pl.ds(at, tile), ls] = conv_back(gx_ref, taps_ref, begin, tile, ls, masks).astype(BF)
        for lane in range(0, states2, LANES):
            ls = slice(lane, lane + LANES)
            bc_all_ref[pl.ds(at, tile), ls] = conv_back(gb_ref, taps_bc_ref, begin, tile, ls, masks)
        return 0

    lax.fori_loop(0, total // tile, back, 0)
    pad = jnp.zeros((8, LANES), F32)
    masks = back_masks(docs_ref, docs, base - 8 + iota((8, LANES), 0))
    for src, taps, first, lanes in ((gx_ref, taps_ref, 0, width), (gb_ref, taps_bc_ref, width, states2)):
        for lane in range(0, lanes, LANES):
            value = conv_back(src, taps, 0, 8, slice(lane, lane + LANES), masks)
            value = jnp.concatenate([pad, value], axis=0)
            rim_ref[:, first + lane : first + lane + LANES] = value.astype(BF)
    mine = pl.ds(pl.multiple_of(k * rows, rows), rows)
    other = pl.ds(pl.multiple_of((1 - k) * rows, rows), rows)
    own_ref[...] = all_ref[mine, :]
    other_ref[...] = all_ref[other, :]
    bc_own_ref[...] = bc_all_ref[mine, :]
    bc_other_ref[...] = bc_all_ref[other, :]


def grads_of(
    meta, doc_starts, adj, late, keep, both, bact, near, far, wx, reach, q, dbc, bpre, delta, sig, dots,
    prm, taps_bc, taps, heads,
):
    total, width = near.shape
    rows, states2 = total // 2, bact.shape[1]
    states = states2 // 2
    whole = lambda shape: pl.BlockSpec(shape, lambda i, m, d: (0,) * len(shape))
    half = pl.BlockSpec((taps.shape[0], width), lambda i, m, d: (0, m[0]))
    first = pl.BlockSpec((total, states), lambda i, m, d: (0, 0))
    ins = [near, far, wx, reach, q, dbc, bpre, delta, sig, dots, prm, taps_bc]
    outs = [
        jax.ShapeDtypeStruct((rows, width), BF),
        jax.ShapeDtypeStruct((rows, width), BF),
        jax.ShapeDtypeStruct((rows, states2 + LANES), F32),
        jax.ShapeDtypeStruct((rows, states2 + LANES), F32),
        jax.ShapeDtypeStruct((16, width + states2), BF),
    ]
    return pl.pallas_call(
        functools.partial(grads_kernel, doc_starts.shape[0], heads),
        grid_spec=pltpu.PrefetchScalarGridSpec(
            num_scalar_prefetch=2,
            grid=(1,),
            in_specs=[whole(a.shape) for a in (adj, late, keep, both)]
            + [first]
            + [whole(a.shape) for a in ins]
            + [half],
            out_specs=[whole(o.shape) for o in outs],
            scratch_shapes=[
                pltpu.VMEM((2, states, width), BF),
                pltpu.VMEM((total + 16, width), F32),
                pltpu.VMEM((total + 16, states2), F32),
                pltpu.VMEM((total, width), BF),
                pltpu.VMEM((total, states2 + LANES), F32),
            ],
        ),
        out_shape=outs,
        compiler_params=params(),
        cost_estimate=cost(4e9, 8e6),
        name="grads_of",
    )(meta, doc_starts, adj, late, keep, both, bact, *ins, taps)


def join_kernel(heads, meta_ref, own_ref, recv_ref, out_ref, send_ref):
    k = meta_ref[0]
    states2 = own_ref.shape[1] - LANES
    total = own_ref[:, :states2] + recv_ref[:, :states2]
    out_ref[:, :states2] = total
    send_ref[:, :states2] = total.astype(BF)
    shape = (LANES, LANES)
    row, col = iota(shape, 0), iota(shape, 1)
    mine = jnp.where((row < heads) & (col == row + k * heads), 1.0, 0.0).astype(BF)
    other = jnp.where((row < heads) & (col == row + (1 - k) * heads), 1.0, 0.0).astype(BF)
    steps = mm(own_ref[:, states2:].astype(BF), mine) + mm(recv_ref[:, states2:].astype(BF), other)
    out_ref[:, states2:] = steps
    send_ref[:, states2:] = steps.astype(BF)


def join(meta, own, recv, heads):
    vm = pl.BlockSpec(memory_space=pltpu.VMEM)
    return pl.pallas_call(
        functools.partial(join_kernel, heads),
        grid_spec=pltpu.PrefetchScalarGridSpec(
            num_scalar_prefetch=1, grid=(), in_specs=[vm] * 2, out_specs=[vm] * 2
        ),
        out_shape=[jax.ShapeDtypeStruct(own.shape, F32), jax.ShapeDtypeStruct(own.shape, BF)],
        compiler_params=params(16),
        cost_estimate=cost(1e8, 1e6),
        name="join",
    )(meta, own, recv)


def first_kernel(meta_ref, mine_ref, other_ref, rim_ref, w_mine_ref, w_other_ref, out_ref):
    rows, width = mine_ref.shape

    def whole(ref, rim):
        tail = ref[rows - 16 :, :].astype(F32) + rim.astype(F32)
        return jnp.concatenate([ref[: rows - 16, :], tail.astype(BF)], axis=0)

    mine = whole(mine_ref, rim_ref[:16, :width])
    other = whole(other_ref, rim_ref[16:, :width])
    out_ref[...] = mm_nt(mine, w_mine_ref[...]) + mm_nt(other, w_other_ref[...])


def first_half(blocks, mine, other, rim, x_weight, tile):
    rows, width = mine.shape
    depth = x_weight.shape[0]
    whole = lambda shape: pl.BlockSpec(shape, lambda i, m: (0, 0))
    return pl.pallas_call(
        first_kernel,
        grid_spec=pltpu.PrefetchScalarGridSpec(
            num_scalar_prefetch=1,
            grid=(depth // tile,),
            in_specs=[
                whole(mine.shape), whole(other.shape), whole(rim.shape),
                pl.BlockSpec((tile, width), lambda i, m: (i, m[0])),
                pl.BlockSpec((tile, width), lambda i, m: (i, m[1])),
            ],
            out_specs=pl.BlockSpec((rows, tile), lambda i, m: (0, i)),
        ),
        out_shape=jax.ShapeDtypeStruct((rows, depth), F32),
        compiler_params=params(16),
        cost_estimate=cost(2e9, 4e6),
        name="first_half",
    )(blocks, mine, other, rim, x_weight, x_weight)


def last_kernel(
    heads, side_ref, part_ref, mine_ref, other_ref, rim_ref, rim0_ref, bc_own_ref, bc_recv_ref,
    w_mine_ref, w_other_ref, bcw_ref, dtw_ref, out_ref, bc_ref, dt_ref, left_ref, right_ref,
):
    rows, width = mine_ref.shape
    states2 = bcw_ref.shape[1]
    all_heads = dtw_ref.shape[0]

    @pl.when(pl.program_id(0) == 0)
    def _():
        for ref, rim, to_ref in (
            (mine_ref, rim_ref[:16, :width], left_ref),
            (other_ref, rim_ref[16:, :width], right_ref),
        ):
            to_ref[: rows - 16, :] = ref[: rows - 16, :]
            to_ref[rows - 16 :, :] = (ref[rows - 16 :, :].astype(F32) + rim.astype(F32)).astype(BF)
        bc = bc_own_ref[:, :states2] + bc_recv_ref[:, :states2].astype(F32)
        rim = rim_ref[...].astype(F32) + rim0_ref[...].astype(F32)
        extra = rim[:16, width:] + rim[16:, width:]
        for at, value in ((0, bc[: rows - 16, :]), (rows - 16, bc[rows - 16 :, :] + extra)):
            high, low = split2(value)
            bc_ref[at : at + value.shape[0], :states2] = high
            bc_ref[at : at + value.shape[0], states2:] = low
        shape = (LANES, all_heads)
        row, col = iota(shape, 0), iota(shape, 1)
        x = side_ref[2]
        here = jnp.where((row < heads) & (col == row + x * heads), 1.0, 0.0).astype(BF)
        there = jnp.where((row < heads) & (col == row + (1 - x) * heads), 1.0, 0.0).astype(BF)
        dt_ref[...] = (mm(bc_own_ref[:, states2:].astype(BF), here) + mm(bc_recv_ref[:, states2:], there)).astype(BF)

    total = part_ref[...] + mm_nt(left_ref[...], w_mine_ref[...])
    total = total + mm_nt(right_ref[...], w_other_ref[...])
    bcw = bcw_ref[...]
    total = total + mm_nt(bc_ref[...], jnp.concatenate([bcw, bcw], axis=1)) + mm(dt_ref[...], dtw_ref[...])
    out_ref[...] = total.astype(BF)


def last_half(blocks, part, mine, other, rim, rim0, bc_own, bc_recv, x_weight, bc_weight, dt_rows, tile):
    rows, width = mine.shape
    depth = x_weight.shape[0]
    states2, all_heads = bc_weight.shape[1], dt_rows.shape[0]
    whole = lambda a: pl.BlockSpec(a.shape, lambda i, m: (0, 0))
    return pl.pallas_call(
        functools.partial(last_kernel, all_heads // 2),
        grid_spec=pltpu.PrefetchScalarGridSpec(
            num_scalar_prefetch=1,
            grid=(depth // tile,),
            in_specs=[
                pl.BlockSpec((rows, tile), lambda i, m: (0, i)),
                whole(mine), whole(other), whole(rim), whole(rim0), whole(bc_own), whole(bc_recv),
                pl.BlockSpec((tile, width), lambda i, m: (i, m[0])),
                pl.BlockSpec((tile, width), lambda i, m: (i, m[1])),
                pl.BlockSpec((tile, states2), lambda i, m: (i, 0)),
                pl.BlockSpec((all_heads, tile), lambda i, m: (0, i)),
            ],
            out_specs=pl.BlockSpec((rows, tile), lambda i, m: (0, i)),
            scratch_shapes=[
                pltpu.VMEM((rows, 2 * states2), BF),
                pltpu.VMEM((rows, all_heads), BF),
                pltpu.VMEM((rows, width), BF),
                pltpu.VMEM((rows, width), BF),
            ],
        ),
        out_shape=jax.ShapeDtypeStruct((rows, depth), BF),
        compiler_params=params(16),
        cost_estimate=cost(2e9, 4e6),
        name="last_half",
    )(blocks, part, mine, other, rim, rim0, bc_own, bc_recv, x_weight, x_weight, bc_weight, dt_rows)


def by_chips(
    tokens, x_weight, bc_weight, dt_weight, conv_inner, conv_shared, dt_bias, decay_rate, norm_gain,
    doc_starts, grad_out,
):
    blocks = lax.axis_size("ctx")
    chips = blocks // 2
    rows = tokens.shape[0]
    all_heads = dt_weight.shape[1]
    heads = decay_rate.shape[0] // 2
    width = heads * HEAD_DIM
    place = lax.axis_index("ctx").astype(jnp.int32)
    x = lax.axis_index("fsdp").astype(jnp.int32)
    k = place % 2
    meta = jnp.stack([k, x, place // 2])

    core = [(i, i ^ 1) for i in range(blocks)]
    pair = [(0, 1), (1, 0)]
    cross = [(2 * i + j, 2 * (i ^ 1) + (1 - j)) for i in range(blocks) for j in range(2)]
    by_core = lambda a: lax.ppermute(a, "ctx", core)
    by_x = lambda a: lax.ppermute(a, "fsdp", pair)
    by_both = lambda a: lax.ppermute(a, ("ctx", "fsdp"), cross)
    groups = [[2 * i for i in range(chips)], [2 * i + 1 for i in range(chips)]]
    exchange = lambda a: lax.all_to_all(a, "ctx", 0, 0, axis_index_groups=groups)

    def column_block(side, half):
        return (side * 2 + half)[None]

    tail = tokens[rows - 16 :]
    ra = lax.ppermute(tail, "ctx", [(2 * i - 1, 2 * i) for i in range(1, chips)])
    rb = lax.ppermute(tail, "ctx", [(2 * i - 1, 2 * i + 1) for i in range(1, chips)])

    dt_rows = dt_weight.T
    to_cross, small, low = lead_proj(
        column_block(1 - x, 1 - k), tokens, x_weight, bc_weight, dt_rows, width
    )
    from_cross = by_both(to_cross)
    small_x = by_x(small)
    to_x, to_core, mine, rim_own, rim_send = rest_proj(
        jnp.stack([(1 - x) * 2 + k, x * 2 + 1 - k, x * 2 + k]), tokens, x_weight, bc_weight, ra, rb, width
    )
    from_x = by_x(to_x)
    from_core = by_core(to_core)
    rim_recv = by_x(rim_send)
    small_core = by_core(small)
    small_cross = by_core(small_x)
    low_x = by_x(low)
    lows = (low, low_x, by_core(low), by_core(low_x))
    go_recv = by_core(lax.dynamic_slice(grad_out, (jnp.int32(0), (1 - k) * width), (rows, width)))

    prm = jnp.stack([lax.dynamic_slice(v, (k * heads,), (heads,)) for v in (dt_bias, decay_rate)])
    prm = jnp.pad(prm, ((0, 6), (0, LANES - heads)))
    bact, bpre, delta, ramp, sig, rampt, dpk, wpk, epk, keep = shared_maps(
        meta, doc_starts, small, small_x, small_core, small_cross, rim_own, rim_recv, conv_shared,
        prm, heads, all_heads,
    )
    pre, xd, loc, send = inner_maps(
        meta, doc_starts, mine, from_x, from_core, from_cross, rim_own, rim_recv, conv_inner, bact,
        dpk, wpk, keep, heads, chips,
    )
    keeps = exchange(send)
    y, cbt = within(
        meta, doc_starts, xd, ramp, rampt, (small, small_x, small_core, small_cross), lows, rim_own, rim_recv,
        conv_shared, heads,
    )
    states = exchange(chain(keeps, keeps, heads, width, False))
    state = states.reshape(STATE, width)
    mix_own, mix_send, dy, edy, dots, both, late, back = outputs_of(
        meta, y, state, loc, bact, epk, keep, grad_out, go_recv, norm_gain[None, :], heads, chips
    )
    act, far, wx, slope, reach = slopes_of(pre, dpk, wpk)
    backs = exchange(back)
    near, q, dbc = within_back(
        meta, doc_starts, dy, edy, both, xd, bact, ramp, rampt, cbt, act, slope, heads
    )
    mix_recv = by_core(mix_send)
    mixed = jnp.where(
        k == 0,
        jnp.concatenate([mix_own, mix_recv], axis=1),
        jnp.concatenate([mix_recv, mix_own], axis=1),
    )
    adj = exchange(chain(backs, keeps, heads, width, True)).reshape(STATE, width)
    g_mine, g_other, bc_mine, bc_other, rim = grads_of(
        meta, doc_starts, adj, late, keep, both, bact, near, far, wx, reach, q, dbc, bpre, delta, sig,
        dots, prm, conv_shared, conv_inner, heads,
    )
    g_x = by_x(g_mine)
    g_cross = by_both(g_other)
    g_core = by_core(g_other)
    rims = jnp.concatenate([rim, by_core(rim)], axis=0)
    back_perm = [(2 * i + 1, 2 * i - 1) for i in range(1, chips)]
    rim0 = lax.ppermute(rims, "ctx", back_perm)
    rim1 = lax.ppermute(
        rims, ("ctx", "fsdp"), [(2 * a + j, 2 * b + (1 - j)) for a, b in back_perm for j in range(2)]
    )
    bc_chip, bc_send = join(meta, bc_mine, by_core(bc_other), heads)
    bc_recv = by_x(bc_send)
    part = first_half(
        jnp.stack([x * 2 + k, x * 2 + 1 - k]), g_mine, g_core, rim0, x_weight, 640
    )
    grad_tokens = last_half(
        jnp.stack([(1 - x) * 2 + k, (1 - x) * 2 + 1 - k, x]), part, g_x, g_cross, rim1, rim0, bc_chip,
        bc_recv, x_weight, bc_weight, dt_rows, 640,
    )
    return (mixed, grad_tokens)


def splits_by_chip(mesh):
    return mesh.shape["fsdp"] == 2 and mesh.shape["ctx"] == 16


def solution(mesh):
    in_specs = (
        P("ctx", "fsdp"),
        P("fsdp", None),
        P("fsdp", None),
        P("fsdp", None),
        P(None, "fsdp"),
        P(),
        P("fsdp"),
        P("fsdp"),
        P("fsdp"),
        P(),
        P("ctx", "fsdp"),
    )
    body = by_chips if splits_by_chip(mesh) else on_device
    out_specs = (P("ctx", "fsdp"), P("ctx", "fsdp"))
    return jax.shard_map(
        body, mesh=mesh, in_specs=in_specs, out_specs=out_specs, check_vma=False
    )
```

```python
import functools

import jax
import jax.numpy as jnp
from jax import lax
from jax.experimental import pallas as pl
from jax.experimental.pallas import tpu as pltpu
from jax.sharding import PartitionSpec as P

HEAD_DIM = 64
STATE = 128


exact = lax.Precision.HIGHEST
epsilon = 1e-05


def from_behind(value, axis, steps):
    count = lax.axis_size(axis)
    leading, last = (max(0, -steps), min(count, count - steps))
    return lax.ppermute(value, axis, [(source, source + steps) for source in range(leading, last)])


def prefix(part, axis, combine, identity, reverse):
    count = lax.axis_size(axis)
    place = lax.axis_index(axis)
    ahead = count - 1 - place if reverse else place
    gathered = jax.tree.map(lambda a: lax.all_gather(a, axis), part)
    state = jax.tree.map(lambda a, e: jnp.zeros_like(a) + jnp.asarray(e, a.dtype), part, identity)

    def one(step, state):
        source = count - 1 - step if reverse else step
        return combine(
            state, jax.tree.map(lambda a: lax.dynamic_index_in_dim(a, source, 0, False), gathered)
        )

    return lax.fori_loop(0, ahead, one, state)


def doc_index(positions, doc_starts):
    hits = (doc_starts[None, :] <= positions[:, None]).astype(jnp.int32)
    return jnp.sum(hits, axis=1) - 1


def causal_conv(padded, docs_ext, taps):
    count = padded.shape[0] - 3
    docs_now = docs_ext[3:]
    total = jnp.zeros((count, padded.shape[1]), jnp.float32)
    for offset in range(4):
        rows = padded[3 - offset : 3 - offset + count]
        same = (docs_ext[3 - offset : 3 - offset + count] == docs_now).astype(jnp.float32)
        total = total + taps[offset][None, :] * rows * same[:, None]
    return total


def block_out(x_act, b_act, c_act, delta, docs, doc_before, state_in, decay_rate):
    count = delta.shape[0]
    places = jnp.arange(count, dtype=jnp.int32)
    lower = places[:, None] >= places[None, :]
    ramp = -jnp.dot(lower.astype(jnp.float32), delta, precision=exact) * decay_rate[None, :]
    same = jnp.logical_and(docs[:, None] == docs[None, :], lower)
    gap = ramp[:, None, :] - ramp[None, :, :]
    decay = jnp.exp(jnp.where(same[:, :, None], gap, 0.0)) * same.astype(jnp.float32)[:, :, None]
    scores = jnp.dot(c_act, b_act.T, precision=exact)
    mixing = decay * scores[:, :, None] * delta[None, :, :]
    inner = jnp.einsum("tsh,shp->thp", mixing, x_act, precision=exact)
    carried = (docs == doc_before).astype(jnp.float32)
    enter = jnp.exp(ramp) * carried[:, None]
    from_state = jnp.einsum("tn,hpn->thp", c_act, state_in, precision=exact) * enter[:, :, None]
    last_doc = docs[count - 1]
    tail = (
        jnp.exp(ramp[count - 1][None, :] - ramp)
        * (docs == last_doc).astype(jnp.float32)[:, None]
        * delta
    )
    weighted = tail[:, :, None] * x_act
    state_loc = jnp.einsum("shp,sn->hpn", weighted, b_act, precision=exact)
    keep = jnp.exp(ramp[count - 1]) * (last_doc == doc_before).astype(jnp.float32)
    return (inner + from_state, state_loc, keep)


def head_norm(values, norm_gain):
    scale = lax.rsqrt(jnp.mean(values * values, axis=-1, keepdims=True) + epsilon)
    normed = values * scale
    return normed.reshape(values.shape[0], values.shape[1] * values.shape[2]) * norm_gain[None, :]


def link(earlier, later):
    return (earlier[0] * later[0], later[0][:, None, None] * earlier[1] + later[1])


def on_device(
    tokens,
    x_weight,
    bc_weight,
    dt_weight,
    conv_inner,
    conv_shared,
    dt_bias,
    decay_rate,
    norm_gain,
    doc_starts,
    grad_out,
):
    count = tokens.shape[0]
    heads_here = decay_rate.shape[0]
    features = lax.all_gather(tokens, "fsdp", axis=1, tiled=True)
    x_cols, dt_cols = (
        lax.all_to_all(x_weight, "fsdp", split_axis=1, concat_axis=0, tiled=True),
        lax.all_to_all(dt_weight, "fsdp", split_axis=1, concat_axis=0, tiled=True),
    )
    bc_all = lax.all_gather(bc_weight, "fsdp", axis=0, tiled=True)
    x_proj = jnp.dot(features, x_cols, preferred_element_type=jnp.float32).astype(jnp.bfloat16)
    bc_proj = jnp.dot(features, bc_all, preferred_element_type=jnp.float32)
    dt_raw = jnp.dot(features, dt_cols, preferred_element_type=jnp.float32)
    x_wide = lax.optimization_barrier(x_proj).astype(jnp.float32)
    rim_x, rim_bc = from_behind((x_wide[count - 3 :], bc_proj[count - 3 :]), "ctx", 1)
    x_ext = jnp.concatenate([rim_x, x_wide], axis=0)
    bc_ext = jnp.concatenate([rim_bc, bc_proj], axis=0)
    first = lax.axis_index("ctx") * count
    positions = first - 3 + jnp.arange(count + 3, dtype=jnp.int32)
    docs_ext = doc_index(positions, doc_starts)
    docs = docs_ext[3:]
    doc_before = docs_ext[2]

    def layer(x_in, bc_in, dt_in, state_in):
        x_act = jax.nn.silu(causal_conv(x_in, docs_ext, conv_inner))
        bc_act = jax.nn.silu(causal_conv(bc_in, docs_ext, conv_shared))
        delta = jax.nn.softplus(dt_in + dt_bias[None, :])
        values, state_loc, keep = block_out(
            x_act.reshape(count, heads_here, HEAD_DIM),
            bc_act[:, :STATE],
            bc_act[:, STATE:],
            delta,
            docs,
            doc_before,
            state_in,
            decay_rate,
        )
        return (head_norm(values, norm_gain), state_loc, keep)

    blank = jnp.zeros((heads_here, HEAD_DIM, STATE), jnp.float32)
    unit = jnp.ones((heads_here,), jnp.float32)
    _, state_loc, keep = layer(x_ext, bc_ext, dt_raw, blank)
    state_in = prefix((keep, state_loc), "ctx", link, (unit, blank), False)[1]
    outputs, pull = jax.vjp(layer, x_ext, bc_ext, dt_raw, state_in)
    normed = outputs[0]
    grads_out = pull((grad_out.astype(jnp.float32), jnp.zeros_like(blank), jnp.zeros_like(unit)))
    adjoint = prefix((keep, grads_out[3]), "ctx", link, (unit, blank), True)[1]
    keep_grad = jnp.sum(adjoint * state_in, axis=(1, 2))
    grads_state = pull((jnp.zeros_like(normed), adjoint, keep_grad))
    grad_xe = grads_out[0] + grads_state[0]
    grad_bce = grads_out[1] + grads_state[1]
    grad_dt = grads_out[2] + grads_state[2]
    back_x, back_bc = from_behind((grad_xe[:3], grad_bce[:3]), "ctx", -1)
    grad_x = grad_xe[3:].at[count - 3 :].add(back_x)
    grad_bc = grad_bce[3:].at[count - 3 :].add(back_bc)
    grad_xb = grad_x.astype(jnp.bfloat16)
    grad_rows = lax.all_gather(grad_xb, "fsdp", axis=1, tiled=True)
    column = lax.axis_index("fsdp") * heads_here
    dt_wide = lax.dynamic_update_slice(
        jnp.zeros((count, dt_weight.shape[1]), jnp.float32), grad_dt, (jnp.int32(0), column)
    )
    bc_total, dt_total = lax.psum((grad_bc, dt_wide), "fsdp")
    grad_local = jnp.dot(grad_rows, x_weight.T, preferred_element_type=jnp.float32)
    grad_local = grad_local + jnp.dot(bc_total, bc_weight.T.astype(jnp.float32), precision=exact)
    grad_local = grad_local + jnp.dot(dt_total, dt_weight.T.astype(jnp.float32), precision=exact)
    grad_tokens = grad_local.astype(jnp.bfloat16)
    return (normed.astype(jnp.bfloat16), grad_tokens)


BF = jnp.bfloat16
F32 = jnp.float32
LOG2E = 1.4426950408889634
LANES = 128
NEG = -1e30


def params(mb=60, **kw):
    return pltpu.CompilerParams(vmem_limit_bytes=mb * 1024 * 1024, **kw)


def cost(flops, nbytes):
    return pl.CostEstimate(flops=int(flops), bytes_accessed=int(nbytes), transcendentals=0)


def mm(a, b):
    return jnp.dot(a, b, preferred_element_type=F32)


def mm_nt(a, b):
    return lax.dot_general(a, b, (((1,), (1,)), ((), ())), preferred_element_type=F32)


def mm_tn(a, b):
    return lax.dot_general(a, b, (((0,), (0,)), ((), ())), preferred_element_type=F32)


def split2(v):
    hi = v.astype(BF)
    return hi, (v - hi.astype(F32)).astype(BF)


def iota(shape, dim):
    return lax.broadcasted_iota(jnp.int32, shape, dim)


def doc_start_of(pos, docs_ref, count):
    start = jnp.zeros_like(pos)
    for i in range(count):
        start = jnp.where(docs_ref[i] <= pos, docs_ref[i], start)
    return start


def spread(heads, width):
    shape = (LANES, width)
    row, col = iota(shape, 0), iota(shape, 1)
    head = jnp.right_shift(col, 6)
    return jnp.where((row == head) | (row == head + 16), 1.0, 0.0).astype(BF)


def gather_heads(width):
    shape = (width, LANES)
    return jnp.where(jnp.right_shift(iota(shape, 0), 6) == iota(shape, 1), 1.0, 0.0).astype(BF)


def packed(v):
    hi = v.astype(BF).astype(F32)
    lo = v - hi
    lane = iota(v.shape, 1)
    return jnp.where(lane < 16, hi, pltpu.roll(lo, 16, 1)).astype(BF)


def over_heads(v, gather):
    hi, lo = split2(v)
    return mm(hi, gather) + mm(lo, gather)


def silu_parts(v):
    sig = 1.0 / (1.0 + jnp.exp(-v))
    return v * sig, sig * (1.0 + v * (1.0 - sig))


def fetch(src, dst, sem):
    copy = pltpu.make_async_copy(src, dst, sem)
    copy.start()
    return copy


def columns(w_ref, block, width):
    return w_ref.at[:, pl.ds(pl.multiple_of(block * width, LANES), width)]


def lead_kernel(
    meta_ref, tok_hbm, w_hbm, bcw_hbm, dtw_hbm, piece_ref, out_ref, low_ref, tok_ref, w_ref, bcw_ref,
    dtw_ref, sems,
):
    width = w_ref.shape[1]
    get_tok = fetch(tok_hbm, tok_ref, sems.at[0])
    get_w = fetch(columns(w_hbm, meta_ref[0], width), w_ref, sems.at[1])
    get_bcw = fetch(bcw_hbm, bcw_ref, sems.at[2])
    get_dtw = fetch(dtw_hbm, dtw_ref, sems.at[3])
    get_tok.wait()
    get_w.wait()
    piece_ref[...] = mm(tok_ref[...], w_ref[...]).astype(BF)
    get_bcw.wait()
    get_dtw.wait()
    states = bcw_ref.shape[1]
    heads = dtw_ref.shape[0]
    out_ref[:, :states], low_ref[...] = split2(mm(tok_ref[...], bcw_ref[...]))
    hi, lo = split2(mm_nt(tok_ref[...], dtw_ref[...]))
    shape = (heads, LANES)
    row, col = iota(shape, 0), iota(shape, 1)
    first = jnp.where(row == col, 1.0, 0.0).astype(BF)
    second = jnp.where(row + heads == col, 1.0, 0.0).astype(BF)
    out_ref[:, states:] = (mm(hi, first) + mm(lo, second)).astype(BF)


def lead_proj(block, tokens, x_weight, bc_weight, dt_rows, width):
    rows, depth = tokens.shape
    states = bc_weight.shape[1]
    hbm = pl.BlockSpec(memory_space=pl.ANY)
    vm = pl.BlockSpec(memory_space=pltpu.VMEM)
    return pl.pallas_call(
        lead_kernel,
        grid_spec=pltpu.PrefetchScalarGridSpec(
            num_scalar_prefetch=1,
            grid=(),
            in_specs=[hbm] * 4,
            out_specs=[vm] * 3,
            scratch_shapes=[
                pltpu.VMEM((rows, depth), BF),
                pltpu.VMEM((depth, width), BF),
                pltpu.VMEM((depth, states), BF),
                pltpu.VMEM(dt_rows.shape, BF),
                pltpu.SemaphoreType.DMA((4,)),
            ],
        ),
        out_shape=[
            jax.ShapeDtypeStruct((rows, width), BF),
            jax.ShapeDtypeStruct((rows, states + LANES), BF),
            jax.ShapeDtypeStruct((rows, states), BF),
        ],
        compiler_params=params(),
        cost_estimate=cost(2 * rows * depth * width, 3e6),
        name="lead_proj",
    )(block, tokens, x_weight, bc_weight, dt_rows)


def rest_kernel(
    meta_ref, tok_hbm, w_hbm, bcw_hbm, ra_hbm, rb_hbm, peer_ref, core_ref, mine_ref, own_ref, send_ref,
    tok_ref, w_ref, bcw_ref, ra_ref, rb_ref, sems,
):
    width = w_ref.shape[2]
    get_tok = fetch(tok_hbm, tok_ref, sems.at[0])
    get_w = [fetch(columns(w_hbm, meta_ref[i], width), w_ref.at[i], sems.at[1 + i]) for i in range(3)]
    get_bcw = fetch(bcw_hbm, bcw_ref, sems.at[4])
    get_ra = fetch(ra_hbm, ra_ref, sems.at[5])
    get_rb = fetch(rb_hbm, rb_ref, sems.at[6])
    get_tok.wait()
    for i, ref in enumerate((peer_ref, core_ref, mine_ref)):
        get_w[i].wait()
        ref[...] = mm(tok_ref[...], w_ref[i]).astype(BF)
    get_bcw.wait()
    get_ra.wait()
    get_rb.wait()
    rim = ra_ref[...] + rb_ref[...]
    shared = mm(rim, bcw_ref[...]).astype(BF)
    own_ref[:, :width] = mm(rim, w_ref[2]).astype(BF)
    own_ref[:, width:] = shared
    send_ref[:, :width] = mm(rim, w_ref[0]).astype(BF)
    send_ref[:, width:] = shared


def rest_proj(blocks, tokens, x_weight, bc_weight, ra, rb, width):
    rows, depth = tokens.shape
    states = bc_weight.shape[1]
    hbm = pl.BlockSpec(memory_space=pl.ANY)
    vm = pl.BlockSpec(memory_space=pltpu.VMEM)
    piece = jax.ShapeDtypeStruct((rows, width), BF)
    rim = jax.ShapeDtypeStruct((ra.shape[0], width + states), BF)
    return pl.pallas_call(
        rest_kernel,
        grid_spec=pltpu.PrefetchScalarGridSpec(
            num_scalar_prefetch=1,
            grid=(),
            in_specs=[hbm] * 5,
            out_specs=[vm] * 5,
            scratch_shapes=[
                pltpu.VMEM((rows, depth), BF),
                pltpu.VMEM((3, depth, width), BF),
                pltpu.VMEM((depth, states), BF),
                pltpu.VMEM(ra.shape, BF),
                pltpu.VMEM(rb.shape, BF),
                pltpu.SemaphoreType.DMA((7,)),
            ],
        ),
        out_shape=[piece, piece, piece, rim, rim],
        compiler_params=params(),
        cost_estimate=cost(6 * rows * depth * width, 6e6),
        name="rest_proj",
    )(blocks, tokens, x_weight, bc_weight, ra, rb)


def conv_masks(docs_ref, count, base, rows, lanes):
    pos = base + iota((rows, lanes), 0)
    start = doc_start_of(pos, docs_ref, count)
    return [jnp.where(pos - k >= start, 1.0, 0.0) for k in range(1, 4)]


def shared_kernel(
    docs, heads, all_heads, meta_ref, docs_ref, own_ref, xr_ref, cr_ref, dr_ref, rim_own_ref,
    rim_recv_ref, taps_ref, prm_ref, bact_ref, bpre_ref, delta_ref, ramp_ref, sig_ref, rampt_ref,
    dpk_ref, wpk_ref, epk_ref, keep_ref, ext_ref,
):
    k, x, chip = meta_ref[0], meta_ref[1], meta_ref[2]
    rows = own_ref.shape[0]
    total = 2 * rows
    states2 = bact_ref.shape[1]
    base = chip * total
    mine = pl.multiple_of(8 + k * rows, 8)
    other = pl.multiple_of(8 + (1 - k) * rows, 8)
    width = rim_own_ref.shape[1] - states2
    rim = rim_own_ref[:, width:].astype(F32) + rim_recv_ref[:, width:].astype(F32)
    ext_ref[0:8, :] = rim[8:16, :]
    ext_ref[pl.ds(mine, rows), :] = own_ref[:, :states2].astype(F32) + xr_ref[:, :states2].astype(F32)
    ext_ref[pl.ds(other, rows), :] = cr_ref[:, :states2].astype(F32) + dr_ref[:, :states2].astype(F32)

    tile = 64

    def conv(step, _):
        at = pl.multiple_of(step * tile, tile)
        masks = conv_masks(docs_ref, docs, base + at, tile, LANES)
        for lane in range(0, states2, LANES):
            sl = slice(lane, lane + LANES)
            window = ext_ref[pl.ds(at, tile + 8), sl]
            value = window[8:] * taps_ref[0:1, sl]
            for j in range(1, 4):
                value = value + window[8 - j : 8 - j + tile] * taps_ref[j : j + 1, sl] * masks[j - 1]
            bpre_ref[pl.ds(at, tile), sl] = value
            bact_ref[pl.ds(at, tile), sl] = (value / (1.0 + jnp.exp(-value))).astype(BF)
        return 0

    lax.fori_loop(0, total // tile, conv, 0)

    shape = (LANES, LANES)
    row, col = iota(shape, 0), iota(shape, 1)
    first = x * (all_heads // 2) + k * heads
    wanted = (col < heads) & ((row == first + col) | (row == all_heads + first + col))
    select = jnp.where(wanted, 1.0, 0.0).astype(BF)
    square = (rows, rows)
    lower = jnp.where(iota(square, 0) >= iota(square, 1), 1.0, 0.0).astype(BF)
    bias, rate = prm_ref[0:1, :], prm_ref[1:2, :]

    def steps(part, ref_a, ref_b):
        at = pl.multiple_of(part * rows, rows)
        raw = mm(ref_a[:, states2:], select) + mm(ref_b[:, states2:], select) + bias
        delta = jnp.maximum(raw, 0.0) + jnp.log1p(jnp.exp(-jnp.abs(raw)))
        delta_ref[pl.ds(at, rows), :] = delta
        sig_ref[pl.ds(at, rows), :] = 1.0 / (1.0 + jnp.exp(-raw))
        dpk_ref[pl.ds(at, rows), :] = packed(delta)
        hi, rest = split2(delta)
        mid = rest
        low = (delta - hi.astype(F32) - mid.astype(F32)).astype(BF)
        ramp = -(mm(lower, hi) + mm(lower, mid) + mm(lower, low)) * (rate * LOG2E)
        ramp_ref[pl.ds(at, rows), :] = ramp
        rampt_ref[part] = jnp.transpose(ramp)[:16, :]
        begin = base + at
        end = begin + rows - 1
        pos = begin + iota((rows, LANES), 0)
        start = doc_start_of(pos, docs_ref, docs)
        last = doc_start_of(jnp.zeros((1, LANES), jnp.int32) + end, docs_ref, docs)
        final = ramp[rows - 1 : rows, :]
        epk_ref[pl.ds(at, rows), :] = packed(jnp.where(start < begin, jnp.exp2(ramp), 0.0))
        wpk_ref[pl.ds(at, rows), :] = packed(jnp.where(pos >= last, jnp.exp2(final - ramp), 0.0))
        keep_ref[part] = jnp.zeros((8, LANES), F32) + jnp.where(last < begin, jnp.exp2(final), 0.0)

    steps(k, own_ref, xr_ref)
    steps(1 - k, cr_ref, dr_ref)


def shared_maps(meta, doc_starts, own, xr, cr, dr, rim_own, rim_recv, taps, prm, heads, all_heads):
    rows = own.shape[0]
    total, states2 = 2 * rows, own.shape[1] - LANES
    compact = jax.ShapeDtypeStruct((total, LANES), F32)
    compact_b = jax.ShapeDtypeStruct((total, LANES), BF)
    vm = pl.BlockSpec(memory_space=pltpu.VMEM)
    return pl.pallas_call(
        functools.partial(shared_kernel, doc_starts.shape[0], heads, all_heads),
        grid_spec=pltpu.PrefetchScalarGridSpec(
            num_scalar_prefetch=2,
            grid=(),
            in_specs=[vm] * 8,
            out_specs=[vm] * 10,
            scratch_shapes=[pltpu.VMEM((total + 8, states2), F32)],
        ),
        out_shape=[
            jax.ShapeDtypeStruct((total, states2), BF),
            jax.ShapeDtypeStruct((total, states2), F32),
            compact,
            compact,
            compact,
            jax.ShapeDtypeStruct((2, 16, rows), F32),
            compact_b,
            compact_b,
            compact_b,
            jax.ShapeDtypeStruct((2, 8, LANES), F32),
        ],
        compiler_params=params(),
        cost_estimate=cost(4e9, 4e6),
        name="shared_maps",
    )(meta, doc_starts, own, xr, cr, dr, rim_own, rim_recv, taps, prm)


def keep_row(keep, heads, width):
    hi, rest = split2(keep)
    low = (keep - hi.astype(F32) - rest.astype(F32)).astype(BF)
    wide = spread(heads, width)
    lane = iota(keep.shape, 1)
    clean = lambda v: jnp.where(lane < 16, v.astype(F32), 0.0).astype(BF)
    return mm(clean(hi), wide) + mm(clean(rest), wide) + mm(clean(low), wide)


def inner_kernel(
    docs, heads, meta_ref, docs_ref, own_ref, xr_ref, cr_ref, dr_ref, rim_own_ref, rim_recv_ref,
    taps_ref, bact_ref, dpk_ref, wpk_ref, keep_ref, pre_ref, xd_ref, loc_ref, send_ref, ext_ref,
    wx_ref,
):
    k, chip = meta_ref[0], meta_ref[2]
    rows, width = own_ref.shape
    total = 2 * rows
    states = bact_ref.shape[1] // 2
    base = chip * total
    mine = pl.multiple_of(8 + k * rows, 8)
    other = pl.multiple_of(8 + (1 - k) * rows, 8)
    rim = (rim_own_ref[:, :width].astype(F32) + rim_recv_ref[:, :width].astype(F32))
    ext_ref[0:8, :] = rim.astype(BF).astype(F32)[8:16, :]

    def total_of(a, b):
        return (a[...].astype(F32) + b[...].astype(F32)).astype(BF).astype(F32)

    ext_ref[pl.ds(mine, rows), :] = total_of(own_ref, xr_ref)
    ext_ref[pl.ds(other, rows), :] = total_of(cr_ref, dr_ref)
    wide = spread(heads, width)
    tile = 64

    def conv(step, _):
        at = pl.multiple_of(step * tile, tile)
        masks = conv_masks(docs_ref, docs, base + at, tile, LANES)
        dpk = dpk_ref[pl.ds(at, tile), :]
        wpk = wpk_ref[pl.ds(at, tile), :]
        for lane in range(0, width, LANES):
            sl = slice(lane, lane + LANES)
            window = ext_ref[pl.ds(at, tile + 8), sl]
            value = window[8:] * taps_ref[0:1, sl]
            for j in range(1, 4):
                value = value + window[8 - j : 8 - j + tile] * taps_ref[j : j + 1, sl] * masks[j - 1]
            pre_ref[pl.ds(at, tile), sl] = value
            act = value / (1.0 + jnp.exp(-value))
            xd = act * mm(dpk, wide[:, sl])
            xd_ref[pl.ds(at, tile), sl] = xd.astype(BF)
            wx_ref[pl.ds(at, tile), sl] = (xd * mm(wpk, wide[:, sl])).astype(BF)
        return 0

    lax.fori_loop(0, total // tile, conv, 0)
    locs = []
    for part in range(2):
        sl = slice(part * rows, (part + 1) * rows)
        loc = mm_tn(bact_ref[sl, :states], wx_ref[sl, :])
        loc_ref[part] = loc
        locs.append(loc)
    second = keep_row(keep_ref[1], heads, width)[0:1, :]
    state = locs[0] * second + locs[1]
    chips, piece = send_ref.shape[0], send_ref.shape[1]
    for i in range(chips):
        send_ref[i, :, :width] = state[i * piece : (i + 1) * piece, :].astype(BF)
    keep = jnp.where(iota((8, LANES), 1) < 16, keep_ref[0] * keep_ref[1], 0.0)
    hi, mid = split2(keep)
    low = (keep - hi.astype(F32) - mid.astype(F32)).astype(BF)
    row = iota((8, LANES), 0)
    stack = jnp.where(row == 0, hi.astype(F32), jnp.where(row == 1, mid.astype(F32), low.astype(F32)))
    stack = jnp.concatenate([stack, jnp.zeros((piece - 8, LANES), F32)], axis=0).astype(BF)
    for i in range(chips):
        send_ref[i, :, width:] = stack


def inner_maps(
    meta, doc_starts, own, xr, cr, dr, rim_own, rim_recv, taps, bact, dpk, wpk, keep, heads, chips
):
    rows, width = own.shape
    total, states = 2 * rows, bact.shape[1] // 2
    vm = pl.BlockSpec(memory_space=pltpu.VMEM)
    whole = lambda shape: pl.BlockSpec(shape, lambda i, m, d: (0,) * len(shape))
    half = pl.BlockSpec((taps.shape[0], width), lambda i, m, d: (0, m[0]))
    outs = [
        jax.ShapeDtypeStruct((total, width), F32),
        jax.ShapeDtypeStruct((total, width), BF),
        jax.ShapeDtypeStruct((2, states, width), F32),
        jax.ShapeDtypeStruct((chips, states // chips, width + LANES), BF),
    ]
    return pl.pallas_call(
        functools.partial(inner_kernel, doc_starts.shape[0], heads),
        grid_spec=pltpu.PrefetchScalarGridSpec(
            num_scalar_prefetch=2,
            grid=(1,),
            in_specs=[
                whole(own.shape), whole(xr.shape), whole(cr.shape), whole(dr.shape),
                whole(rim_own.shape), whole(rim_recv.shape), half, whole(bact.shape),
                whole(dpk.shape), whole(wpk.shape), whole(keep.shape),
            ],
            out_specs=[whole(o.shape) for o in outs],
            scratch_shapes=[pltpu.VMEM((total + 8, width), F32), pltpu.VMEM((total, width), BF)],
        ),
        out_shape=outs,
        compiler_params=params(),
        cost_estimate=cost(4e9, 4e6),
        name="inner_maps",
    )(meta, doc_starts, own, xr, cr, dr, rim_own, rim_recv, taps, bact, dpk, wpk, keep)


def within_kernel(
    docs, heads, meta_ref, docs_ref, xd_ref, ramp_ref, rampt_ref, own_ref, xr_ref, cr_ref, dr_ref,
    own_low_ref, xr_low_ref, cr_low_ref, dr_low_ref, rim_own_ref, rim_recv_ref, taps_ref, y_ref,
    cbt_ref, cb_ref, gate_ref, ext_ref, high_ref, low_ref,
):
    k, chip = meta_ref[0], meta_ref[2]
    total, width = xd_ref.shape
    rows = total // 2
    states2 = own_low_ref.shape[1]
    states = states2 // 2
    mine = pl.multiple_of(8 + k * rows, 8)
    other = pl.multiple_of(8 + (1 - k) * rows, 8)
    rim = rim_own_ref[:, width:].astype(F32) + rim_recv_ref[:, width:].astype(F32)
    ext_ref[0:8, :] = rim[8:16, :]

    def exact_sum(a, a_low, b, b_low):
        high = a[:, :states2].astype(F32) + b[:, :states2].astype(F32)
        return high + (a_low[...].astype(F32) + b_low[...].astype(F32))

    ext_ref[pl.ds(mine, rows), :] = exact_sum(own_ref, own_low_ref, xr_ref, xr_low_ref)
    ext_ref[pl.ds(other, rows), :] = exact_sum(cr_ref, cr_low_ref, dr_ref, dr_low_ref)
    tile = 64

    def conv(step, _):
        at = pl.multiple_of(step * tile, tile)
        masks = conv_masks(docs_ref, docs, chip * total + at, tile, LANES)
        for lane in range(0, states2, LANES):
            sl = slice(lane, lane + LANES)
            window = ext_ref[pl.ds(at, tile + 8), sl]
            value = window[8:] * taps_ref[0:1, sl]
            for j in range(1, 4):
                value = value + window[8 - j : 8 - j + tile] * taps_ref[j : j + 1, sl] * masks[j - 1]
            high, low = split2(value / (1.0 + jnp.exp(-value)))
            high_ref[pl.ds(at, tile), sl] = high
            low_ref[pl.ds(at, tile), sl] = low
        return 0

    lax.fori_loop(0, total // tile, conv, 0)
    square = (rows, rows)
    lane = iota((rows, LANES), 1)
    for part in range(2):
        sl = slice(part * rows, (part + 1) * rows)
        begin = chip * total + part * rows
        b, c = high_ref[sl, :states], high_ref[sl, states:]
        b_low, c_low = low_ref[sl, :states], low_ref[sl, states:]
        cb_ref[...] = mm_nt(c, b) + (mm_nt(c, b_low) + mm_nt(c_low, b))
        cbt_ref[part] = jnp.transpose(cb_ref[...])
        pos, src = begin + iota(square, 0), begin + iota(square, 1)
        start = doc_start_of(pos, docs_ref, docs)
        gate_ref[...] = jnp.where((src <= pos) & (src >= start), 0.0, NEG)
        for pair in range(heads // 2):
            cols = slice(pair * LANES, (pair + 1) * LANES)
            xd = xd_ref[sl, cols]
            found = []
            for head in (2 * pair, 2 * pair + 1):
                gap = ramp_ref[sl, head : head + 1] - rampt_ref[part, head : head + 1, :]
                high, low = split2(jnp.exp2(gap + gate_ref[...]) * cb_ref[...])
                found.append(mm(high, xd) + mm(low, xd))
            y_ref[sl, cols] = jnp.where(lane < HEAD_DIM, found[0], found[1])


def within(meta, doc_starts, xd, ramp, rampt, smalls, lows, rim_own, rim_recv, taps, heads):
    total, width = xd.shape
    rows, states2 = total // 2, lows[0].shape[1]
    vm = pl.BlockSpec(memory_space=pltpu.VMEM)
    return pl.pallas_call(
        functools.partial(within_kernel, doc_starts.shape[0], heads),
        grid_spec=pltpu.PrefetchScalarGridSpec(
            num_scalar_prefetch=2,
            grid=(),
            in_specs=[vm] * 14,
            out_specs=[vm] * 2,
            scratch_shapes=[
                pltpu.VMEM((rows, rows), F32),
                pltpu.VMEM((rows, rows), F32),
                pltpu.VMEM((total + 8, states2), F32),
                pltpu.VMEM((total, states2), BF),
                pltpu.VMEM((total, states2), BF),
            ],
        ),
        out_shape=[
            jax.ShapeDtypeStruct((total, width), F32),
            jax.ShapeDtypeStruct((2, rows, rows), F32),
        ],
        compiler_params=params(),
        cost_estimate=cost(6e9, 4e6),
        name="within",
    )(meta, doc_starts, xd, ramp, rampt, *smalls, *lows, rim_own, rim_recv, taps)


def chain_kernel(heads, reverse, recv_ref, keep_ref, out_ref):
    chips = recv_ref.shape[0]
    width = out_ref.shape[2]
    state = jnp.zeros(out_ref.shape[1:], F32)
    wide = spread(heads, width)
    for step in range(chips):
        i = chips - 1 - step if reverse else step
        out_ref[i] = state.astype(BF)
        if step < chips - 1:
            factor = mm(keep_ref[i, :, width:], wide)
            factor = factor[0:1] + factor[1:2] + factor[2:3]
            state = state * factor + recv_ref[i, :, :width].astype(F32)


def chain(recv, keeps, heads, width, reverse):
    chips, piece = recv.shape[0], recv.shape[1]
    return pl.pallas_call(
        functools.partial(chain_kernel, heads, reverse),
        out_shape=jax.ShapeDtypeStruct((chips, piece, width), BF),
        compiler_params=params(16),
        cost_estimate=cost(1e8, 1e6),
        name="chain",
    )(recv, keeps)


def out_kernel(
    heads, meta_ref, y_ref, state_ref, loc_ref, bact_ref, epk_ref, keep_ref, go_ref, go_recv_ref,
    gain_ref, mix_own_ref, mix_send_ref, dy_ref, edy_ref, dot_ref, both_ref, late_ref, send_ref,
    go_all_ref, mix_ref,
):
    k = meta_ref[0]
    total, width = y_ref.shape
    rows = total // 2
    states = bact_ref.shape[1] // 2
    mine = pl.multiple_of(k * rows, rows)
    other = pl.multiple_of((1 - k) * rows, rows)
    go_all_ref[pl.ds(mine, rows), :] = go_ref[...]
    go_all_ref[pl.ds(other, rows), :] = go_recv_ref[...]
    state = state_ref[...]
    keep0 = keep_row(keep_ref[0], heads, width)[0:1, :]
    both_ref[0] = state
    middle = state.astype(F32) * keep0 + loc_ref[0]
    both_ref[1] = middle.astype(BF)
    both_ref[2] = (middle * keep_row(keep_ref[1], heads, width)[0:1, :] + loc_ref[1]).astype(BF)
    wide = spread(heads, width)
    gather = gather_heads(width)
    tile = 256
    per = rows // tile

    def one(step, _):
        at = pl.multiple_of(step * tile, tile)
        sl = pl.ds(at, tile)
        enter = mm(epk_ref[sl, :], wide)
        carried = mm(bact_ref[sl, states:], both_ref[step // per])
        y = y_ref[sl, :] + carried * enter
        u = go_all_ref[sl, :].astype(F32) * gain_ref[...]
        mean = over_heads(y * y, gather) * (1.0 / HEAD_DIM)
        along = over_heads(u * y, gather)
        scale = lax.rsqrt(mean + epsilon)
        cube = scale * scale * scale
        wide_scale = mm(packed(scale), wide)
        wide_back = mm(packed(cube * along * (1.0 / HEAD_DIM)), wide)
        mix_ref[sl, :] = (y * wide_scale * gain_ref[...]).astype(BF)
        dy = u * wide_scale - y * wide_back
        hi, lo = split2(dy)
        for pair in range(width // LANES):
            cols = slice(pair * LANES, (pair + 1) * LANES)
            dy_ref[sl, 2 * pair * LANES : (2 * pair + 1) * LANES] = hi[:, cols]
            dy_ref[sl, (2 * pair + 1) * LANES : (2 * pair + 2) * LANES] = lo[:, cols]
        edy_ref[sl, :] = (dy * enter).astype(BF)
        dot_ref[sl, :] = epsilon * cube * along
        return 0

    lax.fori_loop(0, total // tile, one, 0)
    mix_own_ref[...] = mix_ref[pl.ds(mine, rows), :]
    mix_send_ref[...] = mix_ref[pl.ds(other, rows), :]
    late = mm_tn(bact_ref[rows:, states:], edy_ref[rows:, :])
    late_ref[...] = late
    back = late * keep0 + mm_tn(bact_ref[:rows, states:], edy_ref[:rows, :])
    chips, piece = send_ref.shape[0], send_ref.shape[1]
    for i in range(chips):
        send_ref[i] = back[i * piece : (i + 1) * piece, :].astype(BF)


def outputs_of(meta, y, state, loc, bact, epk, keep, grad_out, go_recv, gain, heads, chips):
    total, width = y.shape
    rows, states = total // 2, bact.shape[1] // 2
    whole = lambda shape: pl.BlockSpec(shape, lambda i, m: (0,) * len(shape))
    half = lambda count: pl.BlockSpec((count, width), lambda i, m: (0, m[0]))
    outs = [
        jax.ShapeDtypeStruct((rows, width), BF),
        jax.ShapeDtypeStruct((rows, width), BF),
        jax.ShapeDtypeStruct((total, 2 * width), BF),
        jax.ShapeDtypeStruct((total, width), BF),
        jax.ShapeDtypeStruct((total, LANES), F32),
        jax.ShapeDtypeStruct((3, states, width), BF),
        jax.ShapeDtypeStruct((states, width), F32),
        jax.ShapeDtypeStruct((chips, states // chips, width), BF),
    ]
    return pl.pallas_call(
        functools.partial(out_kernel, heads),
        grid_spec=pltpu.PrefetchScalarGridSpec(
            num_scalar_prefetch=1,
            grid=(1,),
            in_specs=[
                whole(y.shape), whole(state.shape), whole(loc.shape), whole(bact.shape),
                whole(epk.shape), whole(keep.shape), half(rows), whole(go_recv.shape), half(1),
            ],
            out_specs=[whole(o.shape) for o in outs],
            scratch_shapes=[pltpu.VMEM((total, width), BF), pltpu.VMEM((total, width), BF)],
        ),
        out_shape=outs,
        compiler_params=params(),
        cost_estimate=cost(4e9, 4e6),
        name="outputs_of",
    )(meta, y, state, loc, bact, epk, keep, grad_out, go_recv, gain)


def within_back_kernel(
    docs, heads, meta_ref, docs_ref, dy_ref, edy_ref, both_ref, xd_ref, bact_ref, ramp_ref,
    rampt_ref, cbt_ref, act_ref, slope_ref, near_ref, q_ref, dbc_ref, gate_ref, sum_ref,
):
    gather = gather_heads(xd_ref.shape[1])
    chip = meta_ref[2]
    total, width = xd_ref.shape
    rows = total // 2
    states = bact_ref.shape[1] // 2
    square = (rows, rows)
    lane = iota((rows, LANES), 1)
    for part in range(2):
        sl = slice(part * rows, (part + 1) * rows)
        begin = chip * total + part * rows
        b, c = bact_ref[sl, :states], bact_ref[sl, states:]
        src, pos = begin + iota(square, 0), begin + iota(square, 1)
        start = doc_start_of(pos, docs_ref, docs)
        gate_ref[...] = jnp.where((src <= pos) & (src >= start), 0.0, NEG)
        sum_ref[...] = jnp.zeros(square, F32)
        q = jnp.zeros((rows, LANES), F32)
        for pair in range(heads // 2):
            cols = slice(pair * LANES, (pair + 1) * LANES)
            xd = xd_ref[sl, cols]
            dy_both = dy_ref[sl, 2 * pair * LANES : (2 * pair + 2) * LANES]
            dy = dy_both[:, :LANES]
            found = []
            for side, head in enumerate((2 * pair, 2 * pair + 1)):
                keep_side = (lane < HEAD_DIM) if side == 0 else (lane >= HEAD_DIM)
                only = jnp.where(keep_side, xd.astype(F32), 0.0).astype(BF)
                only = jnp.concatenate([only, only], axis=1)
                gap = rampt_ref[part, head : head + 1, :] - ramp_ref[sl, head : head + 1]
                decay = jnp.exp2(gap + gate_ref[...])
                found.append(mm((decay * cbt_ref[part]).astype(BF), dy))
                sum_ref[...] += mm_nt(only, dy_both) * decay
            dxd = jnp.where(lane < HEAD_DIM, found[0], found[1])
            near_ref[sl, cols] = (dxd * slope_ref[sl, cols].astype(F32)).astype(BF)
            q = q + mm((dxd * act_ref[sl, cols].astype(F32)).astype(BF), gather[cols, :])
        q_ref[sl, :] = q
        grad, low = split2(sum_ref[...])
        dbc_ref[sl, :states] = mm(grad, c) + mm(low, c)
        dbc_ref[sl, states:] = mm_tn(grad, b) + mm_tn(low, b) + mm_nt(edy_ref[sl, :], both_ref[part])


def within_back(meta, doc_starts, dy, edy, both, xd, bact, ramp, rampt, cbt, act, slope, heads):
    total, width = xd.shape
    rows = total // 2
    vm = pl.BlockSpec(memory_space=pltpu.VMEM)
    return pl.pallas_call(
        functools.partial(within_back_kernel, doc_starts.shape[0], heads),
        grid_spec=pltpu.PrefetchScalarGridSpec(
            num_scalar_prefetch=2,
            grid=(),
            in_specs=[vm] * 10,
            out_specs=[vm] * 3,
            scratch_shapes=[pltpu.VMEM((rows, rows), F32)] * 2,
        ),
        out_shape=[
            jax.ShapeDtypeStruct((total, width), BF),
            jax.ShapeDtypeStruct((total, LANES), F32),
            jax.ShapeDtypeStruct((total, bact.shape[1]), F32),
        ],
        compiler_params=params(),
        cost_estimate=cost(1e10, 6e6),
        name="within_back",
    )(meta, doc_starts, dy, edy, both, xd, bact, ramp, rampt, cbt, act, slope)


def slopes_kernel(pre_ref, dpk_ref, wpk_ref, act_ref, far_ref, wx_ref, slope_ref, reach_ref):
    total, width = pre_ref.shape
    wide = spread(width // HEAD_DIM, width)
    tile = total // 2
    for at in range(0, total, tile):
        sl = slice(at, at + tile)
        for lane in range(0, width, LANES):
            ls = slice(lane, lane + LANES)
            w = mm(wpk_ref[sl, :], wide[:, ls])
            step = mm(dpk_ref[sl, :], wide[:, ls])
            act, slope = silu_parts(pre_ref[sl, ls])
            slope = slope * step
            act_ref[sl, ls] = act.astype(BF)
            far_ref[sl, ls] = (act * w).astype(BF)
            wx_ref[sl, ls] = (act * step * w).astype(BF)
            slope_ref[sl, ls] = slope.astype(BF)
            reach_ref[sl, ls] = (slope * w).astype(BF)


def slopes_of(pre, dpk, wpk):
    return pl.pallas_call(
        slopes_kernel,
        out_shape=[jax.ShapeDtypeStruct(pre.shape, BF)] * 5,
        compiler_params=params(),
        cost_estimate=cost(2e9, 4e6),
        name="slopes_of",
    )(pre, dpk, wpk)


def back_masks(docs_ref, docs, pos):
    return [jnp.where(pos >= doc_start_of(pos + j, docs_ref, docs), 1.0, 0.0) for j in range(1, 4)]


def conv_back(src_ref, taps, at, count, ls, masks):
    window = src_ref[pl.ds(at, count + 8), ls]
    value = window[:count] * taps[0:1, ls]
    for j in range(1, 4):
        value = value + window[j : j + count] * taps[j : j + 1, ls] * masks[j - 1]
    return value


def grads_kernel(
    docs, heads, meta_ref, docs_ref, adj_ref, late_ref, keep_ref, both_ref, b_ref, near_ref, far_ref,
    wx_ref, reach_ref, q_ref, dbc_ref, bpre_ref, delta_ref, sig_ref, dot_ref, prm_ref, taps_bc_ref,
    taps_ref, own_ref, other_ref, bc_own_ref, bc_other_ref, rim_ref, adj2_ref, gx_ref, gb_ref, all_ref,
    bc_all_ref,
):
    k, chip = meta_ref[0], meta_ref[2]
    total, width = near_ref.shape
    rows = total // 2
    states = b_ref.shape[1]
    states2 = 2 * states
    base = chip * total
    adj = adj_ref[...].astype(F32)
    early = adj * keep_row(keep_ref[1], heads, width)[0:1, :] + late_ref[...]
    adj2_ref[0] = early.astype(BF)
    adj2_ref[1] = adj_ref[...]
    gather = gather_heads(width)
    ends = [
        over_heads(
            jnp.sum(a * both_ref[i].astype(F32), axis=0, keepdims=True) + jnp.zeros((8, width), F32),
            gather,
        )
        for i, a in ((1, early), (2, adj))
    ]
    for ref, lanes in ((gx_ref, width), (gb_ref, states2)):
        ref[0:8, :] = jnp.zeros((8, lanes), F32)
        ref[total + 8 :, :] = jnp.zeros((8, lanes), F32)
    square = (rows, rows)
    upper = jnp.where(iota(square, 0) <= iota(square, 1), 1.0, 0.0).astype(BF)
    rate = prm_ref[1:2, :]
    row = iota((rows, LANES), 0)
    for part in range(2):
        sl = slice(part * rows, (part + 1) * rows)
        inside = slice(8 + part * rows, 8 + (part + 1) * rows)
        q = q_ref[sl, :]
        for lane in range(0, width, LANES):
            ls = slice(lane, lane + LANES)
            back = mm(b_ref[sl, :], adj2_ref[part, :, ls])
            gx_ref[inside, ls] = near_ref[sl, ls].astype(F32) + back * reach_ref[sl, ls].astype(F32)
            q = q + mm((back * far_ref[sl, ls].astype(F32)).astype(BF), gather[ls, :])
        ramp_grad = dot_ref[sl, :] - delta_ref[sl, :] * q
        ramp_grad = ramp_grad + jnp.where(row == rows - 1, ends[part][0:1, :], 0.0)
        hi, lo = split2(ramp_grad)
        later = mm(upper, hi) + mm(upper, lo)
        bc_all_ref[sl, states2:] = (q - rate * later) * sig_ref[sl, :]
        back = mm_nt(wx_ref[sl, :], adj2_ref[part])
        for lane, grad in ((0, dbc_ref[sl, :states] + back), (states, dbc_ref[sl, states:])):
            ls = slice(lane, lane + states)
            _, slope = silu_parts(bpre_ref[sl, ls])
            gb_ref[inside, ls] = grad * slope
    tile = 64

    def back(step, _):
        at = pl.multiple_of(step * tile, tile)
        begin = pl.multiple_of(at + 8, 8)
        masks = back_masks(docs_ref, docs, base + at + iota((tile, LANES), 0))
        for lane in range(0, width, LANES):
            ls = slice(lane, lane + LANES)
            all_ref[pl.ds(at, tile), ls] = conv_back(gx_ref, taps_ref, begin, tile, ls, masks).astype(BF)
        for lane in range(0, states2, LANES):
            ls = slice(lane, lane + LANES)
            bc_all_ref[pl.ds(at, tile), ls] = conv_back(gb_ref, taps_bc_ref, begin, tile, ls, masks)
        return 0

    lax.fori_loop(0, total // tile, back, 0)
    pad = jnp.zeros((8, LANES), F32)
    masks = back_masks(docs_ref, docs, base - 8 + iota((8, LANES), 0))
    for src, taps, first, lanes in ((gx_ref, taps_ref, 0, width), (gb_ref, taps_bc_ref, width, states2)):
        for lane in range(0, lanes, LANES):
            value = conv_back(src, taps, 0, 8, slice(lane, lane + LANES), masks)
            value = jnp.concatenate([pad, value], axis=0)
            rim_ref[:, first + lane : first + lane + LANES] = value.astype(BF)
    mine = pl.ds(pl.multiple_of(k * rows, rows), rows)
    other = pl.ds(pl.multiple_of((1 - k) * rows, rows), rows)
    own_ref[...] = all_ref[mine, :]
    other_ref[...] = all_ref[other, :]
    bc_own_ref[...] = bc_all_ref[mine, :]
    bc_other_ref[...] = bc_all_ref[other, :]


def grads_of(
    meta, doc_starts, adj, late, keep, both, bact, near, far, wx, reach, q, dbc, bpre, delta, sig, dots,
    prm, taps_bc, taps, heads,
):
    total, width = near.shape
    rows, states2 = total // 2, bact.shape[1]
    states = states2 // 2
    whole = lambda shape: pl.BlockSpec(shape, lambda i, m, d: (0,) * len(shape))
    half = pl.BlockSpec((taps.shape[0], width), lambda i, m, d: (0, m[0]))
    first = pl.BlockSpec((total, states), lambda i, m, d: (0, 0))
    ins = [near, far, wx, reach, q, dbc, bpre, delta, sig, dots, prm, taps_bc]
    outs = [
        jax.ShapeDtypeStruct((rows, width), BF),
        jax.ShapeDtypeStruct((rows, width), BF),
        jax.ShapeDtypeStruct((rows, states2 + LANES), F32),
        jax.ShapeDtypeStruct((rows, states2 + LANES), F32),
        jax.ShapeDtypeStruct((16, width + states2), BF),
    ]
    return pl.pallas_call(
        functools.partial(grads_kernel, doc_starts.shape[0], heads),
        grid_spec=pltpu.PrefetchScalarGridSpec(
            num_scalar_prefetch=2,
            grid=(1,),
            in_specs=[whole(a.shape) for a in (adj, late, keep, both)]
            + [first]
            + [whole(a.shape) for a in ins]
            + [half],
            out_specs=[whole(o.shape) for o in outs],
            scratch_shapes=[
                pltpu.VMEM((2, states, width), BF),
                pltpu.VMEM((total + 16, width), F32),
                pltpu.VMEM((total + 16, states2), F32),
                pltpu.VMEM((total, width), BF),
                pltpu.VMEM((total, states2 + LANES), F32),
            ],
        ),
        out_shape=outs,
        compiler_params=params(),
        cost_estimate=cost(4e9, 8e6),
        name="grads_of",
    )(meta, doc_starts, adj, late, keep, both, bact, *ins, taps)


def join_kernel(heads, meta_ref, own_ref, recv_ref, out_ref, send_ref):
    k = meta_ref[0]
    states2 = own_ref.shape[1] - LANES
    total = own_ref[:, :states2] + recv_ref[:, :states2]
    out_ref[:, :states2] = total
    send_ref[:, :states2] = total.astype(BF)
    shape = (LANES, LANES)
    row, col = iota(shape, 0), iota(shape, 1)
    mine = jnp.where((row < heads) & (col == row + k * heads), 1.0, 0.0).astype(BF)
    other = jnp.where((row < heads) & (col == row + (1 - k) * heads), 1.0, 0.0).astype(BF)
    steps = mm(own_ref[:, states2:].astype(BF), mine) + mm(recv_ref[:, states2:].astype(BF), other)
    out_ref[:, states2:] = steps
    send_ref[:, states2:] = steps.astype(BF)


def join(meta, own, recv, heads):
    vm = pl.BlockSpec(memory_space=pltpu.VMEM)
    return pl.pallas_call(
        functools.partial(join_kernel, heads),
        grid_spec=pltpu.PrefetchScalarGridSpec(
            num_scalar_prefetch=1, grid=(), in_specs=[vm] * 2, out_specs=[vm] * 2
        ),
        out_shape=[jax.ShapeDtypeStruct(own.shape, F32), jax.ShapeDtypeStruct(own.shape, BF)],
        compiler_params=params(16),
        cost_estimate=cost(1e8, 1e6),
        name="join",
    )(meta, own, recv)


def half_kernel(meta_ref, *refs):
    *before, mine_ref, other_ref, rim_ref, w_mine_ref, w_other_ref, out_ref = refs
    rows, width = mine_ref.shape

    def whole(ref, rim):
        tail = ref[rows - 16 :, :].astype(F32) + rim.astype(F32)
        return jnp.concatenate([ref[: rows - 16, :], tail.astype(BF)], axis=0)

    mine = whole(mine_ref, rim_ref[:16, :width])
    other = whole(other_ref, rim_ref[16:, :width])
    total = mm_nt(mine, w_mine_ref[...]) + mm_nt(other, w_other_ref[...])
    for ref in before:
        total = total + ref[...]
    out_ref[...] = total


def first_half(blocks, before, mine, other, rim, x_weight, tile):
    rows, width = mine.shape
    depth = x_weight.shape[0]
    whole = lambda shape: pl.BlockSpec(shape, lambda i, m: (0, 0))
    part = pl.BlockSpec((rows, tile), lambda i, m: (0, i))
    parts = [] if before is None else [before]
    return pl.pallas_call(
        half_kernel,
        grid_spec=pltpu.PrefetchScalarGridSpec(
            num_scalar_prefetch=1,
            grid=(depth // tile,),
            in_specs=[part] * len(parts)
            + [
                whole(mine.shape), whole(other.shape), whole(rim.shape),
                pl.BlockSpec((tile, width), lambda i, m: (i, m[0])),
                pl.BlockSpec((tile, width), lambda i, m: (i, m[1])),
            ],
            out_specs=part,
        ),
        out_shape=jax.ShapeDtypeStruct((rows, depth), F32),
        compiler_params=params(16),
        cost_estimate=cost(2e9, 4e6),
        name="half_sum",
    )(blocks, *parts, mine, other, rim, x_weight, x_weight)


def last_kernel(
    heads, rim_width, side_ref, part_ref, rim_ref, rim0_ref, bc_own_ref, bc_recv_ref, bcw_ref, dtw_ref,
    out_ref, bc_ref, dt_ref,
):
    rows = part_ref.shape[0]
    states2 = bcw_ref.shape[1]
    all_heads = dtw_ref.shape[0]

    @pl.when(pl.program_id(0) == 0)
    def _():
        bc = bc_own_ref[:, :states2] + bc_recv_ref[:, :states2].astype(F32)
        rim = rim_ref[:, rim_width:].astype(F32) + rim0_ref[:, rim_width:].astype(F32)
        extra = rim[:16] + rim[16:]
        for at, value in ((0, bc[: rows - 16, :]), (rows - 16, bc[rows - 16 :, :] + extra)):
            high, low = split2(value)
            bc_ref[at : at + value.shape[0], :states2] = high
            bc_ref[at : at + value.shape[0], states2:] = low
        shape = (LANES, all_heads)
        row, col = iota(shape, 0), iota(shape, 1)
        x = side_ref[0]
        here = jnp.where((row < heads) & (col == row + x * heads), 1.0, 0.0).astype(BF)
        there = jnp.where((row < heads) & (col == row + (1 - x) * heads), 1.0, 0.0).astype(BF)
        dt = mm(bc_own_ref[:, states2:].astype(BF), here) + mm(bc_recv_ref[:, states2:], there)
        dt_ref[...] = dt.astype(BF)

    bcw = bcw_ref[...]
    total = part_ref[...] + mm_nt(bc_ref[...], jnp.concatenate([bcw, bcw], axis=1))
    out_ref[...] = (total + mm(dt_ref[...], dtw_ref[...])).astype(BF)


def last_half(side, part, rim, rim0, bc_own, bc_recv, bc_weight, dt_rows, tile):
    rows, depth = part.shape
    states2, all_heads = bc_weight.shape[1], dt_rows.shape[0]
    whole = lambda a: pl.BlockSpec(a.shape, lambda i, m: (0, 0))
    return pl.pallas_call(
        functools.partial(last_kernel, all_heads // 2, rim.shape[1] - states2),
        grid_spec=pltpu.PrefetchScalarGridSpec(
            num_scalar_prefetch=1,
            grid=(depth // tile,),
            in_specs=[
                pl.BlockSpec((rows, tile), lambda i, m: (0, i)),
                whole(rim), whole(rim0), whole(bc_own), whole(bc_recv),
                pl.BlockSpec((tile, states2), lambda i, m: (i, 0)),
                pl.BlockSpec((all_heads, tile), lambda i, m: (0, i)),
            ],
            out_specs=pl.BlockSpec((rows, tile), lambda i, m: (0, i)),
            scratch_shapes=[pltpu.VMEM((rows, 2 * states2), BF), pltpu.VMEM((rows, all_heads), BF)],
        ),
        out_shape=jax.ShapeDtypeStruct((rows, depth), BF),
        compiler_params=params(16),
        cost_estimate=cost(5e8, 2e6),
        name="last_half",
    )(side, part, rim, rim0, bc_own, bc_recv, bc_weight, dt_rows)


def by_chips(
    tokens, x_weight, bc_weight, dt_weight, conv_inner, conv_shared, dt_bias, decay_rate, norm_gain,
    doc_starts, grad_out,
):
    blocks = lax.axis_size("ctx")
    chips = blocks // 2
    rows = tokens.shape[0]
    all_heads = dt_weight.shape[1]
    heads = decay_rate.shape[0] // 2
    width = heads * HEAD_DIM
    place = lax.axis_index("ctx").astype(jnp.int32)
    x = lax.axis_index("fsdp").astype(jnp.int32)
    k = place % 2
    meta = jnp.stack([k, x, place // 2])

    core = [(i, i ^ 1) for i in range(blocks)]
    pair = [(0, 1), (1, 0)]
    cross = [(2 * i + j, 2 * (i ^ 1) + (1 - j)) for i in range(blocks) for j in range(2)]
    by_core = lambda a: lax.ppermute(a, "ctx", core)
    by_x = lambda a: lax.ppermute(a, "fsdp", pair)
    by_both = lambda a: lax.ppermute(a, ("ctx", "fsdp"), cross)
    groups = [[2 * i for i in range(chips)], [2 * i + 1 for i in range(chips)]]
    exchange = lambda a: lax.all_to_all(a, "ctx", 0, 0, axis_index_groups=groups)

    def column_block(side, half):
        return (side * 2 + half)[None]

    tail = tokens[rows - 16 :]
    ra = lax.ppermute(tail, "ctx", [(2 * i - 1, 2 * i) for i in range(1, chips)])
    rb = lax.ppermute(tail, "ctx", [(2 * i - 1, 2 * i + 1) for i in range(1, chips)])

    dt_rows = dt_weight.T
    to_cross, small, low = lead_proj(
        column_block(1 - x, 1 - k), tokens, x_weight, bc_weight, dt_rows, width
    )
    from_cross = by_both(to_cross)
    small_x = by_x(small)
    to_x, to_core, mine, rim_own, rim_send = rest_proj(
        jnp.stack([(1 - x) * 2 + k, x * 2 + 1 - k, x * 2 + k]), tokens, x_weight, bc_weight, ra, rb, width
    )
    from_x = by_x(to_x)
    from_core = by_core(to_core)
    rim_recv = by_x(rim_send)
    small_core = by_core(small)
    small_cross = by_core(small_x)
    low_x = by_x(low)
    lows = (low, low_x, by_core(low), by_core(low_x))
    go_recv = by_core(lax.dynamic_slice(grad_out, (jnp.int32(0), (1 - k) * width), (rows, width)))

    prm = jnp.stack([lax.dynamic_slice(v, (k * heads,), (heads,)) for v in (dt_bias, decay_rate)])
    prm = jnp.pad(prm, ((0, 6), (0, LANES - heads)))
    bact, bpre, delta, ramp, sig, rampt, dpk, wpk, epk, keep = shared_maps(
        meta, doc_starts, small, small_x, small_core, small_cross, rim_own, rim_recv, conv_shared,
        prm, heads, all_heads,
    )
    pre, xd, loc, send = inner_maps(
        meta, doc_starts, mine, from_x, from_core, from_cross, rim_own, rim_recv, conv_inner, bact,
        dpk, wpk, keep, heads, chips,
    )
    keeps = exchange(send)
    y, cbt = within(
        meta, doc_starts, xd, ramp, rampt, (small, small_x, small_core, small_cross), lows, rim_own, rim_recv,
        conv_shared, heads,
    )
    states = exchange(chain(keeps, keeps, heads, width, False))
    state = states.reshape(STATE, width)
    mix_own, mix_send, dy, edy, dots, both, late, back = outputs_of(
        meta, y, state, loc, bact, epk, keep, grad_out, go_recv, norm_gain[None, :], heads, chips
    )
    act, far, wx, slope, reach = slopes_of(pre, dpk, wpk)
    backs = exchange(back)
    near, q, dbc = within_back(
        meta, doc_starts, dy, edy, both, xd, bact, ramp, rampt, cbt, act, slope, heads
    )
    mix_recv = by_core(mix_send)
    mixed = jnp.where(
        k == 0,
        jnp.concatenate([mix_own, mix_recv], axis=1),
        jnp.concatenate([mix_recv, mix_own], axis=1),
    )
    adj = exchange(chain(backs, keeps, heads, width, True)).reshape(STATE, width)
    g_mine, g_other, bc_mine, bc_other, rim = grads_of(
        meta, doc_starts, adj, late, keep, both, bact, near, far, wx, reach, q, dbc, bpre, delta, sig,
        dots, prm, conv_shared, conv_inner, heads,
    )
    g_x = by_x(g_mine)
    g_cross = by_both(g_other)
    g_core = by_core(g_other)
    rims = jnp.concatenate([rim, by_core(rim)], axis=0)
    back_perm = [(2 * i + 1, 2 * i - 1) for i in range(1, chips)]
    rim0 = lax.ppermute(rims, "ctx", back_perm)
    rim1 = lax.ppermute(
        rims, ("ctx", "fsdp"), [(2 * a + j, 2 * b + (1 - j)) for a, b in back_perm for j in range(2)]
    )
    bc_chip, bc_send = join(meta, bc_mine, by_core(bc_other), heads)
    bc_recv = by_x(bc_send)
    part = first_half(
        jnp.stack([x * 2 + k, x * 2 + 1 - k]), None, g_mine, g_core, rim0, x_weight, 640
    )
    part = first_half(
        jnp.stack([(1 - x) * 2 + k, (1 - x) * 2 + 1 - k]), part, g_x, g_cross, rim1, x_weight, 640
    )
    grad_tokens = last_half(x[None], part, rim1, rim0, bc_chip, bc_recv, bc_weight, dt_rows, width)
    return (mixed, grad_tokens)


def splits_by_chip(mesh):
    return mesh.shape["fsdp"] == 2 and mesh.shape["ctx"] == 16


def solution(mesh):
    in_specs = (
        P("ctx", "fsdp"),
        P("fsdp", None),
        P("fsdp", None),
        P("fsdp", None),
        P(None, "fsdp"),
        P(),
        P("fsdp"),
        P("fsdp"),
        P("fsdp"),
        P(),
        P("ctx", "fsdp"),
    )
    body = by_chips if splits_by_chip(mesh) else on_device
    out_specs = (P("ctx", "fsdp"), P("ctx", "fsdp"))
    return jax.shard_map(
        body, mesh=mesh, in_specs=in_specs, out_specs=out_specs, check_vma=False
    )
```

```python
import functools

import jax
import jax.numpy as jnp
from jax import lax
from jax.experimental import pallas as pl
from jax.experimental.pallas import tpu as pltpu
from jax.sharding import PartitionSpec as P

HEAD_DIM = 64
STATE = 128


exact = lax.Precision.HIGHEST
epsilon = 1e-05


def from_behind(value, axis, steps):
    count = lax.axis_size(axis)
    leading, last = (max(0, -steps), min(count, count - steps))
    return lax.ppermute(value, axis, [(source, source + steps) for source in range(leading, last)])


def prefix(part, axis, combine, identity, reverse):
    count = lax.axis_size(axis)
    place = lax.axis_index(axis)
    ahead = count - 1 - place if reverse else place
    gathered = jax.tree.map(lambda a: lax.all_gather(a, axis), part)
    state = jax.tree.map(lambda a, e: jnp.zeros_like(a) + jnp.asarray(e, a.dtype), part, identity)

    def one(step, state):
        source = count - 1 - step if reverse else step
        return combine(
            state, jax.tree.map(lambda a: lax.dynamic_index_in_dim(a, source, 0, False), gathered)
        )

    return lax.fori_loop(0, ahead, one, state)


def doc_index(positions, doc_starts):
    hits = (doc_starts[None, :] <= positions[:, None]).astype(jnp.int32)
    return jnp.sum(hits, axis=1) - 1


def causal_conv(padded, docs_ext, taps):
    count = padded.shape[0] - 3
    docs_now = docs_ext[3:]
    total = jnp.zeros((count, padded.shape[1]), jnp.float32)
    for offset in range(4):
        rows = padded[3 - offset : 3 - offset + count]
        same = (docs_ext[3 - offset : 3 - offset + count] == docs_now).astype(jnp.float32)
        total = total + taps[offset][None, :] * rows * same[:, None]
    return total


def block_out(x_act, b_act, c_act, delta, docs, doc_before, state_in, decay_rate):
    count = delta.shape[0]
    places = jnp.arange(count, dtype=jnp.int32)
    lower = places[:, None] >= places[None, :]
    ramp = -jnp.dot(lower.astype(jnp.float32), delta, precision=exact) * decay_rate[None, :]
    same = jnp.logical_and(docs[:, None] == docs[None, :], lower)
    gap = ramp[:, None, :] - ramp[None, :, :]
    decay = jnp.exp(jnp.where(same[:, :, None], gap, 0.0)) * same.astype(jnp.float32)[:, :, None]
    scores = jnp.dot(c_act, b_act.T, precision=exact)
    mixing = decay * scores[:, :, None] * delta[None, :, :]
    inner = jnp.einsum("tsh,shp->thp", mixing, x_act, precision=exact)
    carried = (docs == doc_before).astype(jnp.float32)
    enter = jnp.exp(ramp) * carried[:, None]
    from_state = jnp.einsum("tn,hpn->thp", c_act, state_in, precision=exact) * enter[:, :, None]
    last_doc = docs[count - 1]
    tail = (
        jnp.exp(ramp[count - 1][None, :] - ramp)
        * (docs == last_doc).astype(jnp.float32)[:, None]
        * delta
    )
    weighted = tail[:, :, None] * x_act
    state_loc = jnp.einsum("shp,sn->hpn", weighted, b_act, precision=exact)
    keep = jnp.exp(ramp[count - 1]) * (last_doc == doc_before).astype(jnp.float32)
    return (inner + from_state, state_loc, keep)


def head_norm(values, norm_gain):
    scale = lax.rsqrt(jnp.mean(values * values, axis=-1, keepdims=True) + epsilon)
    normed = values * scale
    return normed.reshape(values.shape[0], values.shape[1] * values.shape[2]) * norm_gain[None, :]


def link(earlier, later):
    return (earlier[0] * later[0], later[0][:, None, None] * earlier[1] + later[1])


def on_device(
    tokens,
    x_weight,
    bc_weight,
    dt_weight,
    conv_inner,
    conv_shared,
    dt_bias,
    decay_rate,
    norm_gain,
    doc_starts,
    grad_out,
):
    count = tokens.shape[0]
    heads_here = decay_rate.shape[0]
    features = lax.all_gather(tokens, "fsdp", axis=1, tiled=True)
    x_cols, dt_cols = (
        lax.all_to_all(x_weight, "fsdp", split_axis=1, concat_axis=0, tiled=True),
        lax.all_to_all(dt_weight, "fsdp", split_axis=1, concat_axis=0, tiled=True),
    )
    bc_all = lax.all_gather(bc_weight, "fsdp", axis=0, tiled=True)
    x_proj = jnp.dot(features, x_cols, preferred_element_type=jnp.float32).astype(jnp.bfloat16)
    bc_proj = jnp.dot(features, bc_all, preferred_element_type=jnp.float32)
    dt_raw = jnp.dot(features, dt_cols, preferred_element_type=jnp.float32)
    x_wide = lax.optimization_barrier(x_proj).astype(jnp.float32)
    rim_x, rim_bc = from_behind((x_wide[count - 3 :], bc_proj[count - 3 :]), "ctx", 1)
    x_ext = jnp.concatenate([rim_x, x_wide], axis=0)
    bc_ext = jnp.concatenate([rim_bc, bc_proj], axis=0)
    first = lax.axis_index("ctx") * count
    positions = first - 3 + jnp.arange(count + 3, dtype=jnp.int32)
    docs_ext = doc_index(positions, doc_starts)
    docs = docs_ext[3:]
    doc_before = docs_ext[2]

    def layer(x_in, bc_in, dt_in, state_in):
        x_act = jax.nn.silu(causal_conv(x_in, docs_ext, conv_inner))
        bc_act = jax.nn.silu(causal_conv(bc_in, docs_ext, conv_shared))
        delta = jax.nn.softplus(dt_in + dt_bias[None, :])
        values, state_loc, keep = block_out(
            x_act.reshape(count, heads_here, HEAD_DIM),
            bc_act[:, :STATE],
            bc_act[:, STATE:],
            delta,
            docs,
            doc_before,
            state_in,
            decay_rate,
        )
        return (head_norm(values, norm_gain), state_loc, keep)

    blank = jnp.zeros((heads_here, HEAD_DIM, STATE), jnp.float32)
    unit = jnp.ones((heads_here,), jnp.float32)
    _, state_loc, keep = layer(x_ext, bc_ext, dt_raw, blank)
    state_in = prefix((keep, state_loc), "ctx", link, (unit, blank), False)[1]
    outputs, pull = jax.vjp(layer, x_ext, bc_ext, dt_raw, state_in)
    normed = outputs[0]
    grads_out = pull((grad_out.astype(jnp.float32), jnp.zeros_like(blank), jnp.zeros_like(unit)))
    adjoint = prefix((keep, grads_out[3]), "ctx", link, (unit, blank), True)[1]
    keep_grad = jnp.sum(adjoint * state_in, axis=(1, 2))
    grads_state = pull((jnp.zeros_like(normed), adjoint, keep_grad))
    grad_xe = grads_out[0] + grads_state[0]
    grad_bce = grads_out[1] + grads_state[1]
    grad_dt = grads_out[2] + grads_state[2]
    back_x, back_bc = from_behind((grad_xe[:3], grad_bce[:3]), "ctx", -1)
    grad_x = grad_xe[3:].at[count - 3 :].add(back_x)
    grad_bc = grad_bce[3:].at[count - 3 :].add(back_bc)
    grad_xb = grad_x.astype(jnp.bfloat16)
    grad_rows = lax.all_gather(grad_xb, "fsdp", axis=1, tiled=True)
    column = lax.axis_index("fsdp") * heads_here
    dt_wide = lax.dynamic_update_slice(
        jnp.zeros((count, dt_weight.shape[1]), jnp.float32), grad_dt, (jnp.int32(0), column)
    )
    bc_total, dt_total = lax.psum((grad_bc, dt_wide), "fsdp")
    grad_local = jnp.dot(grad_rows, x_weight.T, preferred_element_type=jnp.float32)
    grad_local = grad_local + jnp.dot(bc_total, bc_weight.T.astype(jnp.float32), precision=exact)
    grad_local = grad_local + jnp.dot(dt_total, dt_weight.T.astype(jnp.float32), precision=exact)
    grad_tokens = grad_local.astype(jnp.bfloat16)
    return (normed.astype(jnp.bfloat16), grad_tokens)


BF = jnp.bfloat16
F32 = jnp.float32
LOG2E = 1.4426950408889634
LANES = 128
NEG = -1e30


def params(mb=60, **kw):
    return pltpu.CompilerParams(vmem_limit_bytes=mb * 1024 * 1024, **kw)


def cost(flops, nbytes):
    return pl.CostEstimate(flops=int(flops), bytes_accessed=int(nbytes), transcendentals=0)


def mm(a, b):
    return jnp.dot(a, b, preferred_element_type=F32)


def mm_nt(a, b):
    return lax.dot_general(a, b, (((1,), (1,)), ((), ())), preferred_element_type=F32)


def mm_tn(a, b):
    return lax.dot_general(a, b, (((0,), (0,)), ((), ())), preferred_element_type=F32)


def split2(v):
    hi = v.astype(BF)
    return hi, (v - hi.astype(F32)).astype(BF)


def iota(shape, dim):
    return lax.broadcasted_iota(jnp.int32, shape, dim)


def doc_start_of(pos, docs_ref, count):
    start = jnp.zeros_like(pos)
    for i in range(count):
        start = jnp.where(docs_ref[i] <= pos, docs_ref[i], start)
    return start


def spread(heads, width):
    shape = (LANES, width)
    row, col = iota(shape, 0), iota(shape, 1)
    head = jnp.right_shift(col, 6)
    return jnp.where((row == head) | (row == head + 16), 1.0, 0.0).astype(BF)


def gather_heads(width):
    shape = (width, LANES)
    return jnp.where(jnp.right_shift(iota(shape, 0), 6) == iota(shape, 1), 1.0, 0.0).astype(BF)


def packed(v):
    hi = v.astype(BF).astype(F32)
    lo = v - hi
    lane = iota(v.shape, 1)
    return jnp.where(lane < 16, hi, pltpu.roll(lo, 16, 1)).astype(BF)


def over_heads(v, gather):
    hi, lo = split2(v)
    return mm(hi, gather) + mm(lo, gather)


def silu_parts(v):
    sig = 1.0 / (1.0 + jnp.exp(-v))
    return v * sig, sig * (1.0 + v * (1.0 - sig))


def fetch(src, dst, sem):
    copy = pltpu.make_async_copy(src, dst, sem)
    copy.start()
    return copy


def columns(w_ref, block, width):
    return w_ref.at[:, pl.ds(pl.multiple_of(block * width, LANES), width)]


def lead_kernel(
    meta_ref, tok_hbm, w_hbm, bcw_hbm, dtw_hbm, piece_ref, out_ref, low_ref, tok_ref, w_ref, bcw_ref,
    dtw_ref, sems,
):
    width = w_ref.shape[1]
    get_tok = fetch(tok_hbm, tok_ref, sems.at[0])
    get_w = fetch(columns(w_hbm, meta_ref[0], width), w_ref, sems.at[1])
    get_bcw = fetch(bcw_hbm, bcw_ref, sems.at[2])
    get_dtw = fetch(dtw_hbm, dtw_ref, sems.at[3])
    get_tok.wait()
    get_w.wait()
    piece_ref[...] = mm(tok_ref[...], w_ref[...]).astype(BF)
    get_bcw.wait()
    get_dtw.wait()
    states = bcw_ref.shape[1]
    heads = dtw_ref.shape[0]
    out_ref[:, :states], low_ref[...] = split2(mm(tok_ref[...], bcw_ref[...]))
    hi, lo = split2(mm_nt(tok_ref[...], dtw_ref[...]))
    shape = (heads, LANES)
    row, col = iota(shape, 0), iota(shape, 1)
    first = jnp.where(row == col, 1.0, 0.0).astype(BF)
    second = jnp.where(row + heads == col, 1.0, 0.0).astype(BF)
    out_ref[:, states:] = (mm(hi, first) + mm(lo, second)).astype(BF)


def lead_proj(block, tokens, x_weight, bc_weight, dt_rows, width):
    rows, depth = tokens.shape
    states = bc_weight.shape[1]
    hbm = pl.BlockSpec(memory_space=pl.ANY)
    vm = pl.BlockSpec(memory_space=pltpu.VMEM)
    return pl.pallas_call(
        lead_kernel,
        grid_spec=pltpu.PrefetchScalarGridSpec(
            num_scalar_prefetch=1,
            grid=(),
            in_specs=[hbm] * 4,
            out_specs=[vm] * 3,
            scratch_shapes=[
                pltpu.VMEM((rows, depth), BF),
                pltpu.VMEM((depth, width), BF),
                pltpu.VMEM((depth, states), BF),
                pltpu.VMEM(dt_rows.shape, BF),
                pltpu.SemaphoreType.DMA((4,)),
            ],
        ),
        out_shape=[
            jax.ShapeDtypeStruct((rows, width), BF),
            jax.ShapeDtypeStruct((rows, states + LANES), BF),
            jax.ShapeDtypeStruct((rows, states), BF),
        ],
        compiler_params=params(),
        cost_estimate=cost(2 * rows * depth * width, 3e6),
        name="lead_proj",
    )(block, tokens, x_weight, bc_weight, dt_rows)


def rest_kernel(
    meta_ref, tok_hbm, w_hbm, bcw_hbm, ra_hbm, rb_hbm, peer_ref, core_ref, mine_ref, own_ref, send_ref,
    tok_ref, w_ref, bcw_ref, ra_ref, rb_ref, sems,
):
    width = w_ref.shape[2]
    get_tok = fetch(tok_hbm, tok_ref, sems.at[0])
    get_w = [fetch(columns(w_hbm, meta_ref[i], width), w_ref.at[i], sems.at[1 + i]) for i in range(3)]
    get_bcw = fetch(bcw_hbm, bcw_ref, sems.at[4])
    get_ra = fetch(ra_hbm, ra_ref, sems.at[5])
    get_rb = fetch(rb_hbm, rb_ref, sems.at[6])
    get_tok.wait()
    for i, ref in enumerate((peer_ref, core_ref, mine_ref)):
        get_w[i].wait()
        ref[...] = mm(tok_ref[...], w_ref[i]).astype(BF)
    get_bcw.wait()
    get_ra.wait()
    get_rb.wait()
    rim = ra_ref[...] + rb_ref[...]
    shared = mm(rim, bcw_ref[...]).astype(BF)
    own_ref[:, :width] = mm(rim, w_ref[2]).astype(BF)
    own_ref[:, width:] = shared
    send_ref[:, :width] = mm(rim, w_ref[0]).astype(BF)
    send_ref[:, width:] = shared


def rest_proj(blocks, tokens, x_weight, bc_weight, ra, rb, width):
    rows, depth = tokens.shape
    states = bc_weight.shape[1]
    hbm = pl.BlockSpec(memory_space=pl.ANY)
    vm = pl.BlockSpec(memory_space=pltpu.VMEM)
    piece = jax.ShapeDtypeStruct((rows, width), BF)
    rim = jax.ShapeDtypeStruct((ra.shape[0], width + states), BF)
    return pl.pallas_call(
        rest_kernel,
        grid_spec=pltpu.PrefetchScalarGridSpec(
            num_scalar_prefetch=1,
            grid=(),
            in_specs=[hbm] * 5,
            out_specs=[vm] * 5,
            scratch_shapes=[
                pltpu.VMEM((rows, depth), BF),
                pltpu.VMEM((3, depth, width), BF),
                pltpu.VMEM((depth, states), BF),
                pltpu.VMEM(ra.shape, BF),
                pltpu.VMEM(rb.shape, BF),
                pltpu.SemaphoreType.DMA((7,)),
            ],
        ),
        out_shape=[piece, piece, piece, rim, rim],
        compiler_params=params(),
        cost_estimate=cost(6 * rows * depth * width, 6e6),
        name="rest_proj",
    )(blocks, tokens, x_weight, bc_weight, ra, rb)


def conv_masks(docs_ref, count, base, rows, lanes):
    pos = base + iota((rows, lanes), 0)
    start = doc_start_of(pos, docs_ref, count)
    return [jnp.where(pos - k >= start, 1.0, 0.0) for k in range(1, 4)]


def shared_kernel(
    docs, heads, all_heads, meta_ref, docs_ref, own_ref, xr_ref, cr_ref, dr_ref, rim_own_ref,
    rim_recv_ref, taps_ref, prm_ref, bact_ref, bpre_ref, delta_ref, ramp_ref, sig_ref, rampt_ref,
    dpk_ref, wpk_ref, epk_ref, keep_ref, ext_ref,
):
    k, x, chip = meta_ref[0], meta_ref[1], meta_ref[2]
    rows = own_ref.shape[0]
    total = 2 * rows
    states2 = bact_ref.shape[1]
    base = chip * total
    mine = pl.multiple_of(8 + k * rows, 8)
    other = pl.multiple_of(8 + (1 - k) * rows, 8)
    width = rim_own_ref.shape[1] - states2
    rim = rim_own_ref[:, width:].astype(F32) + rim_recv_ref[:, width:].astype(F32)
    ext_ref[0:8, :] = rim[8:16, :]
    ext_ref[pl.ds(mine, rows), :] = own_ref[:, :states2].astype(F32) + xr_ref[:, :states2].astype(F32)
    ext_ref[pl.ds(other, rows), :] = cr_ref[:, :states2].astype(F32) + dr_ref[:, :states2].astype(F32)

    tile = 64

    def conv(step, _):
        at = pl.multiple_of(step * tile, tile)
        masks = conv_masks(docs_ref, docs, base + at, tile, LANES)
        for lane in range(0, states2, LANES):
            sl = slice(lane, lane + LANES)
            window = ext_ref[pl.ds(at, tile + 8), sl]
            value = window[8:] * taps_ref[0:1, sl]
            for j in range(1, 4):
                value = value + window[8 - j : 8 - j + tile] * taps_ref[j : j + 1, sl] * masks[j - 1]
            bpre_ref[pl.ds(at, tile), sl] = value
            bact_ref[pl.ds(at, tile), sl] = (value / (1.0 + jnp.exp(-value))).astype(BF)
        return 0

    lax.fori_loop(0, total // tile, conv, 0)

    shape = (LANES, LANES)
    row, col = iota(shape, 0), iota(shape, 1)
    first = x * (all_heads // 2) + k * heads
    wanted = (col < heads) & ((row == first + col) | (row == all_heads + first + col))
    select = jnp.where(wanted, 1.0, 0.0).astype(BF)
    square = (rows, rows)
    lower = jnp.where(iota(square, 0) >= iota(square, 1), 1.0, 0.0).astype(BF)
    bias, rate = prm_ref[0:1, :], prm_ref[1:2, :]

    def steps(part, ref_a, ref_b):
        at = pl.multiple_of(part * rows, rows)
        raw = mm(ref_a[:, states2:], select) + mm(ref_b[:, states2:], select) + bias
        delta = jnp.maximum(raw, 0.0) + jnp.log1p(jnp.exp(-jnp.abs(raw)))
        delta_ref[pl.ds(at, rows), :] = delta
        sig_ref[pl.ds(at, rows), :] = 1.0 / (1.0 + jnp.exp(-raw))
        dpk_ref[pl.ds(at, rows), :] = packed(delta)
        hi, rest = split2(delta)
        mid = rest
        low = (delta - hi.astype(F32) - mid.astype(F32)).astype(BF)
        ramp = -(mm(lower, hi) + mm(lower, mid) + mm(lower, low)) * (rate * LOG2E)
        ramp_ref[pl.ds(at, rows), :] = ramp
        rampt_ref[part] = jnp.transpose(ramp)[:16, :]
        begin = base + at
        end = begin + rows - 1
        pos = begin + iota((rows, LANES), 0)
        start = doc_start_of(pos, docs_ref, docs)
        last = doc_start_of(jnp.zeros((1, LANES), jnp.int32) + end, docs_ref, docs)
        final = ramp[rows - 1 : rows, :]
        epk_ref[pl.ds(at, rows), :] = packed(jnp.where(start < begin, jnp.exp2(ramp), 0.0))
        wpk_ref[pl.ds(at, rows), :] = packed(jnp.where(pos >= last, jnp.exp2(final - ramp), 0.0))
        keep_ref[part] = jnp.zeros((8, LANES), F32) + jnp.where(last < begin, jnp.exp2(final), 0.0)

    steps(k, own_ref, xr_ref)
    steps(1 - k, cr_ref, dr_ref)


def shared_maps(meta, doc_starts, own, xr, cr, dr, rim_own, rim_recv, taps, prm, heads, all_heads):
    rows = own.shape[0]
    total, states2 = 2 * rows, own.shape[1] - LANES
    compact = jax.ShapeDtypeStruct((total, LANES), F32)
    compact_b = jax.ShapeDtypeStruct((total, LANES), BF)
    vm = pl.BlockSpec(memory_space=pltpu.VMEM)
    return pl.pallas_call(
        functools.partial(shared_kernel, doc_starts.shape[0], heads, all_heads),
        grid_spec=pltpu.PrefetchScalarGridSpec(
            num_scalar_prefetch=2,
            grid=(),
            in_specs=[vm] * 8,
            out_specs=[vm] * 10,
            scratch_shapes=[pltpu.VMEM((total + 8, states2), F32)],
        ),
        out_shape=[
            jax.ShapeDtypeStruct((total, states2), BF),
            jax.ShapeDtypeStruct((total, states2), F32),
            compact,
            compact,
            compact,
            jax.ShapeDtypeStruct((2, 16, rows), F32),
            compact_b,
            compact_b,
            compact_b,
            jax.ShapeDtypeStruct((2, 8, LANES), F32),
        ],
        compiler_params=params(),
        cost_estimate=cost(4e9, 4e6),
        name="shared_maps",
    )(meta, doc_starts, own, xr, cr, dr, rim_own, rim_recv, taps, prm)


def keep_row(keep, heads, width):
    hi, rest = split2(keep)
    low = (keep - hi.astype(F32) - rest.astype(F32)).astype(BF)
    wide = spread(heads, width)
    lane = iota(keep.shape, 1)
    clean = lambda v: jnp.where(lane < 16, v.astype(F32), 0.0).astype(BF)
    return mm(clean(hi), wide) + mm(clean(rest), wide) + mm(clean(low), wide)


def inner_kernel(
    docs, heads, meta_ref, docs_ref, own_ref, xr_ref, cr_ref, dr_ref, rim_own_ref, rim_recv_ref,
    taps_ref, bact_ref, dpk_ref, wpk_ref, keep_ref, pre_ref, xd_ref, loc_ref, send_ref, ext_ref,
    wx_ref,
):
    k, chip = meta_ref[0], meta_ref[2]
    rows, width = own_ref.shape
    total = 2 * rows
    states = bact_ref.shape[1] // 2
    base = chip * total
    mine = pl.multiple_of(8 + k * rows, 8)
    other = pl.multiple_of(8 + (1 - k) * rows, 8)
    rim = (rim_own_ref[:, :width].astype(F32) + rim_recv_ref[:, :width].astype(F32))
    ext_ref[0:8, :] = rim.astype(BF).astype(F32)[8:16, :]

    def total_of(a, b):
        return (a[...].astype(F32) + b[...].astype(F32)).astype(BF).astype(F32)

    ext_ref[pl.ds(mine, rows), :] = total_of(own_ref, xr_ref)
    ext_ref[pl.ds(other, rows), :] = total_of(cr_ref, dr_ref)
    wide = spread(heads, width)
    tile = 64

    def conv(step, _):
        at = pl.multiple_of(step * tile, tile)
        masks = conv_masks(docs_ref, docs, base + at, tile, LANES)
        dpk = dpk_ref[pl.ds(at, tile), :]
        wpk = wpk_ref[pl.ds(at, tile), :]
        for lane in range(0, width, LANES):
            sl = slice(lane, lane + LANES)
            window = ext_ref[pl.ds(at, tile + 8), sl]
            value = window[8:] * taps_ref[0:1, sl]
            for j in range(1, 4):
                value = value + window[8 - j : 8 - j + tile] * taps_ref[j : j + 1, sl] * masks[j - 1]
            pre_ref[pl.ds(at, tile), sl] = value
            act = value / (1.0 + jnp.exp(-value))
            xd = act * mm(dpk, wide[:, sl])
            xd_ref[pl.ds(at, tile), sl] = xd.astype(BF)
            wx_ref[pl.ds(at, tile), sl] = (xd * mm(wpk, wide[:, sl])).astype(BF)
        return 0

    lax.fori_loop(0, total // tile, conv, 0)
    locs = []
    for part in range(2):
        sl = slice(part * rows, (part + 1) * rows)
        loc = mm_tn(bact_ref[sl, :states], wx_ref[sl, :])
        loc_ref[part] = loc
        locs.append(loc)
    second = keep_row(keep_ref[1], heads, width)[0:1, :]
    state = locs[0] * second + locs[1]
    chips, piece = send_ref.shape[0], send_ref.shape[1]
    for i in range(chips):
        send_ref[i, :, :width] = state[i * piece : (i + 1) * piece, :].astype(BF)
    keep = jnp.where(iota((8, LANES), 1) < 16, keep_ref[0] * keep_ref[1], 0.0)
    hi, mid = split2(keep)
    low = (keep - hi.astype(F32) - mid.astype(F32)).astype(BF)
    row = iota((8, LANES), 0)
    stack = jnp.where(row == 0, hi.astype(F32), jnp.where(row == 1, mid.astype(F32), low.astype(F32)))
    stack = jnp.concatenate([stack, jnp.zeros((piece - 8, LANES), F32)], axis=0).astype(BF)
    for i in range(chips):
        send_ref[i, :, width:] = stack


def inner_maps(
    meta, doc_starts, own, xr, cr, dr, rim_own, rim_recv, taps, bact, dpk, wpk, keep, heads, chips
):
    rows, width = own.shape
    total, states = 2 * rows, bact.shape[1] // 2
    vm = pl.BlockSpec(memory_space=pltpu.VMEM)
    whole = lambda shape: pl.BlockSpec(shape, lambda i, m, d: (0,) * len(shape))
    half = pl.BlockSpec((taps.shape[0], width), lambda i, m, d: (0, m[0]))
    outs = [
        jax.ShapeDtypeStruct((total, width), F32),
        jax.ShapeDtypeStruct((total, width), BF),
        jax.ShapeDtypeStruct((2, states, width), F32),
        jax.ShapeDtypeStruct((chips, states // chips, width + LANES), BF),
    ]
    return pl.pallas_call(
        functools.partial(inner_kernel, doc_starts.shape[0], heads),
        grid_spec=pltpu.PrefetchScalarGridSpec(
            num_scalar_prefetch=2,
            grid=(1,),
            in_specs=[
                whole(own.shape), whole(xr.shape), whole(cr.shape), whole(dr.shape),
                whole(rim_own.shape), whole(rim_recv.shape), half, whole(bact.shape),
                whole(dpk.shape), whole(wpk.shape), whole(keep.shape),
            ],
            out_specs=[whole(o.shape) for o in outs],
            scratch_shapes=[pltpu.VMEM((total + 8, width), F32), pltpu.VMEM((total, width), BF)],
        ),
        out_shape=outs,
        compiler_params=params(),
        cost_estimate=cost(4e9, 4e6),
        name="inner_maps",
    )(meta, doc_starts, own, xr, cr, dr, rim_own, rim_recv, taps, bact, dpk, wpk, keep)


def within_kernel(
    docs, heads, meta_ref, docs_ref, xd_ref, ramp_ref, rampt_ref, own_ref, xr_ref, cr_ref, dr_ref,
    own_low_ref, xr_low_ref, cr_low_ref, dr_low_ref, rim_own_ref, rim_recv_ref, taps_ref, y_ref,
    cbt_ref, cb_ref, gate_ref, ext_ref, high_ref, low_ref,
):
    k, chip = meta_ref[0], meta_ref[2]
    total, width = xd_ref.shape
    rows = total // 2
    states2 = own_low_ref.shape[1]
    states = states2 // 2
    mine = pl.multiple_of(8 + k * rows, 8)
    other = pl.multiple_of(8 + (1 - k) * rows, 8)
    rim = rim_own_ref[:, width:].astype(F32) + rim_recv_ref[:, width:].astype(F32)
    ext_ref[0:8, :] = rim[8:16, :]

    def exact_sum(a, a_low, b, b_low):
        high = a[:, :states2].astype(F32) + b[:, :states2].astype(F32)
        return high + (a_low[...].astype(F32) + b_low[...].astype(F32))

    ext_ref[pl.ds(mine, rows), :] = exact_sum(own_ref, own_low_ref, xr_ref, xr_low_ref)
    ext_ref[pl.ds(other, rows), :] = exact_sum(cr_ref, cr_low_ref, dr_ref, dr_low_ref)
    tile = 64

    def conv(step, _):
        at = pl.multiple_of(step * tile, tile)
        masks = conv_masks(docs_ref, docs, chip * total + at, tile, LANES)
        for lane in range(0, states2, LANES):
            sl = slice(lane, lane + LANES)
            window = ext_ref[pl.ds(at, tile + 8), sl]
            value = window[8:] * taps_ref[0:1, sl]
            for j in range(1, 4):
                value = value + window[8 - j : 8 - j + tile] * taps_ref[j : j + 1, sl] * masks[j - 1]
            high, low = split2(value / (1.0 + jnp.exp(-value)))
            high_ref[pl.ds(at, tile), sl] = high
            low_ref[pl.ds(at, tile), sl] = low
        return 0

    lax.fori_loop(0, total // tile, conv, 0)
    square = (rows, rows)
    lane = iota((rows, LANES), 1)
    for part in range(2):
        sl = slice(part * rows, (part + 1) * rows)
        begin = chip * total + part * rows
        b, c = high_ref[sl, :states], high_ref[sl, states:]
        b_low, c_low = low_ref[sl, :states], low_ref[sl, states:]
        cb_ref[...] = mm_nt(c, b) + (mm_nt(c, b_low) + mm_nt(c_low, b))
        cbt_ref[part] = jnp.transpose(cb_ref[...])
        pos, src = begin + iota(square, 0), begin + iota(square, 1)
        start = doc_start_of(pos, docs_ref, docs)
        gate_ref[...] = jnp.where((src <= pos) & (src >= start), 0.0, NEG)
        for pair in range(heads // 2):
            cols = slice(pair * LANES, (pair + 1) * LANES)
            xd = xd_ref[sl, cols]
            found = []
            for head in (2 * pair, 2 * pair + 1):
                gap = ramp_ref[sl, head : head + 1] - rampt_ref[part, head : head + 1, :]
                high, low = split2(jnp.exp2(gap + gate_ref[...]) * cb_ref[...])
                found.append(mm(high, xd) + mm(low, xd))
            y_ref[sl, cols] = jnp.where(lane < HEAD_DIM, found[0], found[1])


def within(meta, doc_starts, xd, ramp, rampt, smalls, lows, rim_own, rim_recv, taps, heads):
    total, width = xd.shape
    rows, states2 = total // 2, lows[0].shape[1]
    vm = pl.BlockSpec(memory_space=pltpu.VMEM)
    return pl.pallas_call(
        functools.partial(within_kernel, doc_starts.shape[0], heads),
        grid_spec=pltpu.PrefetchScalarGridSpec(
            num_scalar_prefetch=2,
            grid=(),
            in_specs=[vm] * 14,
            out_specs=[vm] * 2,
            scratch_shapes=[
                pltpu.VMEM((rows, rows), F32),
                pltpu.VMEM((rows, rows), F32),
                pltpu.VMEM((total + 8, states2), F32),
                pltpu.VMEM((total, states2), BF),
                pltpu.VMEM((total, states2), BF),
            ],
        ),
        out_shape=[
            jax.ShapeDtypeStruct((total, width), F32),
            jax.ShapeDtypeStruct((2, rows, rows), F32),
        ],
        compiler_params=params(),
        cost_estimate=cost(6e9, 4e6),
        name="within",
    )(meta, doc_starts, xd, ramp, rampt, *smalls, *lows, rim_own, rim_recv, taps)


def chain_kernel(heads, reverse, recv_ref, keep_ref, out_ref):
    chips = recv_ref.shape[0]
    width = out_ref.shape[2]
    state = jnp.zeros(out_ref.shape[1:], F32)
    wide = spread(heads, width)
    for step in range(chips):
        i = chips - 1 - step if reverse else step
        out_ref[i] = state.astype(BF)
        if step < chips - 1:
            factor = mm(keep_ref[i, :, width:], wide)
            factor = factor[0:1] + factor[1:2] + factor[2:3]
            state = state * factor + recv_ref[i, :, :width].astype(F32)


def chain(recv, keeps, heads, width, reverse):
    chips, piece = recv.shape[0], recv.shape[1]
    return pl.pallas_call(
        functools.partial(chain_kernel, heads, reverse),
        out_shape=jax.ShapeDtypeStruct((chips, piece, width), BF),
        compiler_params=params(16),
        cost_estimate=cost(1e8, 1e6),
        name="chain",
    )(recv, keeps)


def out_kernel(
    heads, meta_ref, y_ref, state_ref, loc_ref, bact_ref, epk_ref, keep_ref, go_ref, go_recv_ref,
    gain_ref, mix_own_ref, mix_send_ref, dy_ref, edy_ref, dot_ref, both_ref, late_ref, send_ref,
    go_all_ref, mix_ref,
):
    k = meta_ref[0]
    total, width = y_ref.shape
    rows = total // 2
    states = bact_ref.shape[1] // 2
    mine = pl.multiple_of(k * rows, rows)
    other = pl.multiple_of((1 - k) * rows, rows)
    go_all_ref[pl.ds(mine, rows), :] = go_ref[...]
    go_all_ref[pl.ds(other, rows), :] = go_recv_ref[...]
    state = state_ref[...]
    keep0 = keep_row(keep_ref[0], heads, width)[0:1, :]
    both_ref[0] = state
    middle = state.astype(F32) * keep0 + loc_ref[0]
    both_ref[1] = middle.astype(BF)
    both_ref[2] = (middle * keep_row(keep_ref[1], heads, width)[0:1, :] + loc_ref[1]).astype(BF)
    wide = spread(heads, width)
    gather = gather_heads(width)
    tile = 256
    per = rows // tile

    def one(step, _):
        at = pl.multiple_of(step * tile, tile)
        sl = pl.ds(at, tile)
        enter = mm(epk_ref[sl, :], wide)
        carried = mm(bact_ref[sl, states:], both_ref[step // per])
        y = y_ref[sl, :] + carried * enter
        u = go_all_ref[sl, :].astype(F32) * gain_ref[...]
        mean = over_heads(y * y, gather) * (1.0 / HEAD_DIM)
        along = over_heads(u * y, gather)
        scale = lax.rsqrt(mean + epsilon)
        cube = scale * scale * scale
        wide_scale = mm(packed(scale), wide)
        wide_back = mm(packed(cube * along * (1.0 / HEAD_DIM)), wide)
        mix_ref[sl, :] = (y * wide_scale * gain_ref[...]).astype(BF)
        dy = u * wide_scale - y * wide_back
        hi, lo = split2(dy)
        for pair in range(width // LANES):
            cols = slice(pair * LANES, (pair + 1) * LANES)
            dy_ref[sl, 2 * pair * LANES : (2 * pair + 1) * LANES] = hi[:, cols]
            dy_ref[sl, (2 * pair + 1) * LANES : (2 * pair + 2) * LANES] = lo[:, cols]
        edy_ref[sl, :] = (dy * enter).astype(BF)
        dot_ref[sl, :] = epsilon * cube * along
        return 0

    lax.fori_loop(0, total // tile, one, 0)
    mix_own_ref[...] = mix_ref[pl.ds(mine, rows), :]
    mix_send_ref[...] = mix_ref[pl.ds(other, rows), :]
    late = mm_tn(bact_ref[rows:, states:], edy_ref[rows:, :])
    late_ref[...] = late
    back = late * keep0 + mm_tn(bact_ref[:rows, states:], edy_ref[:rows, :])
    chips, piece = send_ref.shape[0], send_ref.shape[1]
    for i in range(chips):
        send_ref[i] = back[i * piece : (i + 1) * piece, :].astype(BF)


def outputs_of(meta, y, state, loc, bact, epk, keep, grad_out, go_recv, gain, heads, chips):
    total, width = y.shape
    rows, states = total // 2, bact.shape[1] // 2
    whole = lambda shape: pl.BlockSpec(shape, lambda i, m: (0,) * len(shape))
    half = lambda count: pl.BlockSpec((count, width), lambda i, m: (0, m[0]))
    outs = [
        jax.ShapeDtypeStruct((rows, width), BF),
        jax.ShapeDtypeStruct((rows, width), BF),
        jax.ShapeDtypeStruct((total, 2 * width), BF),
        jax.ShapeDtypeStruct((total, width), BF),
        jax.ShapeDtypeStruct((total, LANES), F32),
        jax.ShapeDtypeStruct((3, states, width), BF),
        jax.ShapeDtypeStruct((states, width), F32),
        jax.ShapeDtypeStruct((chips, states // chips, width), BF),
    ]
    return pl.pallas_call(
        functools.partial(out_kernel, heads),
        grid_spec=pltpu.PrefetchScalarGridSpec(
            num_scalar_prefetch=1,
            grid=(1,),
            in_specs=[
                whole(y.shape), whole(state.shape), whole(loc.shape), whole(bact.shape),
                whole(epk.shape), whole(keep.shape), half(rows), whole(go_recv.shape), half(1),
            ],
            out_specs=[whole(o.shape) for o in outs],
            scratch_shapes=[pltpu.VMEM((total, width), BF), pltpu.VMEM((total, width), BF)],
        ),
        out_shape=outs,
        compiler_params=params(),
        cost_estimate=cost(4e9, 4e6),
        name="outputs_of",
    )(meta, y, state, loc, bact, epk, keep, grad_out, go_recv, gain)


def within_back_kernel(
    docs, heads, meta_ref, docs_ref, dy_ref, edy_ref, both_ref, xd_ref, bact_ref, ramp_ref,
    rampt_ref, cbt_ref, act_ref, slope_ref, near_ref, q_ref, dbc_ref, gate_ref, sum_ref,
):
    gather = gather_heads(xd_ref.shape[1])
    chip = meta_ref[2]
    total, width = xd_ref.shape
    rows = total // 2
    states = bact_ref.shape[1] // 2
    square = (rows, rows)
    lane = iota((rows, LANES), 1)
    for part in range(2):
        sl = slice(part * rows, (part + 1) * rows)
        begin = chip * total + part * rows
        b, c = bact_ref[sl, :states], bact_ref[sl, states:]
        src, pos = begin + iota(square, 0), begin + iota(square, 1)
        start = doc_start_of(pos, docs_ref, docs)
        gate_ref[...] = jnp.where((src <= pos) & (src >= start), 0.0, NEG)
        sum_ref[...] = jnp.zeros(square, F32)
        q = jnp.zeros((rows, LANES), F32)
        for pair in range(heads // 2):
            cols = slice(pair * LANES, (pair + 1) * LANES)
            xd = xd_ref[sl, cols]
            dy_both = dy_ref[sl, 2 * pair * LANES : (2 * pair + 2) * LANES]
            dy = dy_both[:, :LANES]
            found = []
            for side, head in enumerate((2 * pair, 2 * pair + 1)):
                keep_side = (lane < HEAD_DIM) if side == 0 else (lane >= HEAD_DIM)
                only = jnp.where(keep_side, xd.astype(F32), 0.0).astype(BF)
                only = jnp.concatenate([only, only], axis=1)
                gap = rampt_ref[part, head : head + 1, :] - ramp_ref[sl, head : head + 1]
                decay = jnp.exp2(gap + gate_ref[...])
                found.append(mm((decay * cbt_ref[part]).astype(BF), dy))
                sum_ref[...] += mm_nt(only, dy_both) * decay
            dxd = jnp.where(lane < HEAD_DIM, found[0], found[1])
            near_ref[sl, cols] = (dxd * slope_ref[sl, cols].astype(F32)).astype(BF)
            q = q + mm((dxd * act_ref[sl, cols].astype(F32)).astype(BF), gather[cols, :])
        q_ref[sl, :] = q
        grad, low = split2(sum_ref[...])
        dbc_ref[sl, :states] = mm(grad, c) + mm(low, c)
        dbc_ref[sl, states:] = mm_tn(grad, b) + mm_tn(low, b) + mm_nt(edy_ref[sl, :], both_ref[part])


def within_back(meta, doc_starts, dy, edy, both, xd, bact, ramp, rampt, cbt, act, slope, heads):
    total, width = xd.shape
    rows = total // 2
    vm = pl.BlockSpec(memory_space=pltpu.VMEM)
    return pl.pallas_call(
        functools.partial(within_back_kernel, doc_starts.shape[0], heads),
        grid_spec=pltpu.PrefetchScalarGridSpec(
            num_scalar_prefetch=2,
            grid=(),
            in_specs=[vm] * 10,
            out_specs=[vm] * 3,
            scratch_shapes=[pltpu.VMEM((rows, rows), F32)] * 2,
        ),
        out_shape=[
            jax.ShapeDtypeStruct((total, width), BF),
            jax.ShapeDtypeStruct((total, LANES), F32),
            jax.ShapeDtypeStruct((total, bact.shape[1]), F32),
        ],
        compiler_params=params(),
        cost_estimate=cost(1e10, 6e6),
        name="within_back",
    )(meta, doc_starts, dy, edy, both, xd, bact, ramp, rampt, cbt, act, slope)


def slopes_kernel(pre_ref, dpk_ref, wpk_ref, act_ref, far_ref, wx_ref, slope_ref, reach_ref):
    total, width = pre_ref.shape
    wide = spread(width // HEAD_DIM, width)
    tile = total // 2
    for at in range(0, total, tile):
        sl = slice(at, at + tile)
        for lane in range(0, width, LANES):
            ls = slice(lane, lane + LANES)
            w = mm(wpk_ref[sl, :], wide[:, ls])
            step = mm(dpk_ref[sl, :], wide[:, ls])
            act, slope = silu_parts(pre_ref[sl, ls])
            slope = slope * step
            act_ref[sl, ls] = act.astype(BF)
            far_ref[sl, ls] = (act * w).astype(BF)
            wx_ref[sl, ls] = (act * step * w).astype(BF)
            slope_ref[sl, ls] = slope.astype(BF)
            reach_ref[sl, ls] = (slope * w).astype(BF)


def slopes_of(pre, dpk, wpk):
    return pl.pallas_call(
        slopes_kernel,
        out_shape=[jax.ShapeDtypeStruct(pre.shape, BF)] * 5,
        compiler_params=params(),
        cost_estimate=cost(2e9, 4e6),
        name="slopes_of",
    )(pre, dpk, wpk)


def back_masks(docs_ref, docs, pos):
    return [jnp.where(pos >= doc_start_of(pos + j, docs_ref, docs), 1.0, 0.0) for j in range(1, 4)]


def conv_back(src_ref, taps, at, count, ls, masks):
    window = src_ref[pl.ds(at, count + 8), ls]
    value = window[:count] * taps[0:1, ls]
    for j in range(1, 4):
        value = value + window[j : j + count] * taps[j : j + 1, ls] * masks[j - 1]
    return value


def grads_kernel(
    docs, heads, meta_ref, docs_ref, adj_ref, late_ref, keep_ref, both_ref, b_ref, near_ref, far_ref,
    wx_ref, reach_ref, q_ref, dbc_ref, bpre_ref, delta_ref, sig_ref, dot_ref, prm_ref, taps_bc_ref,
    taps_ref, own_ref, other_ref, bc_own_ref, bc_other_ref, rim_ref, adj2_ref, gx_ref, gb_ref, all_ref,
    bc_all_ref,
):
    k, chip = meta_ref[0], meta_ref[2]
    total, width = near_ref.shape
    rows = total // 2
    states = b_ref.shape[1]
    states2 = 2 * states
    base = chip * total
    adj = adj_ref[...].astype(F32)
    early = adj * keep_row(keep_ref[1], heads, width)[0:1, :] + late_ref[...]
    adj2_ref[0] = early.astype(BF)
    adj2_ref[1] = adj_ref[...]
    gather = gather_heads(width)
    ends = [
        over_heads(
            jnp.sum(a * both_ref[i].astype(F32), axis=0, keepdims=True) + jnp.zeros((8, width), F32),
            gather,
        )
        for i, a in ((1, early), (2, adj))
    ]
    for ref, lanes in ((gx_ref, width), (gb_ref, states2)):
        ref[0:8, :] = jnp.zeros((8, lanes), F32)
        ref[total + 8 :, :] = jnp.zeros((8, lanes), F32)
    square = (rows, rows)
    upper = jnp.where(iota(square, 0) <= iota(square, 1), 1.0, 0.0).astype(BF)
    rate = prm_ref[1:2, :]
    row = iota((rows, LANES), 0)
    for part in range(2):
        sl = slice(part * rows, (part + 1) * rows)
        inside = slice(8 + part * rows, 8 + (part + 1) * rows)
        q = q_ref[sl, :]
        for lane in range(0, width, LANES):
            ls = slice(lane, lane + LANES)
            back = mm(b_ref[sl, :], adj2_ref[part, :, ls])
            gx_ref[inside, ls] = near_ref[sl, ls].astype(F32) + back * reach_ref[sl, ls].astype(F32)
            q = q + mm((back * far_ref[sl, ls].astype(F32)).astype(BF), gather[ls, :])
        ramp_grad = dot_ref[sl, :] - delta_ref[sl, :] * q
        ramp_grad = ramp_grad + jnp.where(row == rows - 1, ends[part][0:1, :], 0.0)
        hi, lo = split2(ramp_grad)
        later = mm(upper, hi) + mm(upper, lo)
        bc_all_ref[sl, states2:] = (q - rate * later) * sig_ref[sl, :]
        back = mm_nt(wx_ref[sl, :], adj2_ref[part])
        for lane, grad in ((0, dbc_ref[sl, :states] + back), (states, dbc_ref[sl, states:])):
            ls = slice(lane, lane + states)
            _, slope = silu_parts(bpre_ref[sl, ls])
            gb_ref[inside, ls] = grad * slope
    tile = 64

    def back(step, _):
        at = pl.multiple_of(step * tile, tile)
        begin = pl.multiple_of(at + 8, 8)
        masks = back_masks(docs_ref, docs, base + at + iota((tile, LANES), 0))
        for lane in range(0, width, LANES):
            ls = slice(lane, lane + LANES)
            all_ref[pl.ds(at, tile), ls] = conv_back(gx_ref, taps_ref, begin, tile, ls, masks).astype(BF)
        for lane in range(0, states2, LANES):
            ls = slice(lane, lane + LANES)
            bc_all_ref[pl.ds(at, tile), ls] = conv_back(gb_ref, taps_bc_ref, begin, tile, ls, masks)
        return 0

    lax.fori_loop(0, total // tile, back, 0)
    pad = jnp.zeros((8, LANES), F32)
    masks = back_masks(docs_ref, docs, base - 8 + iota((8, LANES), 0))
    for src, taps, first, lanes in ((gx_ref, taps_ref, 0, width), (gb_ref, taps_bc_ref, width, states2)):
        for lane in range(0, lanes, LANES):
            value = conv_back(src, taps, 0, 8, slice(lane, lane + LANES), masks)
            value = jnp.concatenate([pad, value], axis=0)
            rim_ref[:, first + lane : first + lane + LANES] = value.astype(BF)
    mine = pl.ds(pl.multiple_of(k * rows, rows), rows)
    other = pl.ds(pl.multiple_of((1 - k) * rows, rows), rows)
    own_ref[...] = all_ref[mine, :]
    other_ref[...] = all_ref[other, :]
    bc_own_ref[...] = bc_all_ref[mine, :]
    bc_other_ref[...] = bc_all_ref[other, :]


def grads_of(
    meta, doc_starts, adj, late, keep, both, bact, near, far, wx, reach, q, dbc, bpre, delta, sig, dots,
    prm, taps_bc, taps, heads,
):
    total, width = near.shape
    rows, states2 = total // 2, bact.shape[1]
    states = states2 // 2
    whole = lambda shape: pl.BlockSpec(shape, lambda i, m, d: (0,) * len(shape))
    half = pl.BlockSpec((taps.shape[0], width), lambda i, m, d: (0, m[0]))
    first = pl.BlockSpec((total, states), lambda i, m, d: (0, 0))
    ins = [near, far, wx, reach, q, dbc, bpre, delta, sig, dots, prm, taps_bc]
    outs = [
        jax.ShapeDtypeStruct((rows, width), BF),
        jax.ShapeDtypeStruct((rows, width), BF),
        jax.ShapeDtypeStruct((rows, states2 + LANES), F32),
        jax.ShapeDtypeStruct((rows, states2 + LANES), F32),
        jax.ShapeDtypeStruct((16, width + states2), BF),
    ]
    return pl.pallas_call(
        functools.partial(grads_kernel, doc_starts.shape[0], heads),
        grid_spec=pltpu.PrefetchScalarGridSpec(
            num_scalar_prefetch=2,
            grid=(1,),
            in_specs=[whole(a.shape) for a in (adj, late, keep, both)]
            + [first]
            + [whole(a.shape) for a in ins]
            + [half],
            out_specs=[whole(o.shape) for o in outs],
            scratch_shapes=[
                pltpu.VMEM((2, states, width), BF),
                pltpu.VMEM((total + 16, width), F32),
                pltpu.VMEM((total + 16, states2), F32),
                pltpu.VMEM((total, width), BF),
                pltpu.VMEM((total, states2 + LANES), F32),
            ],
        ),
        out_shape=outs,
        compiler_params=params(),
        cost_estimate=cost(4e9, 8e6),
        name="grads_of",
    )(meta, doc_starts, adj, late, keep, both, bact, *ins, taps)


def join_kernel(heads, meta_ref, own_ref, recv_ref, out_ref, send_ref):
    k = meta_ref[0]
    states2 = own_ref.shape[1] - LANES
    total = own_ref[:, :states2] + recv_ref[:, :states2]
    out_ref[:, :states2] = total
    send_ref[:, :states2] = total.astype(BF)
    shape = (LANES, LANES)
    row, col = iota(shape, 0), iota(shape, 1)
    mine = jnp.where((row < heads) & (col == row + k * heads), 1.0, 0.0).astype(BF)
    other = jnp.where((row < heads) & (col == row + (1 - k) * heads), 1.0, 0.0).astype(BF)
    steps = mm(own_ref[:, states2:].astype(BF), mine) + mm(recv_ref[:, states2:].astype(BF), other)
    out_ref[:, states2:] = steps
    send_ref[:, states2:] = steps.astype(BF)


def join(meta, own, recv, heads):
    vm = pl.BlockSpec(memory_space=pltpu.VMEM)
    return pl.pallas_call(
        functools.partial(join_kernel, heads),
        grid_spec=pltpu.PrefetchScalarGridSpec(
            num_scalar_prefetch=1, grid=(), in_specs=[vm] * 2, out_specs=[vm] * 2
        ),
        out_shape=[jax.ShapeDtypeStruct(own.shape, F32), jax.ShapeDtypeStruct(own.shape, BF)],
        compiler_params=params(16),
        cost_estimate=cost(1e8, 1e6),
        name="join",
    )(meta, own, recv)


def half_kernel(meta_ref, *refs):
    *before, mine_ref, other_ref, rim_ref, w_mine_ref, w_other_ref, out_ref = refs
    rows, width = mine_ref.shape

    def whole(ref, rim):
        tail = ref[rows - 16 :, :].astype(F32) + rim.astype(F32)
        return jnp.concatenate([ref[: rows - 16, :], tail.astype(BF)], axis=0)

    mine = whole(mine_ref, rim_ref[:16, :width])
    other = whole(other_ref, rim_ref[16:, :width])
    total = mm_nt(mine, w_mine_ref[...]) + mm_nt(other, w_other_ref[...])
    for ref in before:
        total = total + ref[...]
    out_ref[...] = total


def first_half(blocks, before, mine, other, rim, x_weight, tile):
    rows, width = mine.shape
    depth = x_weight.shape[0]
    whole = lambda shape: pl.BlockSpec(shape, lambda i, m: (0, 0))
    part = pl.BlockSpec((rows, tile), lambda i, m: (0, i))
    parts = [] if before is None else [before]
    return pl.pallas_call(
        half_kernel,
        grid_spec=pltpu.PrefetchScalarGridSpec(
            num_scalar_prefetch=1,
            grid=(depth // tile,),
            in_specs=[part] * len(parts)
            + [
                whole(mine.shape), whole(other.shape), whole(rim.shape),
                pl.BlockSpec((tile, width), lambda i, m: (i, m[0])),
                pl.BlockSpec((tile, width), lambda i, m: (i, m[1])),
            ],
            out_specs=part,
        ),
        out_shape=jax.ShapeDtypeStruct((rows, depth), F32),
        compiler_params=params(16),
        cost_estimate=cost(2e9, 4e6),
        name="half_sum",
    )(blocks, *parts, mine, other, rim, x_weight, x_weight)


def last_kernel(
    heads, rim_width, side_ref, part_ref, rim_ref, rim0_ref, bc_own_ref, bc_recv_ref, bcw_ref, dtw_ref,
    out_ref, bc_ref, dt_ref,
):
    rows = part_ref.shape[0]
    states2 = bcw_ref.shape[1]
    all_heads = dtw_ref.shape[0]

    @pl.when(pl.program_id(0) == 0)
    def _():
        bc = bc_own_ref[:, :states2] + bc_recv_ref[:, :states2].astype(F32)
        rim = rim_ref[:, rim_width:].astype(F32) + rim0_ref[:, rim_width:].astype(F32)
        extra = rim[:16] + rim[16:]
        for at, value in ((0, bc[: rows - 16, :]), (rows - 16, bc[rows - 16 :, :] + extra)):
            high, low = split2(value)
            bc_ref[at : at + value.shape[0], :states2] = high
            bc_ref[at : at + value.shape[0], states2:] = low
        shape = (LANES, all_heads)
        row, col = iota(shape, 0), iota(shape, 1)
        x = side_ref[0]
        here = jnp.where((row < heads) & (col == row + x * heads), 1.0, 0.0).astype(BF)
        there = jnp.where((row < heads) & (col == row + (1 - x) * heads), 1.0, 0.0).astype(BF)
        dt = mm(bc_own_ref[:, states2:].astype(BF), here) + mm(bc_recv_ref[:, states2:], there)
        dt_ref[...] = dt.astype(BF)

    bcw = bcw_ref[...]
    total = part_ref[...] + mm_nt(bc_ref[...], jnp.concatenate([bcw, bcw], axis=1))
    out_ref[...] = (total + mm(dt_ref[...], dtw_ref[...])).astype(BF)


def last_half(side, part, rim, rim0, bc_own, bc_recv, bc_weight, dt_rows, tile):
    rows, depth = part.shape
    states2, all_heads = bc_weight.shape[1], dt_rows.shape[0]
    whole = lambda a: pl.BlockSpec(a.shape, lambda i, m: (0, 0))
    return pl.pallas_call(
        functools.partial(last_kernel, all_heads // 2, rim.shape[1] - states2),
        grid_spec=pltpu.PrefetchScalarGridSpec(
            num_scalar_prefetch=1,
            grid=(depth // tile,),
            in_specs=[
                pl.BlockSpec((rows, tile), lambda i, m: (0, i)),
                whole(rim), whole(rim0), whole(bc_own), whole(bc_recv),
                pl.BlockSpec((tile, states2), lambda i, m: (i, 0)),
                pl.BlockSpec((all_heads, tile), lambda i, m: (0, i)),
            ],
            out_specs=pl.BlockSpec((rows, tile), lambda i, m: (0, i)),
            scratch_shapes=[pltpu.VMEM((rows, 2 * states2), BF), pltpu.VMEM((rows, all_heads), BF)],
        ),
        out_shape=jax.ShapeDtypeStruct((rows, depth), BF),
        compiler_params=params(16),
        cost_estimate=cost(5e8, 2e6),
        name="last_half",
    )(side, part, rim, rim0, bc_own, bc_recv, bc_weight, dt_rows)


def by_chips(
    tokens, x_weight, bc_weight, dt_weight, conv_inner, conv_shared, dt_bias, decay_rate, norm_gain,
    doc_starts, grad_out,
):
    blocks = lax.axis_size("ctx")
    chips = blocks // 2
    rows = tokens.shape[0]
    all_heads = dt_weight.shape[1]
    heads = decay_rate.shape[0] // 2
    width = heads * HEAD_DIM
    place = lax.axis_index("ctx").astype(jnp.int32)
    x = lax.axis_index("fsdp").astype(jnp.int32)
    k = place % 2
    meta = jnp.stack([k, x, place // 2])

    core = [(i, i ^ 1) for i in range(blocks)]
    pair = [(0, 1), (1, 0)]
    cross = [(2 * i + j, 2 * (i ^ 1) + (1 - j)) for i in range(blocks) for j in range(2)]
    by_core = lambda a: lax.ppermute(a, "ctx", core)
    by_x = lambda a: lax.ppermute(a, "fsdp", pair)
    by_both = lambda a: lax.ppermute(a, ("ctx", "fsdp"), cross)
    groups = [[2 * i for i in range(chips)], [2 * i + 1 for i in range(chips)]]
    exchange = lambda a: lax.all_to_all(a, "ctx", 0, 0, axis_index_groups=groups)

    def column_block(side, half):
        return (side * 2 + half)[None]

    tail = tokens[rows - 16 :]
    ra = lax.ppermute(tail, "ctx", [(2 * i - 1, 2 * i) for i in range(1, chips)])
    rb = lax.ppermute(tail, "ctx", [(2 * i - 1, 2 * i + 1) for i in range(1, chips)])

    dt_rows = dt_weight.T
    to_cross, small, low = lead_proj(
        column_block(1 - x, 1 - k), tokens, x_weight, bc_weight, dt_rows, width
    )
    from_cross = by_both(to_cross)
    small_x = by_x(small)
    to_x, to_core, mine, rim_own, rim_send = rest_proj(
        jnp.stack([(1 - x) * 2 + k, x * 2 + 1 - k, x * 2 + k]), tokens, x_weight, bc_weight, ra, rb, width
    )
    from_x = by_x(to_x)
    from_core = by_core(to_core)
    rim_recv = by_x(rim_send)
    small_core = by_core(small)
    small_cross = by_core(small_x)
    low_x = by_x(low)
    lows = (low, low_x, by_core(low), by_core(low_x))
    go_recv = by_core(lax.dynamic_slice(grad_out, (jnp.int32(0), (1 - k) * width), (rows, width)))

    prm = jnp.stack([lax.dynamic_slice(v, (k * heads,), (heads,)) for v in (dt_bias, decay_rate)])
    prm = jnp.pad(prm, ((0, 6), (0, LANES - heads)))
    bact, bpre, delta, ramp, sig, rampt, dpk, wpk, epk, keep = shared_maps(
        meta, doc_starts, small, small_x, small_core, small_cross, rim_own, rim_recv, conv_shared,
        prm, heads, all_heads,
    )
    pre, xd, loc, send = inner_maps(
        meta, doc_starts, mine, from_x, from_core, from_cross, rim_own, rim_recv, conv_inner, bact,
        dpk, wpk, keep, heads, chips,
    )
    keeps = exchange(send)
    y, cbt = within(
        meta, doc_starts, xd, ramp, rampt, (small, small_x, small_core, small_cross), lows, rim_own, rim_recv,
        conv_shared, heads,
    )
    states = exchange(chain(keeps, keeps, heads, width, False))
    state = states.reshape(STATE, width)
    mix_own, mix_send, dy, edy, dots, both, late, back = outputs_of(
        meta, y, state, loc, bact, epk, keep, grad_out, go_recv, norm_gain[None, :], heads, chips
    )
    act, far, wx, slope, reach = slopes_of(pre, dpk, wpk)
    backs = exchange(back)
    near, q, dbc = within_back(
        meta, doc_starts, dy, edy, both, xd, bact, ramp, rampt, cbt, act, slope, heads
    )
    mix_recv = by_core(mix_send)
    mixed = jnp.where(
        k == 0,
        jnp.concatenate([mix_own, mix_recv], axis=1),
        jnp.concatenate([mix_recv, mix_own], axis=1),
    )
    adj = exchange(chain(backs, keeps, heads, width, True)).reshape(STATE, width)
    g_mine, g_other, bc_mine, bc_other, rim = grads_of(
        meta, doc_starts, adj, late, keep, both, bact, near, far, wx, reach, q, dbc, bpre, delta, sig,
        dots, prm, conv_shared, conv_inner, heads,
    )
    g_x = by_x(g_mine)
    g_cross = by_both(g_other)
    g_core = by_core(g_other)
    rim, g_core = lax.optimization_barrier((rim, g_core))
    rims = jnp.concatenate([rim, by_core(rim)], axis=0)
    back_perm = [(2 * i + 1, 2 * i - 1) for i in range(1, chips)]
    rim0 = lax.ppermute(rims, "ctx", back_perm)
    rim1 = lax.ppermute(
        rims, ("ctx", "fsdp"), [(2 * a + j, 2 * b + (1 - j)) for a, b in back_perm for j in range(2)]
    )
    bc_chip, bc_send = join(meta, bc_mine, by_core(bc_other), heads)
    bc_recv = by_x(bc_send)
    part = first_half(
        jnp.stack([x * 2 + k, x * 2 + 1 - k]), None, g_mine, g_core, rim0, x_weight, 640
    )
    part = first_half(
        jnp.stack([(1 - x) * 2 + k, (1 - x) * 2 + 1 - k]), part, g_x, g_cross, rim1, x_weight, 640
    )
    grad_tokens = last_half(x[None], part, rim1, rim0, bc_chip, bc_recv, bc_weight, dt_rows, width)
    return (mixed, grad_tokens)


def splits_by_chip(mesh):
    return mesh.shape["fsdp"] == 2 and mesh.shape["ctx"] == 16


def solution(mesh):
    in_specs = (
        P("ctx", "fsdp"),
        P("fsdp", None),
        P("fsdp", None),
        P("fsdp", None),
        P(None, "fsdp"),
        P(),
        P("fsdp"),
        P("fsdp"),
        P("fsdp"),
        P(),
        P("ctx", "fsdp"),
    )
    body = by_chips if splits_by_chip(mesh) else on_device
    out_specs = (P("ctx", "fsdp"), P("ctx", "fsdp"))
    return jax.shard_map(
        body, mesh=mesh, in_specs=in_specs, out_specs=out_specs, check_vma=False
    )
```

```python
import functools

import jax
import jax.numpy as jnp
from jax import lax
from jax.experimental import pallas as pl
from jax.experimental.pallas import tpu as pltpu
from jax.sharding import PartitionSpec as P

HEAD_DIM = 64
STATE = 128


exact = lax.Precision.HIGHEST
epsilon = 1e-05


def from_behind(value, axis, steps):
    count = lax.axis_size(axis)
    leading, last = (max(0, -steps), min(count, count - steps))
    return lax.ppermute(value, axis, [(source, source + steps) for source in range(leading, last)])


def prefix(part, axis, combine, identity, reverse):
    count = lax.axis_size(axis)
    place = lax.axis_index(axis)
    ahead = count - 1 - place if reverse else place
    gathered = jax.tree.map(lambda a: lax.all_gather(a, axis), part)
    state = jax.tree.map(lambda a, e: jnp.zeros_like(a) + jnp.asarray(e, a.dtype), part, identity)

    def one(step, state):
        source = count - 1 - step if reverse else step
        return combine(
            state, jax.tree.map(lambda a: lax.dynamic_index_in_dim(a, source, 0, False), gathered)
        )

    return lax.fori_loop(0, ahead, one, state)


def doc_index(positions, doc_starts):
    hits = (doc_starts[None, :] <= positions[:, None]).astype(jnp.int32)
    return jnp.sum(hits, axis=1) - 1


def causal_conv(padded, docs_ext, taps):
    count = padded.shape[0] - 3
    docs_now = docs_ext[3:]
    total = jnp.zeros((count, padded.shape[1]), jnp.float32)
    for offset in range(4):
        rows = padded[3 - offset : 3 - offset + count]
        same = (docs_ext[3 - offset : 3 - offset + count] == docs_now).astype(jnp.float32)
        total = total + taps[offset][None, :] * rows * same[:, None]
    return total


def block_out(x_act, b_act, c_act, delta, docs, doc_before, state_in, decay_rate):
    count = delta.shape[0]
    places = jnp.arange(count, dtype=jnp.int32)
    lower = places[:, None] >= places[None, :]
    ramp = -jnp.dot(lower.astype(jnp.float32), delta, precision=exact) * decay_rate[None, :]
    same = jnp.logical_and(docs[:, None] == docs[None, :], lower)
    gap = ramp[:, None, :] - ramp[None, :, :]
    decay = jnp.exp(jnp.where(same[:, :, None], gap, 0.0)) * same.astype(jnp.float32)[:, :, None]
    scores = jnp.dot(c_act, b_act.T, precision=exact)
    mixing = decay * scores[:, :, None] * delta[None, :, :]
    inner = jnp.einsum("tsh,shp->thp", mixing, x_act, precision=exact)
    carried = (docs == doc_before).astype(jnp.float32)
    enter = jnp.exp(ramp) * carried[:, None]
    from_state = jnp.einsum("tn,hpn->thp", c_act, state_in, precision=exact) * enter[:, :, None]
    last_doc = docs[count - 1]
    tail = (
        jnp.exp(ramp[count - 1][None, :] - ramp)
        * (docs == last_doc).astype(jnp.float32)[:, None]
        * delta
    )
    weighted = tail[:, :, None] * x_act
    state_loc = jnp.einsum("shp,sn->hpn", weighted, b_act, precision=exact)
    keep = jnp.exp(ramp[count - 1]) * (last_doc == doc_before).astype(jnp.float32)
    return (inner + from_state, state_loc, keep)


def head_norm(values, norm_gain):
    scale = lax.rsqrt(jnp.mean(values * values, axis=-1, keepdims=True) + epsilon)
    normed = values * scale
    return normed.reshape(values.shape[0], values.shape[1] * values.shape[2]) * norm_gain[None, :]


def link(earlier, later):
    return (earlier[0] * later[0], later[0][:, None, None] * earlier[1] + later[1])


def on_device(
    tokens,
    x_weight,
    bc_weight,
    dt_weight,
    conv_inner,
    conv_shared,
    dt_bias,
    decay_rate,
    norm_gain,
    doc_starts,
    grad_out,
):
    count = tokens.shape[0]
    heads_here = decay_rate.shape[0]
    features = lax.all_gather(tokens, "fsdp", axis=1, tiled=True)
    x_cols, dt_cols = (
        lax.all_to_all(x_weight, "fsdp", split_axis=1, concat_axis=0, tiled=True),
        lax.all_to_all(dt_weight, "fsdp", split_axis=1, concat_axis=0, tiled=True),
    )
    bc_all = lax.all_gather(bc_weight, "fsdp", axis=0, tiled=True)
    x_proj = jnp.dot(features, x_cols, preferred_element_type=jnp.float32).astype(jnp.bfloat16)
    bc_proj = jnp.dot(features, bc_all, preferred_element_type=jnp.float32)
    dt_raw = jnp.dot(features, dt_cols, preferred_element_type=jnp.float32)
    x_wide = lax.optimization_barrier(x_proj).astype(jnp.float32)
    rim_x, rim_bc = from_behind((x_wide[count - 3 :], bc_proj[count - 3 :]), "ctx", 1)
    x_ext = jnp.concatenate([rim_x, x_wide], axis=0)
    bc_ext = jnp.concatenate([rim_bc, bc_proj], axis=0)
    first = lax.axis_index("ctx") * count
    positions = first - 3 + jnp.arange(count + 3, dtype=jnp.int32)
    docs_ext = doc_index(positions, doc_starts)
    docs = docs_ext[3:]
    doc_before = docs_ext[2]

    def layer(x_in, bc_in, dt_in, state_in):
        x_act = jax.nn.silu(causal_conv(x_in, docs_ext, conv_inner))
        bc_act = jax.nn.silu(causal_conv(bc_in, docs_ext, conv_shared))
        delta = jax.nn.softplus(dt_in + dt_bias[None, :])
        values, state_loc, keep = block_out(
            x_act.reshape(count, heads_here, HEAD_DIM),
            bc_act[:, :STATE],
            bc_act[:, STATE:],
            delta,
            docs,
            doc_before,
            state_in,
            decay_rate,
        )
        return (head_norm(values, norm_gain), state_loc, keep)

    blank = jnp.zeros((heads_here, HEAD_DIM, STATE), jnp.float32)
    unit = jnp.ones((heads_here,), jnp.float32)
    _, state_loc, keep = layer(x_ext, bc_ext, dt_raw, blank)
    state_in = prefix((keep, state_loc), "ctx", link, (unit, blank), False)[1]
    outputs, pull = jax.vjp(layer, x_ext, bc_ext, dt_raw, state_in)
    normed = outputs[0]
    grads_out = pull((grad_out.astype(jnp.float32), jnp.zeros_like(blank), jnp.zeros_like(unit)))
    adjoint = prefix((keep, grads_out[3]), "ctx", link, (unit, blank), True)[1]
    keep_grad = jnp.sum(adjoint * state_in, axis=(1, 2))
    grads_state = pull((jnp.zeros_like(normed), adjoint, keep_grad))
    grad_xe = grads_out[0] + grads_state[0]
    grad_bce = grads_out[1] + grads_state[1]
    grad_dt = grads_out[2] + grads_state[2]
    back_x, back_bc = from_behind((grad_xe[:3], grad_bce[:3]), "ctx", -1)
    grad_x = grad_xe[3:].at[count - 3 :].add(back_x)
    grad_bc = grad_bce[3:].at[count - 3 :].add(back_bc)
    grad_xb = grad_x.astype(jnp.bfloat16)
    grad_rows = lax.all_gather(grad_xb, "fsdp", axis=1, tiled=True)
    column = lax.axis_index("fsdp") * heads_here
    dt_wide = lax.dynamic_update_slice(
        jnp.zeros((count, dt_weight.shape[1]), jnp.float32), grad_dt, (jnp.int32(0), column)
    )
    bc_total, dt_total = lax.psum((grad_bc, dt_wide), "fsdp")
    grad_local = jnp.dot(grad_rows, x_weight.T, preferred_element_type=jnp.float32)
    grad_local = grad_local + jnp.dot(bc_total, bc_weight.T.astype(jnp.float32), precision=exact)
    grad_local = grad_local + jnp.dot(dt_total, dt_weight.T.astype(jnp.float32), precision=exact)
    grad_tokens = grad_local.astype(jnp.bfloat16)
    return (normed.astype(jnp.bfloat16), grad_tokens)


BF = jnp.bfloat16
F32 = jnp.float32
LOG2E = 1.4426950408889634
LANES = 128
NEG = -1e30


def params(mb=60, **kw):
    return pltpu.CompilerParams(vmem_limit_bytes=mb * 1024 * 1024, **kw)


def cost(flops, nbytes):
    return pl.CostEstimate(flops=int(flops), bytes_accessed=int(nbytes), transcendentals=0)


def mm(a, b):
    return jnp.dot(a, b, preferred_element_type=F32)


def mm_nt(a, b):
    return lax.dot_general(a, b, (((1,), (1,)), ((), ())), preferred_element_type=F32)


def mm_tn(a, b):
    return lax.dot_general(a, b, (((0,), (0,)), ((), ())), preferred_element_type=F32)


def split2(v):
    hi = v.astype(BF)
    return hi, (v - hi.astype(F32)).astype(BF)


def iota(shape, dim):
    return lax.broadcasted_iota(jnp.int32, shape, dim)


def doc_start_of(pos, docs_ref, count):
    start = jnp.zeros_like(pos)
    for i in range(count):
        start = jnp.where(docs_ref[i] <= pos, docs_ref[i], start)
    return start


def spread(heads, width):
    shape = (LANES, width)
    row, col = iota(shape, 0), iota(shape, 1)
    head = jnp.right_shift(col, 6)
    return jnp.where((row == head) | (row == head + 16), 1.0, 0.0).astype(BF)


def gather_heads(width):
    shape = (width, LANES)
    return jnp.where(jnp.right_shift(iota(shape, 0), 6) == iota(shape, 1), 1.0, 0.0).astype(BF)


def packed(v):
    hi = v.astype(BF).astype(F32)
    lo = v - hi
    lane = iota(v.shape, 1)
    return jnp.where(lane < 16, hi, pltpu.roll(lo, 16, 1)).astype(BF)


def over_heads(v, gather):
    hi, lo = split2(v)
    return mm(hi, gather) + mm(lo, gather)


def silu_parts(v):
    sig = 1.0 / (1.0 + jnp.exp(-v))
    return v * sig, sig * (1.0 + v * (1.0 - sig))


def fetch(src, dst, sem):
    copy = pltpu.make_async_copy(src, dst, sem)
    copy.start()
    return copy


def columns(w_ref, block, width):
    return w_ref.at[:, pl.ds(pl.multiple_of(block * width, LANES), width)]


def lead_kernel(
    meta_ref, tok_hbm, w_hbm, bcw_hbm, dtw_hbm, piece_ref, out_ref, low_ref, tok_ref, w_ref, bcw_ref,
    dtw_ref, sems,
):
    width = w_ref.shape[1]
    get_tok = fetch(tok_hbm, tok_ref, sems.at[0])
    get_w = fetch(columns(w_hbm, (1 - meta_ref[1]) * 2 + 1 - meta_ref[0], width), w_ref, sems.at[1])
    get_bcw = fetch(bcw_hbm, bcw_ref, sems.at[2])
    get_dtw = fetch(dtw_hbm, dtw_ref, sems.at[3])
    get_tok.wait()
    get_w.wait()
    piece_ref[...] = mm(tok_ref[...], w_ref[...]).astype(BF)
    get_bcw.wait()
    get_dtw.wait()
    states = bcw_ref.shape[1]
    heads = dtw_ref.shape[0]
    out_ref[:, :states], low_ref[...] = split2(mm(tok_ref[...], bcw_ref[...]))
    hi, lo = split2(mm_nt(tok_ref[...], dtw_ref[...]))
    shape = (heads, LANES)
    row, col = iota(shape, 0), iota(shape, 1)
    first = jnp.where(row == col, 1.0, 0.0).astype(BF)
    second = jnp.where(row + heads == col, 1.0, 0.0).astype(BF)
    out_ref[:, states:] = (mm(hi, first) + mm(lo, second)).astype(BF)


def lead_proj(block, tokens, x_weight, bc_weight, dt_rows, width):
    rows, depth = tokens.shape
    states = bc_weight.shape[1]
    hbm = pl.BlockSpec(memory_space=pl.ANY)
    vm = pl.BlockSpec(memory_space=pltpu.VMEM)
    return pl.pallas_call(
        lead_kernel,
        grid_spec=pltpu.PrefetchScalarGridSpec(
            num_scalar_prefetch=1,
            grid=(),
            in_specs=[hbm] * 4,
            out_specs=[vm] * 3,
            scratch_shapes=[
                pltpu.VMEM((rows, depth), BF),
                pltpu.VMEM((depth, width), BF),
                pltpu.VMEM((depth, states), BF),
                pltpu.VMEM(dt_rows.shape, BF),
                pltpu.SemaphoreType.DMA((4,)),
            ],
        ),
        out_shape=[
            jax.ShapeDtypeStruct((rows, width), BF),
            jax.ShapeDtypeStruct((rows, states + LANES), BF),
            jax.ShapeDtypeStruct((rows, states), BF),
        ],
        compiler_params=params(),
        cost_estimate=cost(2 * rows * depth * width, 3e6),
        name="lead_proj",
    )(block, tokens, x_weight, bc_weight, dt_rows)


def rest_kernel(
    meta_ref, tok_hbm, w_hbm, bcw_hbm, ra_hbm, rb_hbm, peer_ref, core_ref, mine_ref, own_ref, send_ref,
    tok_ref, w_ref, bcw_ref, ra_ref, rb_ref, sems,
):
    width = w_ref.shape[2]
    get_tok = fetch(tok_hbm, tok_ref, sems.at[0])
    k, x = meta_ref[0], meta_ref[1]
    blocks = ((1 - x) * 2 + k, x * 2 + 1 - k, x * 2 + k)
    get_w = [fetch(columns(w_hbm, b, width), w_ref.at[i], sems.at[1 + i]) for i, b in enumerate(blocks)]
    get_bcw = fetch(bcw_hbm, bcw_ref, sems.at[4])
    get_ra = fetch(ra_hbm, ra_ref, sems.at[5])
    get_rb = fetch(rb_hbm, rb_ref, sems.at[6])
    get_tok.wait()
    for i, ref in enumerate((peer_ref, core_ref, mine_ref)):
        get_w[i].wait()
        ref[...] = mm(tok_ref[...], w_ref[i]).astype(BF)
    get_bcw.wait()
    get_ra.wait()
    get_rb.wait()
    rim = ra_ref[...] + rb_ref[...]
    shared = mm(rim, bcw_ref[...]).astype(BF)
    own_ref[:, :width] = mm(rim, w_ref[2]).astype(BF)
    own_ref[:, width:] = shared
    send_ref[:, :width] = mm(rim, w_ref[0]).astype(BF)
    send_ref[:, width:] = shared


def rest_proj(blocks, tokens, x_weight, bc_weight, ra, rb, width):
    rows, depth = tokens.shape
    states = bc_weight.shape[1]
    hbm = pl.BlockSpec(memory_space=pl.ANY)
    vm = pl.BlockSpec(memory_space=pltpu.VMEM)
    piece = jax.ShapeDtypeStruct((rows, width), BF)
    rim = jax.ShapeDtypeStruct((ra.shape[0], width + states), BF)
    return pl.pallas_call(
        rest_kernel,
        grid_spec=pltpu.PrefetchScalarGridSpec(
            num_scalar_prefetch=1,
            grid=(),
            in_specs=[hbm] * 5,
            out_specs=[vm] * 5,
            scratch_shapes=[
                pltpu.VMEM((rows, depth), BF),
                pltpu.VMEM((3, depth, width), BF),
                pltpu.VMEM((depth, states), BF),
                pltpu.VMEM(ra.shape, BF),
                pltpu.VMEM(rb.shape, BF),
                pltpu.SemaphoreType.DMA((7,)),
            ],
        ),
        out_shape=[piece, piece, piece, rim, rim],
        compiler_params=params(),
        cost_estimate=cost(6 * rows * depth * width, 6e6),
        name="rest_proj",
    )(blocks, tokens, x_weight, bc_weight, ra, rb)


def conv_masks(docs_ref, count, base, rows, lanes):
    pos = base + iota((rows, lanes), 0)
    start = doc_start_of(pos, docs_ref, count)
    return [jnp.where(pos - k >= start, 1.0, 0.0) for k in range(1, 4)]


def shared_kernel(
    docs, heads, all_heads, meta_ref, docs_ref, own_ref, xr_ref, cr_ref, dr_ref, rim_own_ref,
    rim_recv_ref, taps_ref, prm_ref, bact_ref, bpre_ref, delta_ref, ramp_ref, sig_ref, rampt_ref,
    dpk_ref, wpk_ref, epk_ref, keep_ref, ext_ref,
):
    k, x, chip = meta_ref[0], meta_ref[1], meta_ref[2]
    rows = own_ref.shape[0]
    total = 2 * rows
    states2 = bact_ref.shape[1]
    base = chip * total
    mine = pl.multiple_of(8 + k * rows, 8)
    other = pl.multiple_of(8 + (1 - k) * rows, 8)
    width = rim_own_ref.shape[1] - states2
    rim = rim_own_ref[:, width:].astype(F32) + rim_recv_ref[:, width:].astype(F32)
    ext_ref[0:8, :] = rim[8:16, :]
    ext_ref[pl.ds(mine, rows), :] = own_ref[:, :states2].astype(F32) + xr_ref[:, :states2].astype(F32)
    ext_ref[pl.ds(other, rows), :] = cr_ref[:, :states2].astype(F32) + dr_ref[:, :states2].astype(F32)

    tile = 64

    def conv(step, _):
        at = pl.multiple_of(step * tile, tile)
        masks = conv_masks(docs_ref, docs, base + at, tile, LANES)
        for lane in range(0, states2, LANES):
            sl = slice(lane, lane + LANES)
            window = ext_ref[pl.ds(at, tile + 8), sl]
            value = window[8:] * taps_ref[0:1, sl]
            for j in range(1, 4):
                value = value + window[8 - j : 8 - j + tile] * taps_ref[j : j + 1, sl] * masks[j - 1]
            bpre_ref[pl.ds(at, tile), sl] = value
            bact_ref[pl.ds(at, tile), sl] = (value / (1.0 + jnp.exp(-value))).astype(BF)
        return 0

    lax.fori_loop(0, total // tile, conv, 0)

    shape = (LANES, LANES)
    row, col = iota(shape, 0), iota(shape, 1)
    first = x * (all_heads // 2) + k * heads
    wanted = (col < heads) & ((row == first + col) | (row == all_heads + first + col))
    select = jnp.where(wanted, 1.0, 0.0).astype(BF)
    square = (rows, rows)
    lower = jnp.where(iota(square, 0) >= iota(square, 1), 1.0, 0.0).astype(BF)
    bias, rate = prm_ref[0:1, :], prm_ref[1:2, :]

    def steps(part, ref_a, ref_b):
        at = pl.multiple_of(part * rows, rows)
        raw = mm(ref_a[:, states2:], select) + mm(ref_b[:, states2:], select) + bias
        delta = jnp.maximum(raw, 0.0) + jnp.log1p(jnp.exp(-jnp.abs(raw)))
        delta_ref[pl.ds(at, rows), :] = delta
        sig_ref[pl.ds(at, rows), :] = 1.0 / (1.0 + jnp.exp(-raw))
        dpk_ref[pl.ds(at, rows), :] = packed(delta)
        hi, rest = split2(delta)
        mid = rest
        low = (delta - hi.astype(F32) - mid.astype(F32)).astype(BF)
        ramp = -(mm(lower, hi) + mm(lower, mid) + mm(lower, low)) * (rate * LOG2E)
        ramp_ref[pl.ds(at, rows), :] = ramp
        rampt_ref[part] = jnp.transpose(ramp)[:16, :]
        begin = base + at
        end = begin + rows - 1
        pos = begin + iota((rows, LANES), 0)
        start = doc_start_of(pos, docs_ref, docs)
        last = doc_start_of(jnp.zeros((1, LANES), jnp.int32) + end, docs_ref, docs)
        final = ramp[rows - 1 : rows, :]
        epk_ref[pl.ds(at, rows), :] = packed(jnp.where(start < begin, jnp.exp2(ramp), 0.0))
        wpk_ref[pl.ds(at, rows), :] = packed(jnp.where(pos >= last, jnp.exp2(final - ramp), 0.0))
        keep_ref[part] = jnp.zeros((8, LANES), F32) + jnp.where(last < begin, jnp.exp2(final), 0.0)

    steps(k, own_ref, xr_ref)
    steps(1 - k, cr_ref, dr_ref)


def shared_maps(meta, doc_starts, own, xr, cr, dr, rim_own, rim_recv, taps, prm, heads, all_heads):
    rows = own.shape[0]
    total, states2 = 2 * rows, own.shape[1] - LANES
    compact = jax.ShapeDtypeStruct((total, LANES), F32)
    compact_b = jax.ShapeDtypeStruct((total, LANES), BF)
    vm = pl.BlockSpec(memory_space=pltpu.VMEM)
    return pl.pallas_call(
        functools.partial(shared_kernel, doc_starts.shape[0], heads, all_heads),
        grid_spec=pltpu.PrefetchScalarGridSpec(
            num_scalar_prefetch=2,
            grid=(),
            in_specs=[vm] * 8,
            out_specs=[vm] * 10,
            scratch_shapes=[pltpu.VMEM((total + 8, states2), F32)],
        ),
        out_shape=[
            jax.ShapeDtypeStruct((total, states2), BF),
            jax.ShapeDtypeStruct((total, states2), F32),
            compact,
            compact,
            compact,
            jax.ShapeDtypeStruct((2, 16, rows), F32),
            compact_b,
            compact_b,
            compact_b,
            jax.ShapeDtypeStruct((2, 8, LANES), F32),
        ],
        compiler_params=params(),
        cost_estimate=cost(4e9, 4e6),
        name="shared_maps",
    )(meta, doc_starts, own, xr, cr, dr, rim_own, rim_recv, taps, prm)


def keep_row(keep, heads, width):
    hi, rest = split2(keep)
    low = (keep - hi.astype(F32) - rest.astype(F32)).astype(BF)
    wide = spread(heads, width)
    lane = iota(keep.shape, 1)
    clean = lambda v: jnp.where(lane < 16, v.astype(F32), 0.0).astype(BF)
    return mm(clean(hi), wide) + mm(clean(rest), wide) + mm(clean(low), wide)


def inner_kernel(
    docs, heads, meta_ref, docs_ref, own_ref, xr_ref, cr_ref, dr_ref, rim_own_ref, rim_recv_ref,
    taps_ref, bact_ref, dpk_ref, wpk_ref, keep_ref, pre_ref, xd_ref, loc_ref, send_ref, ext_ref,
    wx_ref,
):
    k, chip = meta_ref[0], meta_ref[2]
    rows, width = own_ref.shape
    total = 2 * rows
    states = bact_ref.shape[1] // 2
    base = chip * total
    mine = pl.multiple_of(8 + k * rows, 8)
    other = pl.multiple_of(8 + (1 - k) * rows, 8)
    rim = (rim_own_ref[:, :width].astype(F32) + rim_recv_ref[:, :width].astype(F32))
    ext_ref[0:8, :] = rim.astype(BF).astype(F32)[8:16, :]

    def total_of(a, b):
        return (a[...].astype(F32) + b[...].astype(F32)).astype(BF).astype(F32)

    ext_ref[pl.ds(mine, rows), :] = total_of(own_ref, xr_ref)
    ext_ref[pl.ds(other, rows), :] = total_of(cr_ref, dr_ref)
    wide = spread(heads, width)
    tile = 64

    def conv(step, _):
        at = pl.multiple_of(step * tile, tile)
        masks = conv_masks(docs_ref, docs, base + at, tile, LANES)
        dpk = dpk_ref[pl.ds(at, tile), :]
        wpk = wpk_ref[pl.ds(at, tile), :]
        for lane in range(0, width, LANES):
            sl = slice(lane, lane + LANES)
            window = ext_ref[pl.ds(at, tile + 8), sl]
            value = window[8:] * taps_ref[0:1, sl]
            for j in range(1, 4):
                value = value + window[8 - j : 8 - j + tile] * taps_ref[j : j + 1, sl] * masks[j - 1]
            pre_ref[pl.ds(at, tile), sl] = value
            act = value / (1.0 + jnp.exp(-value))
            xd = act * mm(dpk, wide[:, sl])
            xd_ref[pl.ds(at, tile), sl] = xd.astype(BF)
            wx_ref[pl.ds(at, tile), sl] = (xd * mm(wpk, wide[:, sl])).astype(BF)
        return 0

    lax.fori_loop(0, total // tile, conv, 0)
    locs = []
    for part in range(2):
        sl = slice(part * rows, (part + 1) * rows)
        loc = mm_tn(bact_ref[sl, :states], wx_ref[sl, :])
        loc_ref[part] = loc
        locs.append(loc)
    second = keep_row(keep_ref[1], heads, width)[0:1, :]
    state = locs[0] * second + locs[1]
    chips, piece = send_ref.shape[0], send_ref.shape[1]
    for i in range(chips):
        send_ref[i, :, :width] = state[i * piece : (i + 1) * piece, :].astype(BF)
    keep = jnp.where(iota((8, LANES), 1) < 16, keep_ref[0] * keep_ref[1], 0.0)
    hi, mid = split2(keep)
    low = (keep - hi.astype(F32) - mid.astype(F32)).astype(BF)
    row = iota((8, LANES), 0)
    stack = jnp.where(row == 0, hi.astype(F32), jnp.where(row == 1, mid.astype(F32), low.astype(F32)))
    stack = jnp.concatenate([stack, jnp.zeros((piece - 8, LANES), F32)], axis=0).astype(BF)
    for i in range(chips):
        send_ref[i, :, width:] = stack


def inner_maps(
    meta, doc_starts, own, xr, cr, dr, rim_own, rim_recv, taps, bact, dpk, wpk, keep, heads, chips
):
    rows, width = own.shape
    total, states = 2 * rows, bact.shape[1] // 2
    vm = pl.BlockSpec(memory_space=pltpu.VMEM)
    whole = lambda shape: pl.BlockSpec(shape, lambda i, m, d: (0,) * len(shape))
    half = pl.BlockSpec((taps.shape[0], width), lambda i, m, d: (0, m[0]))
    outs = [
        jax.ShapeDtypeStruct((total, width), F32),
        jax.ShapeDtypeStruct((total, width), BF),
        jax.ShapeDtypeStruct((2, states, width), F32),
        jax.ShapeDtypeStruct((chips, states // chips, width + LANES), BF),
    ]
    return pl.pallas_call(
        functools.partial(inner_kernel, doc_starts.shape[0], heads),
        grid_spec=pltpu.PrefetchScalarGridSpec(
            num_scalar_prefetch=2,
            grid=(1,),
            in_specs=[
                whole(own.shape), whole(xr.shape), whole(cr.shape), whole(dr.shape),
                whole(rim_own.shape), whole(rim_recv.shape), half, whole(bact.shape),
                whole(dpk.shape), whole(wpk.shape), whole(keep.shape),
            ],
            out_specs=[whole(o.shape) for o in outs],
            scratch_shapes=[pltpu.VMEM((total + 8, width), F32), pltpu.VMEM((total, width), BF)],
        ),
        out_shape=outs,
        compiler_params=params(),
        cost_estimate=cost(4e9, 4e6),
        name="inner_maps",
    )(meta, doc_starts, own, xr, cr, dr, rim_own, rim_recv, taps, bact, dpk, wpk, keep)


def within_kernel(
    docs, heads, meta_ref, docs_ref, xd_ref, ramp_ref, rampt_ref, own_ref, xr_ref, cr_ref, dr_ref,
    own_low_ref, xr_low_ref, cr_low_ref, dr_low_ref, rim_own_ref, rim_recv_ref, taps_ref, y_ref,
    cbt_ref, cb_ref, gate_ref, ext_ref, high_ref, low_ref,
):
    k, chip = meta_ref[0], meta_ref[2]
    total, width = xd_ref.shape
    rows = total // 2
    states2 = own_low_ref.shape[1]
    states = states2 // 2
    mine = pl.multiple_of(8 + k * rows, 8)
    other = pl.multiple_of(8 + (1 - k) * rows, 8)
    rim = rim_own_ref[:, width:].astype(F32) + rim_recv_ref[:, width:].astype(F32)
    ext_ref[0:8, :] = rim[8:16, :]

    def exact_sum(a, a_low, b, b_low):
        high = a[:, :states2].astype(F32) + b[:, :states2].astype(F32)
        return high + (a_low[...].astype(F32) + b_low[...].astype(F32))

    ext_ref[pl.ds(mine, rows), :] = exact_sum(own_ref, own_low_ref, xr_ref, xr_low_ref)
    ext_ref[pl.ds(other, rows), :] = exact_sum(cr_ref, cr_low_ref, dr_ref, dr_low_ref)
    tile = 64

    def conv(step, _):
        at = pl.multiple_of(step * tile, tile)
        masks = conv_masks(docs_ref, docs, chip * total + at, tile, LANES)
        for lane in range(0, states2, LANES):
            sl = slice(lane, lane + LANES)
            window = ext_ref[pl.ds(at, tile + 8), sl]
            value = window[8:] * taps_ref[0:1, sl]
            for j in range(1, 4):
                value = value + window[8 - j : 8 - j + tile] * taps_ref[j : j + 1, sl] * masks[j - 1]
            high, low = split2(value / (1.0 + jnp.exp(-value)))
            high_ref[pl.ds(at, tile), sl] = high
            low_ref[pl.ds(at, tile), sl] = low
        return 0

    lax.fori_loop(0, total // tile, conv, 0)
    square = (rows, rows)
    lane = iota((rows, LANES), 1)
    for part in range(2):
        sl = slice(part * rows, (part + 1) * rows)
        begin = chip * total + part * rows
        b, c = high_ref[sl, :states], high_ref[sl, states:]
        b_low, c_low = low_ref[sl, :states], low_ref[sl, states:]
        cb_ref[...] = mm_nt(c, b) + (mm_nt(c, b_low) + mm_nt(c_low, b))
        cbt_ref[part] = jnp.transpose(cb_ref[...])
        pos, src = begin + iota(square, 0), begin + iota(square, 1)
        start = doc_start_of(pos, docs_ref, docs)
        gate_ref[...] = jnp.where((src <= pos) & (src >= start), 0.0, NEG)
        for pair in range(heads // 2):
            cols = slice(pair * LANES, (pair + 1) * LANES)
            xd = xd_ref[sl, cols]
            found = []
            for head in (2 * pair, 2 * pair + 1):
                gap = ramp_ref[sl, head : head + 1] - rampt_ref[part, head : head + 1, :]
                high, low = split2(jnp.exp2(gap + gate_ref[...]) * cb_ref[...])
                found.append(mm(high, xd) + mm(low, xd))
            y_ref[sl, cols] = jnp.where(lane < HEAD_DIM, found[0], found[1])


def within(meta, doc_starts, xd, ramp, rampt, smalls, lows, rim_own, rim_recv, taps, heads):
    total, width = xd.shape
    rows, states2 = total // 2, lows[0].shape[1]
    vm = pl.BlockSpec(memory_space=pltpu.VMEM)
    return pl.pallas_call(
        functools.partial(within_kernel, doc_starts.shape[0], heads),
        grid_spec=pltpu.PrefetchScalarGridSpec(
            num_scalar_prefetch=2,
            grid=(),
            in_specs=[vm] * 14,
            out_specs=[vm] * 2,
            scratch_shapes=[
                pltpu.VMEM((rows, rows), F32),
                pltpu.VMEM((rows, rows), F32),
                pltpu.VMEM((total + 8, states2), F32),
                pltpu.VMEM((total, states2), BF),
                pltpu.VMEM((total, states2), BF),
            ],
        ),
        out_shape=[
            jax.ShapeDtypeStruct((total, width), F32),
            jax.ShapeDtypeStruct((2, rows, rows), F32),
        ],
        compiler_params=params(),
        cost_estimate=cost(6e9, 4e6),
        name="within",
    )(meta, doc_starts, xd, ramp, rampt, *smalls, *lows, rim_own, rim_recv, taps)


def chain_kernel(heads, reverse, recv_ref, keep_ref, out_ref):
    chips = recv_ref.shape[0]
    width = out_ref.shape[2]
    state = jnp.zeros(out_ref.shape[1:], F32)
    wide = spread(heads, width)
    for step in range(chips):
        i = chips - 1 - step if reverse else step
        out_ref[i] = state.astype(BF)
        if step < chips - 1:
            factor = mm(keep_ref[i, :, width:], wide)
            factor = factor[0:1] + factor[1:2] + factor[2:3]
            state = state * factor + recv_ref[i, :, :width].astype(F32)


def chain(recv, keeps, heads, width, reverse):
    chips, piece = recv.shape[0], recv.shape[1]
    return pl.pallas_call(
        functools.partial(chain_kernel, heads, reverse),
        out_shape=jax.ShapeDtypeStruct((chips, piece, width), BF),
        compiler_params=params(16),
        cost_estimate=cost(1e8, 1e6),
        name="chain",
    )(recv, keeps)


def out_kernel(
    heads, meta_ref, y_ref, state_ref, loc_ref, bact_ref, epk_ref, keep_ref, go_ref, go_recv_ref,
    gain_ref, mix_own_ref, mix_send_ref, dy_ref, edy_ref, dot_ref, both_ref, late_ref, send_ref,
    go_all_ref, mix_ref,
):
    k = meta_ref[0]
    total, width = y_ref.shape
    rows = total // 2
    states = bact_ref.shape[1] // 2
    mine = pl.multiple_of(k * rows, rows)
    other = pl.multiple_of((1 - k) * rows, rows)
    go_all_ref[pl.ds(mine, rows), :] = go_ref[...]
    go_all_ref[pl.ds(other, rows), :] = go_recv_ref[...]
    state = state_ref[...]
    keep0 = keep_row(keep_ref[0], heads, width)[0:1, :]
    both_ref[0] = state
    middle = state.astype(F32) * keep0 + loc_ref[0]
    both_ref[1] = middle.astype(BF)
    both_ref[2] = (middle * keep_row(keep_ref[1], heads, width)[0:1, :] + loc_ref[1]).astype(BF)
    wide = spread(heads, width)
    gather = gather_heads(width)
    tile = 256
    per = rows // tile

    def one(step, _):
        at = pl.multiple_of(step * tile, tile)
        sl = pl.ds(at, tile)
        enter = mm(epk_ref[sl, :], wide)
        carried = mm(bact_ref[sl, states:], both_ref[step // per])
        y = y_ref[sl, :] + carried * enter
        u = go_all_ref[sl, :].astype(F32) * gain_ref[...]
        mean = over_heads(y * y, gather) * (1.0 / HEAD_DIM)
        along = over_heads(u * y, gather)
        scale = lax.rsqrt(mean + epsilon)
        cube = scale * scale * scale
        wide_scale = mm(packed(scale), wide)
        wide_back = mm(packed(cube * along * (1.0 / HEAD_DIM)), wide)
        mix_ref[sl, :] = (y * wide_scale * gain_ref[...]).astype(BF)
        dy = u * wide_scale - y * wide_back
        hi, lo = split2(dy)
        for pair in range(width // LANES):
            cols = slice(pair * LANES, (pair + 1) * LANES)
            dy_ref[sl, 2 * pair * LANES : (2 * pair + 1) * LANES] = hi[:, cols]
            dy_ref[sl, (2 * pair + 1) * LANES : (2 * pair + 2) * LANES] = lo[:, cols]
        edy_ref[sl, :] = (dy * enter).astype(BF)
        dot_ref[sl, :] = epsilon * cube * along
        return 0

    lax.fori_loop(0, total // tile, one, 0)
    mix_own_ref[...] = mix_ref[pl.ds(mine, rows), :]
    mix_send_ref[...] = mix_ref[pl.ds(other, rows), :]
    late = mm_tn(bact_ref[rows:, states:], edy_ref[rows:, :])
    late_ref[...] = late
    back = late * keep0 + mm_tn(bact_ref[:rows, states:], edy_ref[:rows, :])
    chips, piece = send_ref.shape[0], send_ref.shape[1]
    for i in range(chips):
        send_ref[i] = back[i * piece : (i + 1) * piece, :].astype(BF)


def outputs_of(meta, y, state, loc, bact, epk, keep, grad_out, go_recv, gain, heads, chips):
    total, width = y.shape
    rows, states = total // 2, bact.shape[1] // 2
    whole = lambda shape: pl.BlockSpec(shape, lambda i, m: (0,) * len(shape))
    half = lambda count: pl.BlockSpec((count, width), lambda i, m: (0, m[0]))
    outs = [
        jax.ShapeDtypeStruct((rows, width), BF),
        jax.ShapeDtypeStruct((rows, width), BF),
        jax.ShapeDtypeStruct((total, 2 * width), BF),
        jax.ShapeDtypeStruct((total, width), BF),
        jax.ShapeDtypeStruct((total, LANES), F32),
        jax.ShapeDtypeStruct((3, states, width), BF),
        jax.ShapeDtypeStruct((states, width), F32),
        jax.ShapeDtypeStruct((chips, states // chips, width), BF),
    ]
    return pl.pallas_call(
        functools.partial(out_kernel, heads),
        grid_spec=pltpu.PrefetchScalarGridSpec(
            num_scalar_prefetch=1,
            grid=(1,),
            in_specs=[
                whole(y.shape), whole(state.shape), whole(loc.shape), whole(bact.shape),
                whole(epk.shape), whole(keep.shape), half(rows), whole(go_recv.shape), half(1),
            ],
            out_specs=[whole(o.shape) for o in outs],
            scratch_shapes=[pltpu.VMEM((total, width), BF), pltpu.VMEM((total, width), BF)],
        ),
        out_shape=outs,
        compiler_params=params(),
        cost_estimate=cost(4e9, 4e6),
        name="outputs_of",
    )(meta, y, state, loc, bact, epk, keep, grad_out, go_recv, gain)


def within_back_kernel(
    docs, heads, meta_ref, docs_ref, dy_ref, edy_ref, both_ref, xd_ref, bact_ref, ramp_ref,
    rampt_ref, cbt_ref, act_ref, slope_ref, near_ref, q_ref, dbc_ref, gate_ref, sum_ref,
):
    gather = gather_heads(xd_ref.shape[1])
    chip = meta_ref[2]
    total, width = xd_ref.shape
    rows = total // 2
    states = bact_ref.shape[1] // 2
    square = (rows, rows)
    lane = iota((rows, LANES), 1)
    for part in range(2):
        sl = slice(part * rows, (part + 1) * rows)
        begin = chip * total + part * rows
        b, c = bact_ref[sl, :states], bact_ref[sl, states:]
        src, pos = begin + iota(square, 0), begin + iota(square, 1)
        start = doc_start_of(pos, docs_ref, docs)
        gate_ref[...] = jnp.where((src <= pos) & (src >= start), 0.0, NEG)
        sum_ref[...] = jnp.zeros(square, F32)
        q = jnp.zeros((rows, LANES), F32)
        for pair in range(heads // 2):
            cols = slice(pair * LANES, (pair + 1) * LANES)
            xd = xd_ref[sl, cols]
            dy_both = dy_ref[sl, 2 * pair * LANES : (2 * pair + 2) * LANES]
            dy = dy_both[:, :LANES]
            found = []
            for side, head in enumerate((2 * pair, 2 * pair + 1)):
                keep_side = (lane < HEAD_DIM) if side == 0 else (lane >= HEAD_DIM)
                only = jnp.where(keep_side, xd.astype(F32), 0.0).astype(BF)
                only = jnp.concatenate([only, only], axis=1)
                gap = rampt_ref[part, head : head + 1, :] - ramp_ref[sl, head : head + 1]
                decay = jnp.exp2(gap + gate_ref[...])
                found.append(mm((decay * cbt_ref[part]).astype(BF), dy))
                sum_ref[...] += mm_nt(only, dy_both) * decay
            dxd = jnp.where(lane < HEAD_DIM, found[0], found[1])
            near_ref[sl, cols] = (dxd * slope_ref[sl, cols].astype(F32)).astype(BF)
            q = q + mm((dxd * act_ref[sl, cols].astype(F32)).astype(BF), gather[cols, :])
        q_ref[sl, :] = q
        grad, low = split2(sum_ref[...])
        dbc_ref[sl, :states] = mm(grad, c) + mm(low, c)
        dbc_ref[sl, states:] = mm_tn(grad, b) + mm_tn(low, b) + mm_nt(edy_ref[sl, :], both_ref[part])


def within_back(meta, doc_starts, dy, edy, both, xd, bact, ramp, rampt, cbt, act, slope, heads):
    total, width = xd.shape
    rows = total // 2
    vm = pl.BlockSpec(memory_space=pltpu.VMEM)
    return pl.pallas_call(
        functools.partial(within_back_kernel, doc_starts.shape[0], heads),
        grid_spec=pltpu.PrefetchScalarGridSpec(
            num_scalar_prefetch=2,
            grid=(),
            in_specs=[vm] * 10,
            out_specs=[vm] * 3,
            scratch_shapes=[pltpu.VMEM((rows, rows), F32)] * 2,
        ),
        out_shape=[
            jax.ShapeDtypeStruct((total, width), BF),
            jax.ShapeDtypeStruct((total, LANES), F32),
            jax.ShapeDtypeStruct((total, bact.shape[1]), F32),
        ],
        compiler_params=params(),
        cost_estimate=cost(1e10, 6e6),
        name="within_back",
    )(meta, doc_starts, dy, edy, both, xd, bact, ramp, rampt, cbt, act, slope)


def slopes_kernel(pre_ref, dpk_ref, wpk_ref, act_ref, far_ref, wx_ref, slope_ref, reach_ref):
    total, width = pre_ref.shape
    wide = spread(width // HEAD_DIM, width)
    tile = total // 2
    for at in range(0, total, tile):
        sl = slice(at, at + tile)
        for lane in range(0, width, LANES):
            ls = slice(lane, lane + LANES)
            w = mm(wpk_ref[sl, :], wide[:, ls])
            step = mm(dpk_ref[sl, :], wide[:, ls])
            act, slope = silu_parts(pre_ref[sl, ls])
            slope = slope * step
            act_ref[sl, ls] = act.astype(BF)
            far_ref[sl, ls] = (act * w).astype(BF)
            wx_ref[sl, ls] = (act * step * w).astype(BF)
            slope_ref[sl, ls] = slope.astype(BF)
            reach_ref[sl, ls] = (slope * w).astype(BF)


def slopes_of(pre, dpk, wpk):
    return pl.pallas_call(
        slopes_kernel,
        out_shape=[jax.ShapeDtypeStruct(pre.shape, BF)] * 5,
        compiler_params=params(),
        cost_estimate=cost(2e9, 4e6),
        name="slopes_of",
    )(pre, dpk, wpk)


def back_masks(docs_ref, docs, pos):
    return [jnp.where(pos >= doc_start_of(pos + j, docs_ref, docs), 1.0, 0.0) for j in range(1, 4)]


def conv_back(src_ref, taps, at, count, ls, masks):
    window = src_ref[pl.ds(at, count + 8), ls]
    value = window[:count] * taps[0:1, ls]
    for j in range(1, 4):
        value = value + window[j : j + count] * taps[j : j + 1, ls] * masks[j - 1]
    return value


def grads_kernel(
    docs, heads, meta_ref, docs_ref, adj_ref, late_ref, keep_ref, both_ref, b_ref, near_ref, far_ref,
    wx_ref, reach_ref, q_ref, dbc_ref, bpre_ref, delta_ref, sig_ref, dot_ref, prm_ref, taps_bc_ref,
    taps_ref, own_ref, other_ref, bc_own_ref, bc_other_ref, rim_ref, adj2_ref, gx_ref, gb_ref, all_ref,
    bc_all_ref,
):
    k, chip = meta_ref[0], meta_ref[2]
    total, width = near_ref.shape
    rows = total // 2
    states = b_ref.shape[1]
    states2 = 2 * states
    base = chip * total
    adj = adj_ref[...].astype(F32)
    early = adj * keep_row(keep_ref[1], heads, width)[0:1, :] + late_ref[...]
    adj2_ref[0] = early.astype(BF)
    adj2_ref[1] = adj_ref[...]
    gather = gather_heads(width)
    ends = [
        over_heads(
            jnp.sum(a * both_ref[i].astype(F32), axis=0, keepdims=True) + jnp.zeros((8, width), F32),
            gather,
        )
        for i, a in ((1, early), (2, adj))
    ]
    for ref, lanes in ((gx_ref, width), (gb_ref, states2)):
        ref[0:8, :] = jnp.zeros((8, lanes), F32)
        ref[total + 8 :, :] = jnp.zeros((8, lanes), F32)
    square = (rows, rows)
    upper = jnp.where(iota(square, 0) <= iota(square, 1), 1.0, 0.0).astype(BF)
    rate = prm_ref[1:2, :]
    row = iota((rows, LANES), 0)
    for part in range(2):
        sl = slice(part * rows, (part + 1) * rows)
        inside = slice(8 + part * rows, 8 + (part + 1) * rows)
        q = q_ref[sl, :]
        for lane in range(0, width, LANES):
            ls = slice(lane, lane + LANES)
            back = mm(b_ref[sl, :], adj2_ref[part, :, ls])
            gx_ref[inside, ls] = near_ref[sl, ls].astype(F32) + back * reach_ref[sl, ls].astype(F32)
            q = q + mm((back * far_ref[sl, ls].astype(F32)).astype(BF), gather[ls, :])
        ramp_grad = dot_ref[sl, :] - delta_ref[sl, :] * q
        ramp_grad = ramp_grad + jnp.where(row == rows - 1, ends[part][0:1, :], 0.0)
        hi, lo = split2(ramp_grad)
        later = mm(upper, hi) + mm(upper, lo)
        bc_all_ref[sl, states2:] = (q - rate * later) * sig_ref[sl, :]
        back = mm_nt(wx_ref[sl, :], adj2_ref[part])
        for lane, grad in ((0, dbc_ref[sl, :states] + back), (states, dbc_ref[sl, states:])):
            ls = slice(lane, lane + states)
            _, slope = silu_parts(bpre_ref[sl, ls])
            gb_ref[inside, ls] = grad * slope
    tile = 64

    def back(step, _):
        at = pl.multiple_of(step * tile, tile)
        begin = pl.multiple_of(at + 8, 8)
        masks = back_masks(docs_ref, docs, base + at + iota((tile, LANES), 0))
        for lane in range(0, width, LANES):
            ls = slice(lane, lane + LANES)
            all_ref[pl.ds(at, tile), ls] = conv_back(gx_ref, taps_ref, begin, tile, ls, masks).astype(BF)
        for lane in range(0, states2, LANES):
            ls = slice(lane, lane + LANES)
            bc_all_ref[pl.ds(at, tile), ls] = conv_back(gb_ref, taps_bc_ref, begin, tile, ls, masks)
        return 0

    lax.fori_loop(0, total // tile, back, 0)
    pad = jnp.zeros((8, LANES), F32)
    masks = back_masks(docs_ref, docs, base - 8 + iota((8, LANES), 0))
    for src, taps, first, lanes in ((gx_ref, taps_ref, 0, width), (gb_ref, taps_bc_ref, width, states2)):
        for lane in range(0, lanes, LANES):
            value = conv_back(src, taps, 0, 8, slice(lane, lane + LANES), masks)
            value = jnp.concatenate([pad, value], axis=0)
            rim_ref[:, first + lane : first + lane + LANES] = value.astype(BF)
    mine = pl.ds(pl.multiple_of(k * rows, rows), rows)
    other = pl.ds(pl.multiple_of((1 - k) * rows, rows), rows)
    own_ref[...] = all_ref[mine, :]
    other_ref[...] = all_ref[other, :]
    bc_own_ref[...] = bc_all_ref[mine, :]
    bc_other_ref[...] = bc_all_ref[other, :]


def grads_of(
    meta, doc_starts, adj, late, keep, both, bact, near, far, wx, reach, q, dbc, bpre, delta, sig, dots,
    prm, taps_bc, taps, heads,
):
    total, width = near.shape
    rows, states2 = total // 2, bact.shape[1]
    states = states2 // 2
    whole = lambda shape: pl.BlockSpec(shape, lambda i, m, d: (0,) * len(shape))
    half = pl.BlockSpec((taps.shape[0], width), lambda i, m, d: (0, m[0]))
    first = pl.BlockSpec((total, states), lambda i, m, d: (0, 0))
    ins = [near, far, wx, reach, q, dbc, bpre, delta, sig, dots, prm, taps_bc]
    outs = [
        jax.ShapeDtypeStruct((rows, width), BF),
        jax.ShapeDtypeStruct((rows, width), BF),
        jax.ShapeDtypeStruct((rows, states2 + LANES), F32),
        jax.ShapeDtypeStruct((rows, states2 + LANES), F32),
        jax.ShapeDtypeStruct((16, width + states2), BF),
    ]
    return pl.pallas_call(
        functools.partial(grads_kernel, doc_starts.shape[0], heads),
        grid_spec=pltpu.PrefetchScalarGridSpec(
            num_scalar_prefetch=2,
            grid=(1,),
            in_specs=[whole(a.shape) for a in (adj, late, keep, both)]
            + [first]
            + [whole(a.shape) for a in ins]
            + [half],
            out_specs=[whole(o.shape) for o in outs],
            scratch_shapes=[
                pltpu.VMEM((2, states, width), BF),
                pltpu.VMEM((total + 16, width), F32),
                pltpu.VMEM((total + 16, states2), F32),
                pltpu.VMEM((total, width), BF),
                pltpu.VMEM((total, states2 + LANES), F32),
            ],
        ),
        out_shape=outs,
        compiler_params=params(),
        cost_estimate=cost(4e9, 8e6),
        name="grads_of",
    )(meta, doc_starts, adj, late, keep, both, bact, *ins, taps)


def join_kernel(heads, meta_ref, own_ref, recv_ref, out_ref, send_ref):
    k = meta_ref[0]
    states2 = own_ref.shape[1] - LANES
    total = own_ref[:, :states2] + recv_ref[:, :states2]
    out_ref[:, :states2] = total
    send_ref[:, :states2] = total.astype(BF)
    shape = (LANES, LANES)
    row, col = iota(shape, 0), iota(shape, 1)
    mine = jnp.where((row < heads) & (col == row + k * heads), 1.0, 0.0).astype(BF)
    other = jnp.where((row < heads) & (col == row + (1 - k) * heads), 1.0, 0.0).astype(BF)
    steps = mm(own_ref[:, states2:].astype(BF), mine) + mm(recv_ref[:, states2:].astype(BF), other)
    out_ref[:, states2:] = steps
    send_ref[:, states2:] = steps.astype(BF)


def join(meta, own, recv, heads):
    vm = pl.BlockSpec(memory_space=pltpu.VMEM)
    return pl.pallas_call(
        functools.partial(join_kernel, heads),
        grid_spec=pltpu.PrefetchScalarGridSpec(
            num_scalar_prefetch=1, grid=(), in_specs=[vm] * 2, out_specs=[vm] * 2
        ),
        out_shape=[jax.ShapeDtypeStruct(own.shape, F32), jax.ShapeDtypeStruct(own.shape, BF)],
        compiler_params=params(16),
        cost_estimate=cost(1e8, 1e6),
        name="join",
    )(meta, own, recv)


def half_kernel(meta_ref, *refs):
    *before, mine_ref, other_ref, rim_ref, w_mine_ref, w_other_ref, out_ref = refs
    rows, width = mine_ref.shape

    def whole(ref, rim):
        tail = ref[rows - 16 :, :].astype(F32) + rim.astype(F32)
        return jnp.concatenate([ref[: rows - 16, :], tail.astype(BF)], axis=0)

    mine = whole(mine_ref, rim_ref[:16, :width])
    other = whole(other_ref, rim_ref[16:, :width])
    total = mm_nt(mine, w_mine_ref[...]) + mm_nt(other, w_other_ref[...])
    for ref in before:
        total = total + ref[...]
    out_ref[...] = total


def first_half(meta, far, before, mine, other, rim, x_weight, tile):
    rows, width = mine.shape
    depth = x_weight.shape[0]
    whole = lambda shape: pl.BlockSpec(shape, lambda i, m: (0, 0))
    part = pl.BlockSpec((rows, tile), lambda i, m: (0, i))
    parts = [] if before is None else [before]
    side = lambda m: 1 - m[1] if far else m[1]
    return pl.pallas_call(
        half_kernel,
        grid_spec=pltpu.PrefetchScalarGridSpec(
            num_scalar_prefetch=1,
            grid=(depth // tile,),
            in_specs=[part] * len(parts)
            + [
                whole(mine.shape), whole(other.shape), whole(rim.shape),
                pl.BlockSpec((tile, width), lambda i, m: (i, side(m) * 2 + m[0])),
                pl.BlockSpec((tile, width), lambda i, m: (i, side(m) * 2 + 1 - m[0])),
            ],
            out_specs=part,
        ),
        out_shape=jax.ShapeDtypeStruct((rows, depth), F32),
        compiler_params=params(16),
        cost_estimate=cost(2e9, 4e6),
        name="half_sum",
    )(meta, *parts, mine, other, rim, x_weight, x_weight)


def last_kernel(
    heads, rim_width, side_ref, part_ref, rim_ref, rim0_ref, bc_own_ref, bc_recv_ref, bcw_ref, dtw_ref,
    out_ref, bc_ref, dt_ref,
):
    rows = part_ref.shape[0]
    states2 = bcw_ref.shape[1]
    all_heads = dtw_ref.shape[0]

    @pl.when(pl.program_id(0) == 0)
    def _():
        bc = bc_own_ref[:, :states2] + bc_recv_ref[:, :states2].astype(F32)
        rim = rim_ref[:, rim_width:].astype(F32) + rim0_ref[:, rim_width:].astype(F32)
        extra = rim[:16] + rim[16:]
        for at, value in ((0, bc[: rows - 16, :]), (rows - 16, bc[rows - 16 :, :] + extra)):
            high, low = split2(value)
            bc_ref[at : at + value.shape[0], :states2] = high
            bc_ref[at : at + value.shape[0], states2:] = low
        shape = (LANES, all_heads)
        row, col = iota(shape, 0), iota(shape, 1)
        x = side_ref[1]
        here = jnp.where((row < heads) & (col == row + x * heads), 1.0, 0.0).astype(BF)
        there = jnp.where((row < heads) & (col == row + (1 - x) * heads), 1.0, 0.0).astype(BF)
        dt = mm(bc_own_ref[:, states2:].astype(BF), here) + mm(bc_recv_ref[:, states2:], there)
        dt_ref[...] = dt.astype(BF)

    bcw = bcw_ref[...]
    total = part_ref[...] + mm_nt(bc_ref[...], jnp.concatenate([bcw, bcw], axis=1))
    out_ref[...] = (total + mm(dt_ref[...], dtw_ref[...])).astype(BF)


def last_half(side, part, rim, rim0, bc_own, bc_recv, bc_weight, dt_rows, tile):
    rows, depth = part.shape
    states2, all_heads = bc_weight.shape[1], dt_rows.shape[0]
    whole = lambda a: pl.BlockSpec(a.shape, lambda i, m: (0, 0))
    return pl.pallas_call(
        functools.partial(last_kernel, all_heads // 2, rim.shape[1] - states2),
        grid_spec=pltpu.PrefetchScalarGridSpec(
            num_scalar_prefetch=1,
            grid=(depth // tile,),
            in_specs=[
                pl.BlockSpec((rows, tile), lambda i, m: (0, i)),
                whole(rim), whole(rim0), whole(bc_own), whole(bc_recv),
                pl.BlockSpec((tile, states2), lambda i, m: (i, 0)),
                pl.BlockSpec((all_heads, tile), lambda i, m: (0, i)),
            ],
            out_specs=pl.BlockSpec((rows, tile), lambda i, m: (0, i)),
            scratch_shapes=[pltpu.VMEM((rows, 2 * states2), BF), pltpu.VMEM((rows, all_heads), BF)],
        ),
        out_shape=jax.ShapeDtypeStruct((rows, depth), BF),
        compiler_params=params(16),
        cost_estimate=cost(5e8, 2e6),
        name="last_half",
    )(side, part, rim, rim0, bc_own, bc_recv, bc_weight, dt_rows)


def by_chips(
    tokens, x_weight, bc_weight, dt_weight, conv_inner, conv_shared, dt_bias, decay_rate, norm_gain,
    doc_starts, grad_out,
):
    blocks = lax.axis_size("ctx")
    chips = blocks // 2
    rows = tokens.shape[0]
    all_heads = dt_weight.shape[1]
    heads = decay_rate.shape[0] // 2
    width = heads * HEAD_DIM
    place = lax.axis_index("ctx").astype(jnp.int32)
    x = lax.axis_index("fsdp").astype(jnp.int32)
    k = place % 2
    meta = jnp.stack([k, x, place // 2])

    core = [(i, i ^ 1) for i in range(blocks)]
    pair = [(0, 1), (1, 0)]
    cross = [(2 * i + j, 2 * (i ^ 1) + (1 - j)) for i in range(blocks) for j in range(2)]
    by_core = lambda a: lax.ppermute(a, "ctx", core)
    by_x = lambda a: lax.ppermute(a, "fsdp", pair)
    by_both = lambda a: lax.ppermute(a, ("ctx", "fsdp"), cross)
    groups = [[2 * i for i in range(chips)], [2 * i + 1 for i in range(chips)]]
    exchange = lambda a: lax.all_to_all(a, "ctx", 0, 0, axis_index_groups=groups)

    tail = tokens[rows - 16 :]
    ra = lax.ppermute(tail, "ctx", [(2 * i - 1, 2 * i) for i in range(1, chips)])
    rb = lax.ppermute(tail, "ctx", [(2 * i - 1, 2 * i + 1) for i in range(1, chips)])

    dt_rows = dt_weight.T
    to_cross, small, low = lead_proj(
        meta, tokens, x_weight, bc_weight, dt_rows, width
    )
    from_cross = by_both(to_cross)
    small_x = by_x(small)
    to_x, to_core, mine, rim_own, rim_send = rest_proj(
        meta, tokens, x_weight, bc_weight, ra, rb, width
    )
    from_x = by_x(to_x)
    from_core = by_core(to_core)
    rim_recv = by_x(rim_send)
    small_core = by_core(small)
    small_cross = by_core(small_x)
    low_x = by_x(low)
    lows = (low, low_x, by_core(low), by_core(low_x))
    go_recv = by_core(lax.dynamic_slice(grad_out, (jnp.int32(0), (1 - k) * width), (rows, width)))

    prm = jnp.stack([lax.dynamic_slice(v, (k * heads,), (heads,)) for v in (dt_bias, decay_rate)])
    prm = jnp.pad(prm, ((0, 6), (0, LANES - heads)))
    bact, bpre, delta, ramp, sig, rampt, dpk, wpk, epk, keep = shared_maps(
        meta, doc_starts, small, small_x, small_core, small_cross, rim_own, rim_recv, conv_shared,
        prm, heads, all_heads,
    )
    pre, xd, loc, send = inner_maps(
        meta, doc_starts, mine, from_x, from_core, from_cross, rim_own, rim_recv, conv_inner, bact,
        dpk, wpk, keep, heads, chips,
    )
    keeps = exchange(send)
    y, cbt = within(
        meta, doc_starts, xd, ramp, rampt, (small, small_x, small_core, small_cross), lows, rim_own, rim_recv,
        conv_shared, heads,
    )
    states = exchange(chain(keeps, keeps, heads, width, False))
    state = states.reshape(STATE, width)
    mix_own, mix_send, dy, edy, dots, both, late, back = outputs_of(
        meta, y, state, loc, bact, epk, keep, grad_out, go_recv, norm_gain[None, :], heads, chips
    )
    act, far, wx, slope, reach = slopes_of(pre, dpk, wpk)
    backs = exchange(back)
    near, q, dbc = within_back(
        meta, doc_starts, dy, edy, both, xd, bact, ramp, rampt, cbt, act, slope, heads
    )
    mix_recv = by_core(mix_send)
    mixed = jnp.where(
        k == 0,
        jnp.concatenate([mix_own, mix_recv], axis=1),
        jnp.concatenate([mix_recv, mix_own], axis=1),
    )
    adj = exchange(chain(backs, keeps, heads, width, True)).reshape(STATE, width)
    g_mine, g_other, bc_mine, bc_other, rim = grads_of(
        meta, doc_starts, adj, late, keep, both, bact, near, far, wx, reach, q, dbc, bpre, delta, sig,
        dots, prm, conv_shared, conv_inner, heads,
    )
    g_x = by_x(g_mine)
    g_cross = by_both(g_other)
    g_core = by_core(g_other)
    rim, g_core = lax.optimization_barrier((rim, g_core))
    rims = jnp.concatenate([rim, by_core(rim)], axis=0)
    back_perm = [(2 * i + 1, 2 * i - 1) for i in range(1, chips)]
    rim0 = lax.ppermute(rims, "ctx", back_perm)
    rim1 = lax.ppermute(
        rims, ("ctx", "fsdp"), [(2 * a + j, 2 * b + (1 - j)) for a, b in back_perm for j in range(2)]
    )
    bc_chip, bc_send = join(meta, bc_mine, by_core(bc_other), heads)
    bc_recv = by_x(bc_send)
    part = first_half(
        meta, False, None, g_mine, g_core, rim0, x_weight, 640
    )
    part = first_half(
        meta, True, part, g_x, g_cross, rim1, x_weight, 640
    )
    grad_tokens = last_half(meta, part, rim1, rim0, bc_chip, bc_recv, bc_weight, dt_rows, width)
    return (mixed, grad_tokens)


def splits_by_chip(mesh):
    return mesh.shape["fsdp"] == 2 and mesh.shape["ctx"] == 16


def solution(mesh):
    in_specs = (
        P("ctx", "fsdp"),
        P("fsdp", None),
        P("fsdp", None),
        P("fsdp", None),
        P(None, "fsdp"),
        P(),
        P("fsdp"),
        P("fsdp"),
        P("fsdp"),
        P(),
        P("ctx", "fsdp"),
    )
    body = by_chips if splits_by_chip(mesh) else on_device
    out_specs = (P("ctx", "fsdp"), P("ctx", "fsdp"))
    return jax.shard_map(
        body, mesh=mesh, in_specs=in_specs, out_specs=out_specs, check_vma=False
    )
```
